32 devices in a mesh: dp: 4 (over y, core), fsdp: 8 (over z, x).
Axes of the slice: x: 2, y: 2, z: 4, core: 2. Of those that a mesh axis runs over, the one named last changes fastest.
Arguments:
- inputs: bfloat16 [64, 256, 1024], P(('dp', 'fsdp')), may hold values from -6 to 6
- image_ids: int32 [64, 256], P(('dp', 'fsdp')), may hold values from -1 to 7, as said below
- cotangent: bfloat16 [64, 256, 1024], P(('dp', 'fsdp')), may hold values from -6 to 6
- gains: bfloat16 [32, 64], P(('dp', 'fsdp')), may hold values from 0.25 to 1.75
- biases: bfloat16 [32, 320], P(('dp', 'fsdp')), may hold values from -2 to 2
- w_qkv: bfloat16 [32, 98304], P(('dp', 'fsdp')), may hold values from -0.1875 to 0.1875
- w_out: bfloat16 [32, 32768], P(('dp', 'fsdp')), may hold values from -0.5 to 0.5
- w_in: bfloat16 [32, 131072], P(('dp', 'fsdp')), may hold values from -0.1875 to 0.1875
- w_mlp: bfloat16 [32, 131072], P(('dp', 'fsdp')), may hold values from -0.09375 to 0.09375
Outputs:
- block_out: bfloat16 [64, 256, 1024], P(('dp', 'fsdp'))
- grad_inputs: float32 [64, 256, 1024], P(('dp', 'fsdp'))
- grad_gains: float32 [32, 64], P(('dp', 'fsdp'))
- grad_biases: float32 [32, 320], P(('dp', 'fsdp'))
- grad_w_qkv: float32 [32, 98304], P(('dp', 'fsdp'))
- grad_w_out: float32 [32, 32768], P(('dp', 'fsdp'))
- grad_w_in: float32 [32, 131072], P(('dp', 'fsdp'))
- grad_w_mlp: float32 [32, 131072], P(('dp', 'fsdp'))
The draws below stay inside these ranges and needn't reach their ends.
Inputs may be any that keep to these rules, and one draw needn't show every extreme that they name: `image_ids`: -1 marks padding, which takes the last 1 to 64 positions of every row; the other positions hold their image's number within the row, counted from 0 in order, each image one run of positions; every row holds images 0 to 7.
All inputs are finite; a program needn't handle non-finite values.
Results may differ from the reference program's by a relative error of at most 0.014.
Values may be sent and summed in bfloat16 or wider, within the bound.
No kernel may reach another device: no remote copies, remote signals or barrier semaphores. Data moves between devices by JAX's collectives and lax.ppermute only.
A program may use at most 192 MiB of HBM per device.

```python
import math
import jax
import jax.numpy as jnp
from jax import lax

D = 1024
FF = 4096
HEADS = 16
HEAD_DIM = 64
SEQ = 256
ROWS = 64
GAIN_DEV = 64
BIAS_DEV = 320
QKV_DEV = 98304
OUT_DEV = 32768
IN_DEV = 131072
DEVICES = 32


def draw_image_ids(key, part):
    key = jax.random.fold_in(key, 11)
    start_key, pad_key = jax.random.split(key)
    chance = max(3, SEQ // 5)
    starts = jax.random.randint(start_key, (ROWS, SEQ), 0, chance) == 0
    position = jnp.arange(SEQ, dtype=jnp.int32)[None, :]
    stride = SEQ // 16
    forced = jnp.logical_and(position % stride == 0, position < 8 * stride)
    starts = jnp.logical_or(starts, forced)
    numbers = jnp.minimum(jnp.cumsum(starts.astype(jnp.int32), axis=1) - 1, 7)
    padding = jax.random.randint(pad_key, (ROWS, 1), 1, SEQ // 4 + 1)
    return jnp.where(position >= SEQ - padding, -1, numbers).astype(jnp.int32)


def with_spikes(values, own_key, source, target, blocks, factor):
    owner, partner = [(jnp.arange(values.shape[dim]) // (values.shape[dim] // blocks)).reshape([-1 if axis == dim else 1 for axis in range(values.ndim)]) for dim in (source, target)]
    chosen = jax.random.permutation(own_key, blocks)[partner]
    strong = (owner == chosen) | (owner == (partner + blocks // 2) % blocks)
    return jnp.where(strong, factor * values, values)


def block_levels(stream_key, extent, shards, least, largest):
    level = 1.0
    for dim, shards_of in shards:
        steps = jax.random.uniform(jax.random.fold_in(jax.random.fold_in(stream_key, 6), dim), (shards_of,), jnp.float32, least / len(shards), largest / len(shards))
        level = level * jnp.repeat(jnp.exp(steps), extent[dim] // shards_of).reshape((-1,) + (1,) * (len(extent) - 1 - dim))
    return level


def bell_draw(rng, extent, scale, limit, cuts=(), kind=jnp.bfloat16):
    factor_of = block_levels(rng, extent, cuts, -0.22, 0.18) if cuts else 1.0
    values = jax.random.normal(rng, extent, jnp.float32) * scale * factor_of
    return jnp.minimum(jnp.maximum(values, -limit), limit).astype(kind)


def heavy_noise(own_key, shape, width, most, cuts, heavy, held_as=jnp.bfloat16):
    values = width * jax.random.normal(own_key, shape, jnp.float32)
    if cuts:
        values = values * block_levels(own_key, shape, cuts, -0.22, 0.18)
    return jnp.clip(with_spikes(values, jax.random.fold_in(own_key, 3), *heavy), -most, most).astype(held_as)


def setup_inputs(seed: int = 0) -> dict:
    keys = jax.random.split(jax.random.key(seed), 10)
    inputs = bell_draw(keys[0], (ROWS, SEQ, D), 1.0, 6.0, ((0, 32),))
    image_ids = draw_image_ids(jax.random.fold_in(keys[9], 71), 0)
    cotangent = heavy_noise(keys[2], (ROWS, SEQ, D), 1.0, 6.0, ((0, 32),), (0, 2, 32, 2.75))
    gains = jnp.clip(1.0 + 0.15 * jax.random.normal(keys[3], (DEVICES, GAIN_DEV), jnp.float32), 0.25, 1.75).astype(jnp.bfloat16)
    biases = bell_draw(keys[4], (DEVICES, BIAS_DEV), 0.3, 2.0, ((0, 32),))
    w_qkv = bell_draw(keys[5], (DEVICES, QKV_DEV), D ** -0.5, 0.1875, ((0, 32),))
    w_out = bell_draw(keys[6], (DEVICES, OUT_DEV), (D // 8) ** -0.5, 0.5, ((0, 32),))
    w_in = bell_draw(keys[7], (DEVICES, IN_DEV), D ** -0.5, 0.1875, ((0, 32),))
    w_mlp = bell_draw(keys[8], (DEVICES, IN_DEV), FF ** -0.5, 0.09375, ((0, 32),))
    return {"inputs": inputs, "image_ids": image_ids, "cotangent": cotangent, "gains": gains, "biases": biases, "w_qkv": w_qkv, "w_out": w_out, "w_in": w_in, "w_mlp": w_mlp}


@jax.custom_vjp
def low(v):
    return lax.optimization_barrier(v.astype(jnp.bfloat16)).astype(jnp.float32)

@jax.custom_vjp
def low_back(v):
    return v

def low_keep(v):
    return (low(v), None)

def low_pass(kept, grad):
    return (grad,)

def back_keep(v):
    return (v, None)

def back_low(kept, grad):
    return (low(grad),)
low.defvjp(low_keep, low_pass)
low_back.defvjp(back_keep, back_low)
highest = lax.Precision.HIGHEST
eps = 1e-06

def round_both(value):
    return low_back(low(value))

def layer_norm(values, gain, shift):
    centre = values - lax.optimization_barrier(jnp.mean(values, axis=-1, keepdims=True))
    spread = lax.optimization_barrier(jnp.mean(centre * centre, axis=-1, keepdims=True))
    return centre * lax.rsqrt(spread + eps) * gain + shift

def forward(gains, biases, w_qkv, w_out, w_in, w_mlp, inputs, image_ids):
    blocks = inputs.shape[0]
    gain_vec = gains.reshape(-1)[:2 * D]
    bias_vec = biases.reshape(-1)[:6 * D + FF]
    matrix_qkv = w_qkv.reshape(-1)[:3 * D * D].reshape(D, 3 * D)
    matrix_out = w_out.reshape(-1)[:D * D].reshape(D, D)
    matrix_in = w_in.reshape(-1)[:D * FF].reshape(D, FF)
    matrix_mlp = w_mlp.reshape(-1)[:FF * D].reshape(FF, D)
    pieces = [bias_vec[index * D:(index + 1) * D] for index in range(6)]
    scale = HEAD_DIM ** (-0.5)
    tokens = inputs.reshape(blocks * SEQ, D)
    entry = low(layer_norm(tokens, gain_vec[:D], pieces[0]))
    bias_qkv = jnp.concatenate([pieces[1], jnp.zeros_like(pieces[1]), pieces[2]])
    project = round_both(jnp.dot(entry, matrix_qkv, precision=highest) + bias_qkv)
    queries = project[:, :D].reshape(blocks, SEQ, HEADS, HEAD_DIM)
    keys_all = project[:, D:2 * D].reshape(blocks, SEQ, HEADS, HEAD_DIM)
    values = project[:, 2 * D:].reshape(blocks, SEQ, HEADS, HEAD_DIM)
    scores = low_back(jnp.einsum('rqhd,rkhd->rhqk', queries, keys_all, precision=highest) * scale)
    same_image = (image_ids[:, :, None] == image_ids[:, None, :])[:, None]
    masked = jnp.where(same_image, scores, -1000000000.0)
    ceiling = lax.optimization_barrier(jnp.max(masked, axis=-1, keepdims=True))
    expo = jnp.exp(masked - ceiling)
    probs = low(expo / lax.optimization_barrier(jnp.sum(expo, axis=-1, keepdims=True)))
    mixed = round_both(jnp.einsum('rhqk,rkhd->rqhd', probs, values, precision=highest).reshape(blocks * SEQ, D))
    branch = low_back(jnp.dot(mixed, matrix_out, precision=highest) + pieces[3])
    middle = tokens + branch
    second = low(layer_norm(middle, gain_vec[D:], pieces[4]))
    hidden = low_back(jnp.dot(second, matrix_in, precision=highest) + bias_vec[6 * D:])
    active = low(jax.nn.gelu(hidden, approximate=False))
    result = middle + low_back(jnp.dot(active, matrix_mlp, precision=highest) + pieces[5])
    return result.reshape(blocks, SEQ, D)

def reference(inputs, image_ids, cotangent, gains, biases, w_qkv, w_out, w_in, w_mlp):
    params = tuple((param.astype(jnp.float32) for param in (gains, biases, w_qkv, w_out, w_in, w_mlp)))
    group = math.gcd(ROWS, max(1, 4096 // SEQ))
    turns = ROWS // group
    keep_rows = (image_ids >= 0).astype(jnp.float32)[..., None]
    masked_cot = cotangent.astype(jnp.float32) * keep_rows
    stacks = (inputs.astype(jnp.float32).reshape(turns, group, SEQ, D), image_ids.reshape(turns, group, SEQ), masked_cot.reshape(turns, group, SEQ, D))

    def advance(totals, block):
        block_in, block_ids, block_cot = block

        def local(*members):
            return forward(*members, block_ids)
        outputs, pull = jax.vjp(local, *params, block_in)
        grads = pull(block_cot)
        summed = tuple((total + grad for total, grad in zip(totals, grads[:6])))
        return (summed, (outputs.astype(jnp.bfloat16), grads[6]))
    start = tuple((jnp.zeros_like(param) for param in params))
    sums, (outs_all, grads_in) = lax.scan(advance, start, stacks)
    return (outs_all.reshape(ROWS, SEQ, D), grads_in.reshape(ROWS, SEQ, D), sums[0], sums[1], sums[2], sums[3], sums[4], sums[5])
```

```python
import jax
import jax.numpy as jnp
from jax import lax
from jax.experimental import pallas as pl
from jax.experimental.pallas import tpu as pltpu
from jax.sharding import PartitionSpec as P

D = 1024
FF = 4096
HEADS = 16
HEAD_DIM = 64
AXES = ("dp", "fsdp")


eps = 1e-06


def normalize(values):
    centre = values - jnp.mean(values, axis=-1, keepdims=True)
    inverse = lax.rsqrt(jnp.mean(centre * centre, axis=-1, keepdims=True) + eps)
    return (centre * inverse, inverse)


def norm_back(grad_norm, normed, inverse):
    return inverse * (
        grad_norm
        - jnp.mean(grad_norm, axis=-1, keepdims=True)
        - normed * jnp.mean(grad_norm * normed, axis=-1, keepdims=True)
    )


def masked_scores(queries, keys_all, same_image, scale):
    raw = (
        jnp.einsum("rqhd,rkhd->rhqk", queries, keys_all, preferred_element_type=jnp.float32) * scale
    )
    return jnp.where(same_image, raw, -1000000000.0)


def column_sums(values):
    return jnp.sum(values.astype(jnp.float32), axis=0)


class Plan:
    def __init__(self, mesh):
        outer, inner = mesh.shape["dp"], mesh.shape["fsdp"]
        ys = outer // 2
        xs = min(ys, inner)
        zs = inner // xs
        self.devices = outer * inner
        self.half = self.devices // 2

        def bits(size, unit):
            found = []
            while size > 1:
                size //= 2
                found.append(size * unit)
            return found

        xbits = bits(xs, 1)
        zbits = bits(zs, xs)
        self.core = inner
        ybits = bits(ys, 2 * inner)
        self.orders = (zbits + xbits + ybits, zbits + ybits + xbits)
        self.stages = len(self.orders[0])

    def pairs(self, stage):
        return [
            (i, i ^ self.orders[1 if i & self.core else 0][stage]) for i in range(self.devices)
        ]

    def core_pairs(self):
        return [(i, i ^ self.core) for i in range(self.devices)]

    def masks(self, which):
        found = [0]
        for bit in self.orders[which]:
            found = found + [mask ^ bit for mask in found]
        return found

    def positions(self, me):
        tables = jnp.array(
            [
                self.masks(0) + [mask ^ self.core for mask in self.masks(1)],
                self.masks(1) + [mask ^ self.core for mask in self.masks(0)],
            ],
            jnp.int32,
        )
        mine = jnp.where((me & self.core) > 0, tables[1], tables[0])
        return mine ^ me


def gather(plan, block):
    held = block[None]
    for stage in range(plan.stages):
        held = jnp.concatenate([held, lax.ppermute(held, AXES, plan.pairs(stage))], 0)
    return held, lax.ppermute(held, AXES, plan.core_pairs())


def total(parts):
    result = parts[0].astype(jnp.float32)
    for part in parts[1:]:
        result = result + part.astype(jnp.float32)
    return result


def scatter_sum(plan, keep, send):
    parts = [keep, lax.ppermute(send, AXES, plan.core_pairs())]
    count = plan.half
    for stage in reversed(range(plan.stages)):
        count //= 2
        outgoing = total([part[count : 2 * count] for part in parts]).astype(jnp.bfloat16)
        parts.append(lax.ppermute(outgoing, AXES, plan.pairs(stage)))
    return total([part[0] for part in parts])


def one_hot(order):
    return (order[:, None] == jnp.arange(order.shape[0])[None, :]).astype(jnp.bfloat16)


def assemble(order, own, other):
    half, rows, width = own.shape
    shape = (half, rows, width) if rows % 16 == 0 else (half, 16, rows * width // 16)

    def body(order_ref, own_ref, other_ref, out_ref, sems):
        copies = []
        for place in range(2 * half):
            source = own_ref.at[place] if place < half else other_ref.at[place - half]
            copies.append(
                pltpu.make_async_copy(source, out_ref.at[order_ref[place]], sems.at[place])
            )
        for copy in copies:
            copy.start()
        for copy in copies:
            copy.wait()

    return pl.pallas_call(
        body,
        out_shape=jax.ShapeDtypeStruct((2 * half, *shape[1:]), own.dtype),
        in_specs=[
            pl.BlockSpec(memory_space=pltpu.SMEM),
            pl.BlockSpec(memory_space=pl.ANY),
            pl.BlockSpec(memory_space=pl.ANY),
        ],
        out_specs=pl.BlockSpec(memory_space=pl.ANY),
        scratch_shapes=[pltpu.SemaphoreType.DMA((2 * half,))],
    )(order, own.reshape(shape), other.reshape(shape)).reshape(2 * half * rows, width)


def disassemble(order, matrix):
    blocks = order.shape[0]
    half = blocks // 2
    rows, width = matrix.shape[0] // blocks, matrix.shape[1]
    shape = (rows, width) if rows % 16 == 0 else (16, rows * width // 16)

    def body(order_ref, in_ref, own_ref, other_ref, sems):
        copies = []
        for place in range(blocks):
            target = own_ref.at[place] if place < half else other_ref.at[place - half]
            copies.append(
                pltpu.make_async_copy(in_ref.at[order_ref[place]], target, sems.at[place])
            )
        for copy in copies:
            copy.start()
        for copy in copies:
            copy.wait()

    own, other = pl.pallas_call(
        body,
        out_shape=[jax.ShapeDtypeStruct((half, *shape), matrix.dtype)] * 2,
        in_specs=[pl.BlockSpec(memory_space=pltpu.SMEM), pl.BlockSpec(memory_space=pl.ANY)],
        out_specs=[pl.BlockSpec(memory_space=pl.ANY)] * 2,
        scratch_shapes=[pltpu.SemaphoreType.DMA((blocks,))],
    )(order, matrix.reshape(blocks, *shape))
    return own.reshape(half, rows, width), other.reshape(half, rows, width)


def per_device(plan, inputs, image_ids, cotangent, gains, biases, w_qkv, w_out, w_in, w_mlp):
    me = lax.axis_index(AXES)
    order = plan.positions(me)
    gain_dev, bias_dev = gains.shape[1], biases.shape[1]
    small = jnp.concatenate([gains, biases], 1)
    rows = D // plan.devices
    first = jnp.concatenate([w_qkv.reshape(rows, 3 * D), w_out.reshape(rows, D)], 1)
    small_own, small_other = gather(plan, small)
    first_own, first_other = gather(plan, first)
    in_own, in_other = gather(plan, w_in.reshape(rows, FF))
    mlp_own, mlp_other = gather(plan, w_mlp.reshape(FF // plan.devices, D))
    placed = jnp.concatenate([small_own, small_other], 0)[:, 0]
    small_all = lax.dot_general(
        one_hot(order), placed, (((0,), (0,)), ((), ())), preferred_element_type=jnp.float32
    )
    gain_vec = small_all[:, :gain_dev].reshape(-1)
    bias_vec = small_all[:, gain_dev:].reshape(-1)
    matrix_first = assemble(order, first_own, first_other)
    matrix_qkv = matrix_first[:, : 3 * D]
    matrix_out = matrix_first[:, 3 * D :]
    matrix_in = assemble(order, in_own, in_other)
    matrix_mlp = assemble(order, mlp_own, mlp_other)
    blocks, length = image_ids.shape
    count = blocks * length
    scale = HEAD_DIM ** (-0.5)
    tokens = inputs.astype(jnp.float32).reshape(count, D)
    normed_one, inverse_one = normalize(tokens)
    entry = (normed_one * gain_vec[:D] + bias_vec[:D]).astype(jnp.bfloat16)
    bias_qkv = jnp.concatenate(
        [bias_vec[D : 2 * D], jnp.zeros((D,), jnp.float32), bias_vec[2 * D : 3 * D]]
    )
    project = (jnp.dot(entry, matrix_qkv, preferred_element_type=jnp.float32) + bias_qkv).astype(
        jnp.bfloat16
    )
    queries = project[:, :D].reshape(blocks, length, HEADS, HEAD_DIM)
    keys_all = project[:, D : 2 * D].reshape(blocks, length, HEADS, HEAD_DIM)
    values = project[:, 2 * D :].reshape(blocks, length, HEADS, HEAD_DIM)
    same_image = (image_ids[:, :, None] == image_ids[:, None, :])[:, None]
    scores = masked_scores(queries, keys_all, same_image, scale)
    ceiling = jnp.max(scores, axis=-1, keepdims=True)
    expo = jnp.exp(scores - ceiling)
    totals = jnp.sum(expo, axis=-1, keepdims=True)
    log_total = ceiling + jnp.log(totals)
    probs_low = (expo / totals).astype(jnp.bfloat16)
    mixed = (
        jnp.einsum("rhqk,rkhd->rqhd", probs_low, values, preferred_element_type=jnp.float32)
        .reshape(count, D)
        .astype(jnp.bfloat16)
    )
    middle = tokens + (
        jnp.dot(mixed, matrix_out, preferred_element_type=jnp.float32) + bias_vec[3 * D : 4 * D]
    )
    normed_two, inverse_two = normalize(middle)
    second = (normed_two * gain_vec[D:] + bias_vec[4 * D : 5 * D]).astype(jnp.bfloat16)
    hidden = jnp.dot(second, matrix_in, preferred_element_type=jnp.float32) + bias_vec[6 * D :]
    active, gelu_pull = jax.vjp(lambda point: jax.nn.gelu(point, approximate=False), hidden)
    active = active.astype(jnp.bfloat16)
    result = middle + (
        jnp.dot(active, matrix_mlp, preferred_element_type=jnp.float32) + bias_vec[5 * D : 6 * D]
    )
    output = result.reshape(blocks, length, D).astype(jnp.bfloat16)
    keep_rows = (image_ids.reshape(count, 1) >= 0).astype(jnp.float32)
    grad_out = cotangent.astype(jnp.float32).reshape(count, D) * keep_rows
    grad_top = grad_out.astype(jnp.bfloat16)
    grad_bias_mlp = column_sums(grad_top)
    grad_mlp = jnp.einsum(
        "nf,nd->fd", active, grad_top, preferred_element_type=jnp.float32
    ).astype(jnp.bfloat16)
    sum_mlp = scatter_sum(plan, *disassemble(order, grad_mlp))
    grad_active = jnp.einsum("nd,fd->nf", grad_top, matrix_mlp, preferred_element_type=jnp.float32)
    grad_hidden = gelu_pull(grad_active)[0].astype(jnp.bfloat16)
    grad_bias_in = column_sums(grad_hidden)
    grad_in = jnp.einsum(
        "nd,nf->df", second, grad_hidden, preferred_element_type=jnp.float32
    ).astype(jnp.bfloat16)
    sum_in = scatter_sum(plan, *disassemble(order, grad_in))
    grad_second = jnp.einsum(
        "nf,df->nd", grad_hidden, matrix_in, preferred_element_type=jnp.float32
    )
    grad_gain_two = jnp.sum(grad_second * normed_two, axis=0)
    grad_shift_two = jnp.sum(grad_second, axis=0)
    grad_middle = grad_out + norm_back(grad_second * gain_vec[D:], normed_two, inverse_two)
    grad_branch = grad_middle.astype(jnp.bfloat16)
    grad_bias_out = column_sums(grad_branch)
    grad_out_matrix = jnp.einsum(
        "nd,ne->de", mixed, grad_branch, preferred_element_type=jnp.float32
    ).astype(jnp.bfloat16)
    grad_mixed = (
        jnp.einsum("ne,de->nd", grad_branch, matrix_out, preferred_element_type=jnp.float32)
        .astype(jnp.bfloat16)
        .reshape(blocks, length, HEADS, HEAD_DIM)
    )
    probs_again = jnp.exp(masked_scores(queries, keys_all, same_image, scale) - log_total)
    grad_probs = jnp.einsum(
        "rqhd,rkhd->rhqk", grad_mixed, values, preferred_element_type=jnp.float32
    )
    grad_values = jnp.einsum(
        "rhqk,rqhd->rkhd",
        probs_again.astype(jnp.bfloat16),
        grad_mixed,
        preferred_element_type=jnp.float32,
    )
    grad_scores = (
        probs_again * (grad_probs - jnp.sum(probs_again * grad_probs, axis=-1, keepdims=True))
    ).astype(jnp.bfloat16)
    grad_queries = (
        jnp.einsum("rhqk,rkhd->rqhd", grad_scores, keys_all, preferred_element_type=jnp.float32)
        * scale
    )
    grad_keys = (
        jnp.einsum("rhqk,rqhd->rkhd", grad_scores, queries, preferred_element_type=jnp.float32)
        * scale
    )
    grad_project = jnp.concatenate(
        [
            grad_queries.reshape(count, D),
            grad_keys.reshape(count, D),
            grad_values.reshape(count, D),
        ],
        axis=1,
    ).astype(jnp.bfloat16)
    grad_bias_qkv = column_sums(grad_project)
    grad_qkv = jnp.einsum(
        "nd,ne->de", entry, grad_project, preferred_element_type=jnp.float32
    ).astype(jnp.bfloat16)
    sum_first = scatter_sum(
        plan, *disassemble(order, jnp.concatenate([grad_qkv, grad_out_matrix], 1))
    )
    grad_entry = jnp.einsum(
        "ne,de->nd", grad_project, matrix_qkv, preferred_element_type=jnp.float32
    )
    grad_gain_one = jnp.sum(grad_entry * normed_one, axis=0)
    grad_shift_one = jnp.sum(grad_entry, axis=0)
    grad_inputs = grad_middle + norm_back(grad_entry * gain_vec[:D], normed_one, inverse_one)
    flat_gains = jnp.concatenate([grad_gain_one, grad_gain_two]).reshape(-1, gain_dev)
    flat_biases = jnp.concatenate(
        [
            grad_shift_one,
            grad_bias_qkv[:D],
            grad_bias_qkv[2 * D :],
            grad_bias_out,
            grad_shift_two,
            grad_bias_mlp,
            grad_bias_in,
        ]
    ).reshape(-1, bias_dev)
    flat_small = jnp.concatenate([flat_gains, flat_biases], 1).astype(jnp.bfloat16)
    moved = jnp.dot(one_hot(order), flat_small, preferred_element_type=jnp.float32)
    moved = moved.astype(jnp.bfloat16)[:, None]
    sum_small = scatter_sum(plan, moved[: plan.half], moved[plan.half :])
    return (
        output,
        grad_inputs.reshape(blocks, length, D),
        sum_small[:, :gain_dev],
        sum_small[:, gain_dev:],
        sum_first[:, : 3 * D].reshape(1, -1),
        sum_first[:, 3 * D :].reshape(1, -1),
        sum_in.reshape(1, -1),
        sum_mlp.reshape(1, -1),
    )


def solution(mesh):
    plan = Plan(mesh)
    whole = P(AXES, None, None)
    flat = P(AXES, None)

    def body(*arrays):
        return per_device(plan, *arrays)

    return jax.shard_map(
        body,
        mesh=mesh,
        in_specs=(whole, flat, whole, flat, flat, flat, flat, flat, flat),
        out_specs=(whole, whole, flat, flat, flat, flat, flat, flat),
        check_vma=False,
    )
```

```python
import jax
import jax.numpy as jnp
from jax import lax
from jax.experimental import pallas as pl
from jax.experimental.pallas import tpu as pltpu
from jax.sharding import PartitionSpec as P

D = 1024
FF = 4096
HEADS = 16
HEAD_DIM = 64
SEQ = 256
AXES = ("dp", "fsdp")
BLOCKS = 32
GROUP = 4
WIDE = GROUP * HEAD_DIM
TILE = 512
CHUNK = 32
BF = jnp.bfloat16
F32 = jnp.float32

eps = 1e-06
ANY = pl.BlockSpec(memory_space=pl.ANY)
VMEM = pl.BlockSpec(memory_space=pltpu.VMEM)
SMEM = pl.BlockSpec(memory_space=pltpu.SMEM)


class Plan:
    def __init__(self, mesh):
        outer, inner = mesh.shape["dp"], mesh.shape["fsdp"]
        ys = outer // 2
        xs = min(ys, inner)
        zs = inner // xs
        self.devices = outer * inner
        self.half = self.devices // 2

        def bits(size, unit):
            found = []
            while size > 1:
                size //= 2
                found.append(size * unit)
            return found

        xbits = bits(xs, 1)
        zbits = bits(zs, xs)
        self.core = inner
        ybits = bits(ys, 2 * inner)
        self.orders = (zbits + xbits + ybits, zbits + ybits + xbits)
        self.stages = len(self.orders[0])

    def pairs(self, stage):
        return [
            (i, i ^ self.orders[1 if i & self.core else 0][stage]) for i in range(self.devices)
        ]

    def core_pairs(self):
        return [(i, i ^ self.core) for i in range(self.devices)]

    def masks(self, which):
        found = [0]
        for bit in self.orders[which]:
            found = found + [mask ^ bit for mask in found]
        return found

    def positions(self, me):
        tables = jnp.array(
            [
                self.masks(0) + [mask ^ self.core for mask in self.masks(1)],
                self.masks(1) + [mask ^ self.core for mask in self.masks(0)],
            ],
            jnp.int32,
        )
        mine = jnp.where((me & self.core) > 0, tables[1], tables[0])
        return mine ^ me


def gather(plan, block):
    held = block[None]
    for stage in range(plan.stages):
        held = jnp.concatenate([held, lax.ppermute(held, AXES, plan.pairs(stage))], 0)
    return held, lax.ppermute(held, AXES, plan.core_pairs())


def total(parts):
    result = parts[0].astype(F32)
    for part in parts[1:]:
        result = result + part.astype(F32)
    return result


def scatter_sum(plan, keep, send):
    parts = [keep, lax.ppermute(send, AXES, plan.core_pairs())]
    count = plan.half
    for stage in reversed(range(plan.stages)):
        count //= 2
        outgoing = total([part[count : 2 * count] for part in parts]).astype(BF)
        parts.append(lax.ppermute(outgoing, AXES, plan.pairs(stage)))
    return total([part[0] for part in parts])


def one_hot(order):
    return (order[:, None] == jnp.arange(order.shape[0])[None, :]).astype(BF)


def to_blocks(order, own, other):
    half, rows, width = own.shape
    if 2 * half == BLOCKS:
        return order, own, other
    joined = jnp.concatenate([own, other], 0).reshape(2 * half, rows * width)
    spread = lax.dot_general(
        one_hot(order), joined, (((0,), (0,)), ((), ())), preferred_element_type=BF
    ).reshape(2, BLOCKS // 2, -1, width)
    return jnp.arange(BLOCKS, dtype=jnp.int32), spread[0], spread[1]


def from_blocks(order, own, other):
    count = order.shape[0]
    if count == BLOCKS:
        return own, other
    half, _, width = own.shape
    joined = jnp.concatenate([own, other], 0).reshape(count, -1)
    moved = jnp.dot(one_hot(order), joined, preferred_element_type=BF).reshape(count, -1, width)
    return moved[: count // 2], moved[count // 2 :]


def params(limit):
    return pltpu.CompilerParams(vmem_limit_bytes=limit << 20)


def rows_of(ref, number, rows):
    return ref.at[pl.ds(pl.multiple_of(number * rows, rows), rows), :]


def fetches(order_ref, own_ref, other_ref, held_ref, sems, width=None):
    half, rows, _ = own_ref.shape
    copies = []
    for place in range(2 * half):
        source = own_ref.at[place] if place < half else other_ref.at[place - half]
        if width is not None:
            source = source.at[:, pl.ds(0, width)]
        number = order_ref[place]
        copies.append(
            pltpu.make_async_copy(source, rows_of(held_ref, number, rows), sems.at[number])
        )
    return copies


def stores(order_ref, held_ref, own_ref, other_ref, sems):
    half, rows, _ = own_ref.shape
    copies = []
    for place in list(range(half, 2 * half)) + list(range(half)):
        target = own_ref.at[place] if place < half else other_ref.at[place - half]
        copies.append(
            pltpu.make_async_copy(
                rows_of(held_ref, order_ref[place], rows), target, sems.at[place]
            )
        )
    return copies


def norm_parts(values):
    centre = values - jnp.mean(values, axis=-1, keepdims=True)
    inverse = lax.rsqrt(jnp.mean(centre * centre, axis=-1, keepdims=True) + eps)
    return centre * inverse, inverse


def norm_back(grad_norm, normed, inverse):
    return inverse * (
        grad_norm
        - jnp.mean(grad_norm, axis=-1, keepdims=True)
        - normed * jnp.mean(grad_norm * normed, axis=-1, keepdims=True)
    )


def span(index, size):
    return pl.ds(pl.multiple_of(index * size, size), size)


def dot(a, b):
    return jnp.dot(a, b, preferred_element_type=F32)


def dot_nt(a, b):
    return lax.dot_general(a, b, (((1,), (1,)), ((), ())), preferred_element_type=F32)


def dot_tn(a, b):
    return lax.dot_general(a, b, (((0,), (0,)), ((), ())), preferred_element_type=F32)


def stacked(values):
    head = lax.broadcasted_iota(jnp.int32, values.shape, 1) // HEAD_DIM
    zero = jnp.zeros_like(values)
    return jnp.concatenate([jnp.where(head == h, values, zero) for h in range(GROUP)], 0)


def unstacked(values):
    rows = values.shape[0] // GROUP
    head = lax.broadcasted_iota(jnp.int32, (rows, values.shape[1]), 1) // HEAD_DIM
    result = values[:rows]
    for h in range(1, GROUP):
        result = jnp.where(head == h, values[h * rows : (h + 1) * rows], result)
    return result


def attend_kernel(
    order_ref, vec_ref, x_ref, idr_ref, idc_ref, own_ref, other_ref,
    entry_ref, project_ref, probs_ref, mixed_ref, middle_ref, second_ref,
    held, project, probs, sems, out_sems,
):
    copies = fetches(order_ref, own_ref, other_ref, held, sems)
    for copy in copies:
        copy.start()
    count = x_ref.shape[0]

    @pl.loop(0, count // CHUNK)
    def _(i):
        normed, _ = norm_parts(x_ref[span(i, CHUNK), :].astype(F32))
        entry_ref[span(i, CHUNK), :] = (normed * vec_ref[0:1, :] + vec_ref[2:3, :]).astype(BF)

    for copy in copies:
        copy.wait()

    @pl.loop(0, 3 * D // TILE)
    def _(i):
        third = i // (D // TILE)
        column = span(lax.rem(i, D // TILE), TILE)
        bias_row = jnp.where(third == 0, 3, 4)
        bias = jnp.where(third == 1, 0.0, vec_ref[pl.ds(bias_row, 1), column])
        project[:, span(i, TILE)] = (dot(entry_ref[...], held[:, span(i, TILE)]) + bias).astype(BF)

    project_out = pltpu.make_async_copy(project, project_ref, out_sems.at[0])
    project_out.start()
    groups = D // WIDE

    @pl.loop(0, (count // SEQ) * groups)
    def _(i):
        row, group = i // groups, lax.rem(i, groups)
        rows = span(row, SEQ)
        queries = project[rows, span(group, WIDE)] * BF(HEAD_DIM**-0.5)
        keys = project[rows, span(groups + group, WIDE)]
        values = project[rows, span(2 * groups + group, WIDE)]
        scores = dot_nt(stacked(queries), keys)
        same = idc_ref[rows, :] == idr_ref[pl.ds(row, 1), :]
        scores = jnp.where(same[None], scores.reshape(GROUP, SEQ, SEQ), -1e9)
        expo = jnp.exp(scores - jnp.max(scores, axis=-1, keepdims=True))
        low = (expo / jnp.sum(expo, axis=-1, keepdims=True)).astype(BF)
        low = low.reshape(GROUP * SEQ, SEQ)
        probs[i] = low
        pltpu.make_async_copy(probs.at[i], probs_ref.at[i], out_sems.at[1 + i]).start()
        mixed_ref[rows, span(group, WIDE)] = unstacked(dot(low, values)).astype(BF)

    @pl.loop(0, D // TILE)
    def _(i):
        columns = span(i, TILE)
        branch = dot(mixed_ref[...], held[:, span(3 * D // TILE + i, TILE)])
        middle_ref[:, columns] = x_ref[:, columns].astype(F32) + (branch + vec_ref[5:6, columns])

    @pl.loop(0, count // CHUNK)
    def _(i):
        normed, _ = norm_parts(middle_ref[span(i, CHUNK), :])
        second_ref[span(i, CHUNK), :] = (normed * vec_ref[1:2, :] + vec_ref[6:7, :]).astype(BF)

    project_out.wait()
    for i in range((count // SEQ) * groups):
        pltpu.make_async_copy(probs.at[i], probs_ref.at[i], out_sems.at[1 + i]).wait()


def attend(order, vec, x, ids, own, other):
    count = x.shape[0]
    steps = (count // SEQ) * (D // WIDE)
    shape = jax.ShapeDtypeStruct
    return pl.pallas_call(
        attend_kernel,
        out_shape=[
            shape((count, D), BF),
            shape((count, 3 * D), BF),
            shape((steps, GROUP * SEQ, SEQ), BF),
            shape((count, D), BF),
            shape((count, D), F32),
            shape((count, D), BF),
        ],
        in_specs=[SMEM, VMEM, VMEM, VMEM, VMEM, ANY, ANY],
        out_specs=[VMEM, ANY, ANY, VMEM, VMEM, VMEM],
        scratch_shapes=[
            pltpu.VMEM((D, 4 * D), BF),
            pltpu.VMEM((count, 3 * D), BF),
            pltpu.VMEM((steps, GROUP * SEQ, SEQ), BF),
            pltpu.SemaphoreType.DMA((BLOCKS,)),
            pltpu.SemaphoreType.DMA((1 + steps,)),
        ],
        compiler_params=params(48),
        name="attend",
    )(order, vec, x, ids, ids.reshape(count, 1), own, other)


def rise_kernel(
    order_ref, spot_ref, bias_ref, second_ref, top_ref, own_ref, other_ref,
    active_ref, slope_ref, gown_ref, gother_ref,
    held, grads, sems, out_sems,
):
    step = pl.program_id(0)
    half, rows, _ = gown_ref.shape

    @pl.when(step == 0)
    def _():
        copies = fetches(order_ref, own_ref, other_ref, held, sems)
        for copy in copies:
            copy.start()
        for copy in copies:
            copy.wait()

    hidden = dot(second_ref[...], held[:, span(step, TILE)]) + bias_ref[...]
    cdf = 0.5 + 0.5 * lax.erf(hidden * (0.5**0.5))
    slope = cdf + hidden * jnp.exp(-0.5 * hidden * hidden) * 0.3989422804014327
    active = (hidden * cdf).astype(BF)
    active_ref[...] = active
    slope_ref[...] = slope.astype(BF)
    grads[span(step, TILE), :] = dot_tn(active, top_ref[...]).astype(BF)
    for block in range(TILE // rows):
        number = step * (TILE // rows) + block
        place = spot_ref[number]

        @pl.when(place < half)
        def _():
            pltpu.make_async_copy(
                rows_of(grads, number, rows), gown_ref.at[place], out_sems.at[number]
            ).start()

        @pl.when(place >= half)
        def _():
            pltpu.make_async_copy(
                rows_of(grads, number, rows), gother_ref.at[place - half], out_sems.at[number]
            ).start()

    @pl.when(step == FF // TILE - 1)
    def _():
        for number in range(2 * half):
            pltpu.make_async_copy(
                rows_of(grads, number, rows), gown_ref.at[0], out_sems.at[number]
            ).wait()


def rise(order, spot, bias, second, top, own, other):
    count = second.shape[0]
    shape = jax.ShapeDtypeStruct
    whole = pl.BlockSpec((count, D), lambda t: (0, 0))
    columns = pl.BlockSpec((count, TILE), lambda t: (0, t))
    grad = shape((BLOCKS // 2, FF // BLOCKS, D), BF)
    return pl.pallas_call(
        rise_kernel,
        grid=(FF // TILE,),
        out_shape=[shape((count, FF), BF), shape((count, FF), BF), grad, grad],
        in_specs=[SMEM, SMEM, pl.BlockSpec((1, TILE), lambda t: (0, t)), whole, whole, ANY, ANY],
        out_specs=[columns, columns, ANY, ANY],
        scratch_shapes=[
            pltpu.VMEM((D, FF), BF),
            pltpu.VMEM((FF, D), BF),
            pltpu.SemaphoreType.DMA((BLOCKS,)),
            pltpu.SemaphoreType.DMA((BLOCKS,)),
        ],
        compiler_params=params(48),
        name="rise",
    )(order, spot, bias, second, top, own, other)


def fall_kernel(
    order_ref, top_ref, slope_ref, second_ref, mown_ref, mother_ref, iown_ref, iother_ref,
    gsecond_ref, bias_ref, gown_ref, gother_ref,
    mheld, iheld, turned, grads, msems, isems, out_sems,
):
    step = pl.program_id(0)
    rows = mown_ref.shape[1]

    @pl.when(step == 0)
    def _():
        for copy in fetches(order_ref, mown_ref, mother_ref, mheld, msems):
            copy.start()
        for copy in fetches(order_ref, iown_ref, iother_ref, iheld, isems):
            copy.start()
        turned[...] = second_ref[...].T

    for block in range(TILE // rows):
        number = step * (TILE // rows) + block
        pltpu.make_async_copy(
            mown_ref.at[0], rows_of(mheld, number, rows), msems.at[number]
        ).wait()
    grad_active = dot_nt(top_ref[...], mheld[span(step, TILE), :])
    grad_hidden = (grad_active * slope_ref[...].astype(F32)).astype(BF)
    bias_ref[...] = jnp.sum(grad_hidden.astype(F32), axis=0, keepdims=True)
    grads[:, span(step, TILE)] = dot(turned[...], grad_hidden).astype(BF)

    @pl.when(step == 0)
    def _():
        for copy in fetches(order_ref, iown_ref, iother_ref, iheld, isems):
            copy.wait()
        gsecond_ref[...] = jnp.zeros_like(gsecond_ref)

    gsecond_ref[...] += dot_nt(grad_hidden, iheld[:, span(step, TILE)])

    @pl.when(step == FF // TILE - 1)
    def _():
        copies = stores(order_ref, grads, gown_ref, gother_ref, out_sems)
        for copy in copies:
            copy.start()
        for copy in copies:
            copy.wait()


def fall(order, top, slope, second, mlp, win):
    count = second.shape[0]
    shape = jax.ShapeDtypeStruct
    whole = pl.BlockSpec((count, D), lambda t: (0, 0))
    grad = shape((BLOCKS // 2, D // BLOCKS, FF), BF)
    return pl.pallas_call(
        fall_kernel,
        grid=(FF // TILE,),
        out_shape=[shape((count, D), F32), shape((1, FF), F32), grad, grad],
        in_specs=[
            SMEM, whole, pl.BlockSpec((count, TILE), lambda t: (0, t)), whole, ANY, ANY, ANY, ANY,
        ],
        out_specs=[whole, pl.BlockSpec((1, TILE), lambda t: (0, t)), ANY, ANY],
        scratch_shapes=[
            pltpu.VMEM((FF, D), BF),
            pltpu.VMEM((D, FF), BF),
            pltpu.VMEM((D, count), BF),
            pltpu.VMEM((D, FF), BF),
            pltpu.SemaphoreType.DMA((BLOCKS,)),
            pltpu.SemaphoreType.DMA((BLOCKS,)),
            pltpu.SemaphoreType.DMA((BLOCKS,)),
        ],
        compiler_params=params(56),
        name="fall",
    )(order, top, slope, second, *mlp, *win)


def unattend_kernel(
    order_ref, vec_ref, gsecond_ref, middle_ref, top_ref, mixed_ref, entry_ref, project_ref,
    probs_ref, own_ref, other_ref,
    gmiddle_ref, gproject_ref, sums_ref, gown_ref, gother_ref,
    held, branch, gmixed, turned, grads, sems, out_sems,
):
    copies = fetches(order_ref, own_ref, other_ref, held, sems)
    for copy in copies:
        copy.start()
    count = middle_ref.shape[0]
    sums_ref[...] = jnp.zeros_like(sums_ref)

    @pl.loop(0, count // CHUNK)
    def _(i):
        rows = span(i, CHUNK)
        normed, inverse = norm_parts(middle_ref[rows, :])
        grad = gsecond_ref[rows, :]
        sums_ref[0:1, :] += jnp.sum(grad * normed, axis=0, keepdims=True)
        sums_ref[1:2, :] += jnp.sum(grad, axis=0, keepdims=True)
        top = top_ref[rows, :].astype(F32)
        sums_ref[3:4, :] += jnp.sum(top, axis=0, keepdims=True)
        gmiddle = top + norm_back(grad * vec_ref[1:2, :], normed, inverse)
        gmiddle_ref[rows, :] = gmiddle
        low = gmiddle.astype(BF)
        branch[rows, :] = low
        sums_ref[2:3, :] += jnp.sum(low.astype(F32), axis=0, keepdims=True)

    turned[...] = mixed_ref[...].T
    for copy in copies:
        copy.wait()

    @pl.loop(0, D // TILE)
    def _(i):
        columns = span(i, TILE)
        grads[:, span(3 * D // TILE + i, TILE)] = dot(turned[...], branch[:, columns]).astype(BF)
        gmixed[:, columns] = dot_nt(branch[...], held[columns, 3 * D :]).astype(BF)

    turned[...] = entry_ref[...].T
    groups = D // WIDE

    @pl.loop(0, (count // SEQ) * groups)
    def _(i):
        row, group = i // groups, lax.rem(i, groups)
        rows = span(row, SEQ)
        scale = HEAD_DIM**-0.5
        queries = stacked(project_ref[rows, span(group, WIDE)] * BF(scale))
        keys = project_ref[rows, span(groups + group, WIDE)]
        values = project_ref[rows, span(2 * groups + group, WIDE)]
        gmix = stacked(gmixed[rows, span(group, WIDE)])
        low = probs_ref[i]
        gprobs = dot_nt(gmix, values)
        gvalues = dot_tn(low, gmix)
        weight = low.astype(F32)
        inner = jnp.sum(weight * gprobs, axis=-1, keepdims=True)
        gscores = (weight * (gprobs - inner)).astype(BF)
        gqueries = unstacked(dot(gscores, keys)) * scale
        gkeys = dot_tn(gscores, queries)
        gproject_ref[rows, span(group, WIDE)] = gqueries.astype(BF)
        gproject_ref[rows, span(groups + group, WIDE)] = gkeys.astype(BF)
        gproject_ref[rows, span(2 * groups + group, WIDE)] = gvalues.astype(BF)

    @pl.loop(0, 3 * D // TILE)
    def _(i):
        gpart = gproject_ref[:, span(i, TILE)]
        grads[:, span(i, TILE)] = dot(turned[...], gpart).astype(BF)
        third = i // (D // TILE)
        column = span(lax.rem(i, D // TILE), TILE)
        sums_ref[pl.ds(4 + third, 1), column] = jnp.sum(gpart.astype(F32), axis=0, keepdims=True)

    copies = stores(order_ref, grads, gown_ref, gother_ref, out_sems)
    for copy in copies:
        copy.start()
    for copy in copies:
        copy.wait()


def unattend(order, vec, gsecond, middle, top, mixed, entry, project, probs, first):
    count = middle.shape[0]
    shape = jax.ShapeDtypeStruct
    grad = shape((BLOCKS // 2, D // BLOCKS, 4 * D), BF)
    return pl.pallas_call(
        unattend_kernel,
        out_shape=[
            shape((count, D), F32), shape((count, 3 * D), BF), shape((8, D), F32), grad, grad,
        ],
        in_specs=[SMEM] + [VMEM] * 8 + [ANY] * 2,
        out_specs=[VMEM] * 3 + [ANY] * 2,
        scratch_shapes=[
            pltpu.VMEM((D, 4 * D), BF),
            pltpu.VMEM((count, D), BF),
            pltpu.VMEM((count, D), BF),
            pltpu.VMEM((D, count), BF),
            pltpu.VMEM((D, 4 * D), BF),
            pltpu.SemaphoreType.DMA((BLOCKS,)),
            pltpu.SemaphoreType.DMA((BLOCKS,)),
        ],
        compiler_params=params(56),
        name="unattend",
    )(order, vec, gsecond, middle, top, mixed, entry, project, probs, *first)


def enter_kernel(
    order_ref, vec_ref, x_ref, gmiddle_ref, gproject_ref, own_ref, other_ref,
    ginputs_ref, sums_ref,
    held, gentry, sems,
):
    copies = fetches(order_ref, own_ref, other_ref, held, sems, 3 * D)
    for copy in copies:
        copy.start()
    count = x_ref.shape[0]
    sums_ref[...] = jnp.zeros_like(sums_ref)
    for copy in copies:
        copy.wait()

    @pl.loop(0, D // TILE)
    def _(i):
        gentry[:, span(i, TILE)] = dot_nt(gproject_ref[...], held[span(i, TILE), :])

    @pl.loop(0, count // CHUNK)
    def _(i):
        rows = span(i, CHUNK)
        normed, inverse = norm_parts(x_ref[rows, :].astype(F32))
        grad = gentry[rows, :]
        sums_ref[0:1, :] += jnp.sum(grad * normed, axis=0, keepdims=True)
        sums_ref[1:2, :] += jnp.sum(grad, axis=0, keepdims=True)
        back = norm_back(grad * vec_ref[0:1, :], normed, inverse)
        ginputs_ref[rows, :] = gmiddle_ref[rows, :] + back


def enter(order, vec, x, gmiddle, gproject, first):
    count = x.shape[0]
    shape = jax.ShapeDtypeStruct
    return pl.pallas_call(
        enter_kernel,
        out_shape=[shape((count, D), F32), shape((8, D), F32)],
        in_specs=[SMEM] + [VMEM] * 4 + [ANY] * 2,
        out_specs=[VMEM] * 2,
        scratch_shapes=[
            pltpu.VMEM((D, 3 * D), BF),
            pltpu.VMEM((count, D), F32),
            pltpu.SemaphoreType.DMA((BLOCKS,)),
        ],
        compiler_params=params(48),
        name="enter",
    )(order, vec, x, gmiddle, gproject, *first)


def finish_kernel(order_ref, vec_ref, middle_ref, active_ref, own_ref, other_ref, out_ref, held, sems):
    copies = fetches(order_ref, own_ref, other_ref, held, sems)
    for copy in copies:
        copy.start()
    for copy in copies:
        copy.wait()

    @pl.loop(0, D // WIDE)
    def _(i):
        columns = span(i, WIDE)
        result = dot(active_ref[...], held[:, columns]) + vec_ref[7:8, columns]
        out_ref[:, columns] = (middle_ref[:, columns] + result).astype(BF)


def finish(order, vec, middle, active, mlp):
    count = middle.shape[0]
    return pl.pallas_call(
        finish_kernel,
        out_shape=jax.ShapeDtypeStruct((count, D), BF),
        in_specs=[SMEM] + [VMEM] * 3 + [ANY] * 2,
        out_specs=VMEM,
        scratch_shapes=[pltpu.VMEM((FF, D), BF), pltpu.SemaphoreType.DMA((BLOCKS,))],
        compiler_params=params(48),
        name="finish",
    )(order, vec, middle, active, *mlp)


def per_device(plan, inputs, image_ids, cotangent, gains, biases, w_qkv, w_out, w_in, w_mlp):
    me = lax.axis_index(AXES)
    order = plan.positions(me)
    gain_dev, bias_dev = gains.shape[1], biases.shape[1]
    small = jnp.concatenate([gains, biases], 1)
    rows = D // plan.devices
    first = jnp.concatenate([w_qkv.reshape(rows, 3 * D), w_out.reshape(rows, D)], 1)
    first = gather(plan, first)
    small_own, small_other = gather(plan, small)
    win = gather(plan, w_in.reshape(rows, FF))
    mlp = gather(plan, w_mlp.reshape(FF // plan.devices, D))
    placed = jnp.concatenate([small_own, small_other], 0)[:, 0]
    small_all = lax.dot_general(
        one_hot(order), placed, (((0,), (0,)), ((), ())), preferred_element_type=F32
    )
    vec = jnp.concatenate(
        [small_all[:, :gain_dev].reshape(-1), small_all[:, gain_dev:].reshape(-1)]
    ).reshape(-1, D)
    bias_in = vec[8:12].reshape(1, FF)
    vec = vec[:8]
    numbers, *first = to_blocks(order, *first)
    _, *win = to_blocks(order, *win)
    _, *mlp = to_blocks(order, *mlp)
    spot = jnp.sum(
        jnp.where(numbers[:, None] == jnp.arange(BLOCKS)[None, :], jnp.arange(BLOCKS)[:, None], 0),
        axis=0,
    ).astype(jnp.int32)
    blocks, length = image_ids.shape
    count = blocks * length
    x = inputs.reshape(count, D)
    top = jnp.where(image_ids.reshape(count, 1) >= 0, cotangent.reshape(count, D), BF(0))
    entry, project, probs, mixed, middle, second = attend(numbers, vec, x, image_ids, *first)
    active, slope, *grad_mlp = rise(numbers, spot, bias_in, second, top, *win)
    sum_mlp = scatter_sum(plan, *from_blocks(order, *grad_mlp))
    gsecond, grad_bias_in, *grad_in = fall(numbers, top, slope, second, mlp, win)
    sum_in = scatter_sum(plan, *from_blocks(order, *grad_in))
    gmiddle, gproject, sums, *grad_first = unattend(
        numbers, vec, gsecond, middle, top, mixed, entry, project, probs, first
    )
    sum_first = scatter_sum(plan, *from_blocks(order, *grad_first))
    grad_inputs, sums_one = enter(numbers, vec, x, gmiddle, gproject, first)
    output = finish(numbers, vec, middle, active, mlp)
    flat_gains = jnp.concatenate([sums_one[0], sums[0]]).reshape(-1, gain_dev)
    flat_biases = jnp.concatenate(
        [sums_one[1], sums[4], sums[6], sums[2], sums[1], sums[3], grad_bias_in[0]]
    ).reshape(-1, bias_dev)
    flat_small = jnp.concatenate([flat_gains, flat_biases], 1).astype(BF)
    moved = jnp.dot(one_hot(order), flat_small, preferred_element_type=F32).astype(BF)[:, None]
    sum_small = scatter_sum(plan, moved[: plan.half], moved[plan.half :])
    return (
        output.reshape(blocks, length, D),
        grad_inputs.reshape(blocks, length, D),
        sum_small[:, :gain_dev],
        sum_small[:, gain_dev:],
        sum_first[:, : 3 * D].reshape(1, -1),
        sum_first[:, 3 * D :].reshape(1, -1),
        sum_in.reshape(1, -1),
        sum_mlp.reshape(1, -1),
    )


def solution(mesh):
    plan = Plan(mesh)
    whole = P(AXES, None, None)
    flat = P(AXES, None)

    def body(*arrays):
        return per_device(plan, *arrays)

    return jax.shard_map(
        body,
        mesh=mesh,
        in_specs=(whole, flat, whole, flat, flat, flat, flat, flat, flat),
        out_specs=(whole, whole, flat, flat, flat, flat, flat, flat),
        check_vma=False,
    )
```

```python
import jax
import jax.numpy as jnp
from jax import lax
from jax.experimental import pallas as pl
from jax.experimental.pallas import tpu as pltpu
from jax.sharding import PartitionSpec as P

D = 1024
FF = 4096
HEADS = 16
HEAD_DIM = 64
SEQ = 256
AXES = ("dp", "fsdp")
BLOCKS = 32
GROUP = 4
WIDE = GROUP * HEAD_DIM
TILE = 512
CHUNK = 32
BF = jnp.bfloat16
F32 = jnp.float32

eps = 1e-06
ANY = pl.BlockSpec(memory_space=pl.ANY)
VMEM = pl.BlockSpec(memory_space=pltpu.VMEM)
SMEM = pl.BlockSpec(memory_space=pltpu.SMEM)


class Plan:
    def __init__(self, mesh):
        outer, inner = mesh.shape["dp"], mesh.shape["fsdp"]
        ys = outer // 2
        xs = min(ys, inner)
        zs = inner // xs
        self.devices = outer * inner
        self.half = self.devices // 2

        def bits(size, unit):
            found = []
            while size > 1:
                size //= 2
                found.append(size * unit)
            return found

        xbits = bits(xs, 1)
        zbits = bits(zs, xs)
        self.core = inner
        ybits = bits(ys, 2 * inner)
        self.orders = (zbits + xbits + ybits, zbits + ybits + xbits)
        self.legs = [list(range(1)), list(range(1, len(zbits)))]
        for _ in range(2):
            start = self.legs[-1][-1] + 1
            self.legs.append(list(range(start, start + len(xbits))))

    def pairs(self, stage):
        return [
            (i, i ^ self.orders[1 if i & self.core else 0][stage]) for i in range(self.devices)
        ]

    def core_pairs(self):
        return [(i, i ^ self.core) for i in range(self.devices)]

    def masks(self, which):
        found = [0]
        for bit in self.orders[which]:
            found = found + [mask ^ bit for mask in found]
        return found

    def positions(self, me):
        tables = jnp.array(
            [
                self.masks(0) + [mask ^ self.core for mask in self.masks(1)],
                self.masks(1) + [mask ^ self.core for mask in self.masks(0)],
            ],
            jnp.int32,
        )
        mine = jnp.where((me & self.core) > 0, tables[1], tables[0])
        return mine ^ me


class Line:
    def __init__(self):
        self.last = []

    def tie(self, *arrays):
        if not self.last:
            return arrays
        tied = lax.optimization_barrier((arrays, tuple(self.last)))
        return tied[0]

    def run(self, step, *arrays):
        result = step(*self.tie(*arrays))
        self.last = [result[0] if isinstance(result, (list, tuple)) else result]
        return result

    def send(self, array, pairs):
        return lax.ppermute(self.tie(array)[0], AXES, pairs)

    def wait(self, *arrays):
        self.last.extend(arrays)


class Gather:
    def __init__(self, plan, line, block):
        self.plan, self.line = plan, line
        self.held = block[None]
        self.coming = None

    def take(self):
        self.line.wait(self.coming)
        self.held = self.line.run(
            lambda held, coming: jnp.concatenate([held, coming], 0), self.held, self.coming
        )

    def start(self, leg):
        for stage in self.plan.legs[leg]:
            if stage != self.plan.legs[leg][0]:
                self.take()
            self.coming = self.line.send(self.held, self.plan.pairs(stage))

    def swap_first(self):
        self.first = self.line.send(self.held, self.plan.core_pairs())

    def arrive(self):
        self.line.wait(self.coming)

    def swap_second(self):
        self.second = self.line.send(self.coming, self.plan.core_pairs())

    def parts(self):
        self.line.wait(self.first, self.second)
        return [self.held, self.coming, self.first, self.second]


def total(parts):
    result = parts[0].astype(F32)
    for part in parts[1:]:
        result = result + part.astype(F32)
    return result


class Scatter:
    def __init__(self, plan, line, parts):
        self.plan, self.line = plan, line
        keep_low, keep_high, send_low, send_high = parts
        self.high = [keep_high, line.send(send_high, plan.core_pairs())]
        self.low = [keep_low, line.send(send_low, plan.core_pairs())]
        self.count = keep_low.shape[0]

    def start(self, leg):
        for stage in reversed(self.plan.legs[leg]):
            if self.high is not None:
                parts, self.high, low = self.high, None, 0
            else:
                self.count //= 2
                parts, low = self.low, self.count
            self.line.wait(parts[-1])

            def add(*parts, low=low, high=low + self.count):
                return total([part[low:high] for part in parts]).astype(BF)

            outgoing = self.line.run(add, *parts)
            self.low.append(self.line.send(outgoing, self.plan.pairs(stage)))

    def result(self, *shape):
        self.line.wait(self.low[-1])
        return self.line.run(lambda *parts: total([part[0] for part in parts]), *self.low)


def one_hot(order):
    return (order[:, None] == jnp.arange(order.shape[0])[None, :]).astype(BF)


def to_blocks(order, parts):
    if order.shape[0] == BLOCKS:
        return parts
    width = parts[0].shape[-1]
    joined = jnp.concatenate(parts, 0).reshape(order.shape[0], -1)
    spread = lax.dot_general(
        one_hot(order), joined, (((0,), (0,)), ((), ())), preferred_element_type=BF
    ).reshape(4, BLOCKS // 4, -1, width)
    return [spread[i] for i in range(4)]


def from_blocks(order, parts):
    count = order.shape[0]
    if count == BLOCKS:
        return parts
    width = parts[0].shape[-1]
    joined = jnp.concatenate(parts, 0).reshape(count, -1)
    moved = jnp.dot(one_hot(order), joined, preferred_element_type=BF)
    moved = moved.reshape(4, count // 4, -1, width)
    return [moved[i] for i in range(4)]


def params(limit):
    return pltpu.CompilerParams(vmem_limit_bytes=limit << 20)


def rows_of(ref, number, rows):
    return ref.at[pl.ds(pl.multiple_of(number * rows, rows), rows), :]


def fetches(order_ref, part_refs, held_ref, sems, width=None):
    each, rows, _ = part_refs[0].shape
    copies = []
    for place in range(BLOCKS):
        source = part_refs[place // each].at[place % each]
        if width is not None:
            source = source.at[:, pl.ds(0, width)]
        number = order_ref[place]
        copies.append(
            pltpu.make_async_copy(source, rows_of(held_ref, number, rows), sems.at[number])
        )
    return copies


def stores(order_ref, held_ref, part_refs, sems):
    each, rows, _ = part_refs[0].shape
    copies = []
    for place in reversed(range(BLOCKS)):
        target = part_refs[place // each].at[place % each]
        copies.append(
            pltpu.make_async_copy(
                rows_of(held_ref, order_ref[place], rows), target, sems.at[place]
            )
        )
    return copies


def norm_parts(values):
    centre = values - jnp.mean(values, axis=-1, keepdims=True)
    inverse = lax.rsqrt(jnp.mean(centre * centre, axis=-1, keepdims=True) + eps)
    return centre * inverse, inverse


def norm_back(grad_norm, normed, inverse):
    return inverse * (
        grad_norm
        - jnp.mean(grad_norm, axis=-1, keepdims=True)
        - normed * jnp.mean(grad_norm * normed, axis=-1, keepdims=True)
    )


def span(index, size):
    return pl.ds(pl.multiple_of(index * size, size), size)


def dot(a, b):
    return jnp.dot(a, b, preferred_element_type=F32)


def dot_nt(a, b):
    return lax.dot_general(a, b, (((1,), (1,)), ((), ())), preferred_element_type=F32)


def dot_tn(a, b):
    return lax.dot_general(a, b, (((0,), (0,)), ((), ())), preferred_element_type=F32)


def stacked(values):
    head = lax.broadcasted_iota(jnp.int32, values.shape, 1) // HEAD_DIM
    zero = jnp.zeros_like(values)
    return jnp.concatenate([jnp.where(head == h, values, zero) for h in range(GROUP)], 0)


def unstacked(values):
    rows = values.shape[0] // GROUP
    head = lax.broadcasted_iota(jnp.int32, (rows, values.shape[1]), 1) // HEAD_DIM
    result = values[:rows]
    for h in range(1, GROUP):
        result = jnp.where(head == h, values[h * rows : (h + 1) * rows], result)
    return result


def attend_kernel(
    order_ref, vec_ref, x_ref, idr_ref, idc_ref, w0, w1, w2, w3,
    entry_ref, project_ref, probs_ref, mixed_ref, middle_ref, second_ref,
    held, project, probs, sems, out_sems,
):
    copies = fetches(order_ref, (w0, w1, w2, w3), held, sems)
    for copy in copies:
        copy.start()
    count = x_ref.shape[0]

    @pl.loop(0, count // CHUNK)
    def _(i):
        normed, _ = norm_parts(x_ref[span(i, CHUNK), :].astype(F32))
        entry_ref[span(i, CHUNK), :] = (normed * vec_ref[0:1, :] + vec_ref[2:3, :]).astype(BF)

    for copy in copies:
        copy.wait()

    @pl.loop(0, 3 * D // TILE)
    def _(i):
        third = i // (D // TILE)
        column = span(lax.rem(i, D // TILE), TILE)
        bias_row = jnp.where(third == 0, 3, 4)
        bias = jnp.where(third == 1, 0.0, vec_ref[pl.ds(bias_row, 1), column])
        project[:, span(i, TILE)] = (dot(entry_ref[...], held[:, span(i, TILE)]) + bias).astype(BF)

    project_out = pltpu.make_async_copy(project, project_ref, out_sems.at[0])
    project_out.start()
    groups = D // WIDE

    @pl.loop(0, (count // SEQ) * groups)
    def _(i):
        row, group = i // groups, lax.rem(i, groups)
        rows = span(row, SEQ)
        queries = project[rows, span(group, WIDE)] * BF(HEAD_DIM**-0.5)
        keys = project[rows, span(groups + group, WIDE)]
        values = project[rows, span(2 * groups + group, WIDE)]
        scores = dot_nt(stacked(queries), keys)
        same = idc_ref[rows, :] == idr_ref[pl.ds(row, 1), :]
        scores = jnp.where(same[None], scores.reshape(GROUP, SEQ, SEQ), -1e9)
        expo = jnp.exp(scores - jnp.max(scores, axis=-1, keepdims=True))
        low = (expo / jnp.sum(expo, axis=-1, keepdims=True)).astype(BF)
        low = low.reshape(GROUP * SEQ, SEQ)
        probs[i] = low
        pltpu.make_async_copy(probs.at[i], probs_ref.at[i], out_sems.at[1 + i]).start()
        mixed_ref[rows, span(group, WIDE)] = unstacked(dot(low, values)).astype(BF)

    @pl.loop(0, D // TILE)
    def _(i):
        columns = span(i, TILE)
        branch = dot(mixed_ref[...], held[:, span(3 * D // TILE + i, TILE)])
        middle_ref[:, columns] = x_ref[:, columns].astype(F32) + (branch + vec_ref[5:6, columns])

    @pl.loop(0, count // CHUNK)
    def _(i):
        normed, _ = norm_parts(middle_ref[span(i, CHUNK), :])
        second_ref[span(i, CHUNK), :] = (normed * vec_ref[1:2, :] + vec_ref[6:7, :]).astype(BF)

    project_out.wait()
    for i in range((count // SEQ) * groups):
        pltpu.make_async_copy(probs.at[i], probs_ref.at[i], out_sems.at[1 + i]).wait()


def attend(order, vec, x, ids, *first):
    count = x.shape[0]
    steps = (count // SEQ) * (D // WIDE)
    shape = jax.ShapeDtypeStruct
    return pl.pallas_call(
        attend_kernel,
        out_shape=[
            shape((count, D), BF),
            shape((count, 3 * D), BF),
            shape((steps, GROUP * SEQ, SEQ), BF),
            shape((count, D), BF),
            shape((count, D), F32),
            shape((count, D), BF),
        ],
        in_specs=[SMEM] + [VMEM] * 4 + [ANY] * 4,
        out_specs=[VMEM, ANY, ANY, VMEM, VMEM, VMEM],
        scratch_shapes=[
            pltpu.VMEM((D, 4 * D), BF),
            pltpu.VMEM((count, 3 * D), BF),
            pltpu.VMEM((steps, GROUP * SEQ, SEQ), BF),
            pltpu.SemaphoreType.DMA((BLOCKS,)),
            pltpu.SemaphoreType.DMA((1 + steps,)),
        ],
        compiler_params=params(48),
        name="attend",
    )(order, vec, x, ids, ids.reshape(count, 1), *first)


def rise_kernel(
    order_ref, spot_ref, bias_ref, second_ref, top_ref, w0, w1, w2, w3,
    active_ref, slope_ref, g0, g1, g2, g3,
    held, grads, sems, out_sems,
):
    step = pl.program_id(0)
    each, rows, _ = g0.shape

    @pl.when(step == 0)
    def _():
        copies = fetches(order_ref, (w0, w1, w2, w3), held, sems)
        for copy in copies:
            copy.start()
        for copy in copies:
            copy.wait()

    hidden = dot(second_ref[...], held[:, span(step, TILE)]) + bias_ref[...]
    cdf = 0.5 + 0.5 * lax.erf(hidden * (0.5**0.5))
    slope = cdf + hidden * jnp.exp(-0.5 * hidden * hidden) * 0.3989422804014327
    active = (hidden * cdf).astype(BF)
    active_ref[...] = active
    slope_ref[...] = slope.astype(BF)
    grads[span(step, TILE), :] = dot_tn(active, top_ref[...]).astype(BF)
    for block in range(TILE // rows):
        number = step * (TILE // rows) + block
        place = spot_ref[number]

        for part, target in enumerate((g0, g1, g2, g3)):

            @pl.when(place // each == part)
            def _(part=part, target=target):
                pltpu.make_async_copy(
                    rows_of(grads, number, rows),
                    target.at[place - part * each],
                    out_sems.at[number],
                ).start()

    @pl.when(step == FF // TILE - 1)
    def _():
        for number in range(BLOCKS):
            pltpu.make_async_copy(
                rows_of(grads, number, rows), g0.at[0], out_sems.at[number]
            ).wait()


def rise(order, spot, bias, second, top, *win):
    count = second.shape[0]
    shape = jax.ShapeDtypeStruct
    whole = pl.BlockSpec((count, D), lambda t: (0, 0))
    columns = pl.BlockSpec((count, TILE), lambda t: (0, t))
    grad = shape((BLOCKS // 4, FF // BLOCKS, D), BF)
    return pl.pallas_call(
        rise_kernel,
        grid=(FF // TILE,),
        out_shape=[shape((count, FF), BF)] * 2 + [grad] * 4,
        in_specs=[SMEM, SMEM, pl.BlockSpec((1, TILE), lambda t: (0, t)), whole, whole] + [ANY] * 4,
        out_specs=[columns] * 2 + [ANY] * 4,
        scratch_shapes=[
            pltpu.VMEM((D, FF), BF),
            pltpu.VMEM((FF, D), BF),
            pltpu.SemaphoreType.DMA((BLOCKS,)),
            pltpu.SemaphoreType.DMA((BLOCKS,)),
        ],
        compiler_params=params(48),
        name="rise",
    )(order, spot, bias, second, top, *win)


def fall_kernel(
    order_ref, top_ref, slope_ref, second_ref, w0, w1, w2, w3,
    ghidden_ref, bias_ref, g0, g1, g2, g3,
    held, turned, grads, sems, out_sems,
):
    step = pl.program_id(0)
    rows = w0.shape[1]

    @pl.when(step == 0)
    def _():
        for copy in fetches(order_ref, (w0, w1, w2, w3), held, sems):
            copy.start()
        turned[...] = second_ref[...].T

    for block in range(TILE // rows):
        number = step * (TILE // rows) + block
        pltpu.make_async_copy(w0.at[0], rows_of(held, number, rows), sems.at[number]).wait()
    grad_active = dot_nt(top_ref[...], held[span(step, TILE), :])
    grad_hidden = (grad_active * slope_ref[...].astype(F32)).astype(BF)
    ghidden_ref[...] = grad_hidden
    bias_ref[...] = jnp.sum(grad_hidden.astype(F32), axis=0, keepdims=True)
    grads[:, span(step, TILE)] = dot(turned[...], grad_hidden).astype(BF)

    @pl.when(step == FF // TILE - 1)
    def _():
        copies = stores(order_ref, grads, (g0, g1, g2, g3), out_sems)
        for copy in copies:
            copy.start()
        for copy in copies:
            copy.wait()


def fall(order, top, slope, second, *mlp):
    count = second.shape[0]
    shape = jax.ShapeDtypeStruct
    whole = pl.BlockSpec((count, D), lambda t: (0, 0))
    columns = pl.BlockSpec((count, TILE), lambda t: (0, t))
    grad = shape((BLOCKS // 4, D // BLOCKS, FF), BF)
    return pl.pallas_call(
        fall_kernel,
        grid=(FF // TILE,),
        out_shape=[shape((count, FF), BF), shape((1, FF), F32)] + [grad] * 4,
        in_specs=[SMEM, whole, columns, whole] + [ANY] * 4,
        out_specs=[columns, pl.BlockSpec((1, TILE), lambda t: (0, t))] + [ANY] * 4,
        scratch_shapes=[
            pltpu.VMEM((FF, D), BF),
            pltpu.VMEM((D, count), BF),
            pltpu.VMEM((D, FF), BF),
            pltpu.SemaphoreType.DMA((BLOCKS,)),
            pltpu.SemaphoreType.DMA((BLOCKS,)),
        ],
        compiler_params=params(48),
        name="fall",
    )(order, top, slope, second, *mlp)


def back_kernel(
    order_ref, vec_ref, ghidden_ref, middle_ref, top_ref, w0, w1, w2, w3,
    gmiddle_ref, sums_ref,
    held, gsecond, sems,
):
    copies = fetches(order_ref, (w0, w1, w2, w3), held, sems)
    for copy in copies:
        copy.start()
    count = middle_ref.shape[0]
    sums_ref[...] = jnp.zeros_like(sums_ref)
    for copy in copies:
        copy.wait()

    @pl.loop(0, D // WIDE)
    def _(i):
        gsecond[:, span(i, WIDE)] = dot_nt(ghidden_ref[...], held[span(i, WIDE), :])

    @pl.loop(0, count // CHUNK)
    def _(i):
        rows = span(i, CHUNK)
        normed, inverse = norm_parts(middle_ref[rows, :])
        grad = gsecond[rows, :]
        sums_ref[0:1, :] += jnp.sum(grad * normed, axis=0, keepdims=True)
        sums_ref[1:2, :] += jnp.sum(grad, axis=0, keepdims=True)
        top = top_ref[rows, :].astype(F32)
        sums_ref[3:4, :] += jnp.sum(top, axis=0, keepdims=True)
        gmiddle = top + norm_back(grad * vec_ref[1:2, :], normed, inverse)
        gmiddle_ref[rows, :] = gmiddle
        low = gmiddle.astype(BF)
        sums_ref[2:3, :] += jnp.sum(low.astype(F32), axis=0, keepdims=True)


def back(order, vec, ghidden, middle, top, *win):
    count = middle.shape[0]
    shape = jax.ShapeDtypeStruct
    return pl.pallas_call(
        back_kernel,
        out_shape=[shape((count, D), F32), shape((8, D), F32)],
        in_specs=[SMEM] + [VMEM] * 4 + [ANY] * 4,
        out_specs=[VMEM] * 2,
        scratch_shapes=[
            pltpu.VMEM((D, FF), BF),
            pltpu.VMEM((count, D), F32),
            pltpu.SemaphoreType.DMA((BLOCKS,)),
        ],
        compiler_params=params(48),
        name="back",
    )(order, vec, ghidden, middle, top, *win)


def unattend_kernel(
    order_ref, gmiddle_ref, mixed_ref, entry_ref, project_ref,
    probs_ref, w0, w1, w2, w3,
    gproject_ref, sums_ref, g0, g1, g2, g3,
    held, branch, gmixed, turned, grads, sems, out_sems,
):
    rows = w0.shape[1]
    copies = []
    for place in range(BLOCKS):
        source = (w0, w1, w2, w3)[place // w0.shape[0]].at[place % w0.shape[0]]
        copies.append(
            pltpu.make_async_copy(
                source.at[:, pl.ds(3 * D, D)],
                rows_of(held, order_ref[place], rows),
                sems.at[place],
            )
        )
    for copy in copies:
        copy.start()
    count = gmiddle_ref.shape[0]
    branch[...] = gmiddle_ref[...].astype(BF)
    turned[...] = mixed_ref[...].T
    for copy in copies:
        copy.wait()

    @pl.loop(0, D // TILE)
    def _(i):
        columns = span(i, TILE)
        grads[:, span(3 * D // TILE + i, TILE)] = dot(turned[...], branch[:, columns]).astype(BF)
        gmixed[:, columns] = dot_nt(branch[...], held[columns, :]).astype(BF)

    turned[...] = entry_ref[...].T
    groups = D // WIDE

    @pl.loop(0, (count // SEQ) * groups)
    def _(i):
        row, group = i // groups, lax.rem(i, groups)
        rows = span(row, SEQ)
        scale = HEAD_DIM**-0.5
        queries = stacked(project_ref[rows, span(group, WIDE)] * BF(scale))
        keys = project_ref[rows, span(groups + group, WIDE)]
        values = project_ref[rows, span(2 * groups + group, WIDE)]
        gmix = stacked(gmixed[rows, span(group, WIDE)])
        low = probs_ref[i]
        gprobs = dot_nt(gmix, values)
        gvalues = dot_tn(low, gmix)
        weight = low.astype(F32)
        inner = jnp.sum(weight * gprobs, axis=-1, keepdims=True)
        gscores = (weight * (gprobs - inner)).astype(BF)
        gqueries = unstacked(dot(gscores, keys)) * scale
        gkeys = dot_tn(gscores, queries)
        gproject_ref[rows, span(group, WIDE)] = gqueries.astype(BF)
        gproject_ref[rows, span(groups + group, WIDE)] = gkeys.astype(BF)
        gproject_ref[rows, span(2 * groups + group, WIDE)] = gvalues.astype(BF)

    @pl.loop(0, 3 * D // TILE)
    def _(i):
        gpart = gproject_ref[:, span(i, TILE)]
        grads[:, span(i, TILE)] = dot(turned[...], gpart).astype(BF)
        third = i // (D // TILE)
        column = span(lax.rem(i, D // TILE), TILE)
        sums_ref[pl.ds(third, 1), column] = jnp.sum(gpart.astype(F32), axis=0, keepdims=True)

    copies = stores(order_ref, grads, (g0, g1, g2, g3), out_sems)
    for copy in copies:
        copy.start()
    for copy in copies:
        copy.wait()


def unattend(order, gmiddle, mixed, entry, project, probs, *first):
    count = gmiddle.shape[0]
    shape = jax.ShapeDtypeStruct
    grad = shape((BLOCKS // 4, D // BLOCKS, 4 * D), BF)
    return pl.pallas_call(
        unattend_kernel,
        out_shape=[
            shape((count, 3 * D), BF), shape((8, D), F32), grad, grad, grad, grad,
        ],
        in_specs=[SMEM] + [VMEM] * 5 + [ANY] * 4,
        out_specs=[VMEM] * 2 + [ANY] * 4,
        scratch_shapes=[
            pltpu.VMEM((D, D), BF),
            pltpu.VMEM((count, D), BF),
            pltpu.VMEM((count, D), BF),
            pltpu.VMEM((D, count), BF),
            pltpu.VMEM((D, 4 * D), BF),
            pltpu.SemaphoreType.DMA((BLOCKS,)),
            pltpu.SemaphoreType.DMA((BLOCKS,)),
        ],
        compiler_params=params(56),
        name="unattend",
    )(order, gmiddle, mixed, entry, project, probs, *first)


def enter_kernel(
    order_ref, vec_ref, x_ref, gmiddle_ref, gproject_ref, w0, w1, w2, w3,
    ginputs_ref, sums_ref,
    held, gentry, sems,
):
    copies = fetches(order_ref, (w0, w1, w2, w3), held, sems, 3 * D)
    for copy in copies:
        copy.start()
    count = x_ref.shape[0]
    sums_ref[...] = jnp.zeros_like(sums_ref)
    for copy in copies:
        copy.wait()

    @pl.loop(0, D // TILE)
    def _(i):
        gentry[:, span(i, TILE)] = dot_nt(gproject_ref[...], held[span(i, TILE), :])

    @pl.loop(0, count // CHUNK)
    def _(i):
        rows = span(i, CHUNK)
        normed, inverse = norm_parts(x_ref[rows, :].astype(F32))
        grad = gentry[rows, :]
        sums_ref[0:1, :] += jnp.sum(grad * normed, axis=0, keepdims=True)
        sums_ref[1:2, :] += jnp.sum(grad, axis=0, keepdims=True)
        back = norm_back(grad * vec_ref[0:1, :], normed, inverse)
        ginputs_ref[rows, :] = gmiddle_ref[rows, :] + back


def enter(order, vec, x, gmiddle, gproject, *first):
    count = x.shape[0]
    shape = jax.ShapeDtypeStruct
    return pl.pallas_call(
        enter_kernel,
        out_shape=[shape((count, D), F32), shape((8, D), F32)],
        in_specs=[SMEM] + [VMEM] * 4 + [ANY] * 4,
        out_specs=[VMEM] * 2,
        scratch_shapes=[
            pltpu.VMEM((D, 3 * D), BF),
            pltpu.VMEM((count, D), F32),
            pltpu.SemaphoreType.DMA((BLOCKS,)),
        ],
        compiler_params=params(48),
        name="enter",
    )(order, vec, x, gmiddle, gproject, *first)


def finish_kernel(
    order_ref, vec_ref, middle_ref, active_ref, w0, w1, w2, w3, out_ref, held, sems
):
    copies = fetches(order_ref, (w0, w1, w2, w3), held, sems)
    for copy in copies:
        copy.start()
    for copy in copies:
        copy.wait()

    @pl.loop(0, D // WIDE)
    def _(i):
        columns = span(i, WIDE)
        result = dot(active_ref[...], held[:, columns]) + vec_ref[7:8, columns]
        out_ref[:, columns] = (middle_ref[:, columns] + result).astype(BF)


def finish(order, vec, middle, active, *mlp):
    count = middle.shape[0]
    return pl.pallas_call(
        finish_kernel,
        out_shape=jax.ShapeDtypeStruct((count, D), BF),
        in_specs=[SMEM] + [VMEM] * 3 + [ANY] * 4,
        out_specs=VMEM,
        scratch_shapes=[pltpu.VMEM((FF, D), BF), pltpu.SemaphoreType.DMA((BLOCKS,))],
        compiler_params=params(48),
        name="finish",
    )(order, vec, middle, active, *mlp)


def per_device(plan, inputs, image_ids, cotangent, gains, biases, w_qkv, w_out, w_in, w_mlp):
    me = lax.axis_index(AXES)
    order = plan.positions(me)
    gain_dev, bias_dev = gains.shape[1], biases.shape[1]
    rows = D // plan.devices
    blocks, length = image_ids.shape
    count = blocks * length
    x = inputs.reshape(count, D)
    numbers = order if plan.devices == BLOCKS else jnp.arange(BLOCKS, dtype=jnp.int32)
    spot = jnp.sum(
        jnp.where(numbers[:, None] == jnp.arange(BLOCKS)[None, :], jnp.arange(BLOCKS)[:, None], 0),
        axis=0,
    ).astype(jnp.int32)
    line = Line()

    first = Gather(
        plan, line, jnp.concatenate([w_qkv.reshape(rows, 3 * D), w_out.reshape(rows, D)], 1)
    )
    first.start(0)
    small = Gather(plan, line, jnp.concatenate([gains, biases], 1))
    small.start(0)
    win = Gather(plan, line, w_in.reshape(rows, FF))
    mlp = Gather(plan, line, w_mlp.reshape(FF // plan.devices, D))
    top = jnp.where(image_ids.reshape(count, 1) >= 0, cotangent.reshape(count, D), BF(0))
    first.take()
    first.start(1)
    win.start(0)
    small.take()
    small.start(1)
    first.take()
    first.start(2)
    win.take()
    win.start(1)
    mlp.start(0)
    small.take()
    small.start(2)
    first.take()
    first.start(3)
    first.swap_first()
    win.take()
    mlp.take()
    mlp.start(1)
    small.take()
    small.start(3)
    small.swap_first()
    small.arrive()
    small.swap_second()
    first.arrive()
    win.start(2)
    first.swap_second()
    mlp.take()
    placed = jnp.concatenate(small.parts(), 0)[:, 0]

    def unpack(placed):
        spread = lax.dot_general(
            one_hot(order), placed, (((0,), (0,)), ((), ())), preferred_element_type=F32
        )
        return jnp.concatenate(
            [spread[:, :gain_dev].reshape(-1), spread[:, gain_dev:].reshape(-1)]
        ).reshape(-1, D)

    vec = line.run(unpack, placed)
    bias_in = vec[8:12].reshape(1, FF)
    vec = vec[:8]
    first_parts = to_blocks(order, first.parts())
    win.take()
    win.start(3)
    win.swap_first()
    entry, project, probs, mixed, middle, second = line.run(
        attend, numbers, vec, x, image_ids, *first_parts
    )
    win.arrive()
    mlp.start(2)
    win.swap_second()
    win_parts = to_blocks(order, win.parts())
    mlp.take()
    mlp.start(3)
    mlp.swap_first()
    active, slope, *grads = line.run(rise, numbers, spot, bias_in, second, top, *win_parts)
    sum_mlp = Scatter(plan, line, from_blocks(order, grads))
    mlp.arrive()
    mlp.swap_second()
    sum_mlp.start(3)
    mlp_parts = to_blocks(order, mlp.parts())
    ghidden, grad_bias_in, *grads = line.run(fall, numbers, top, slope, second, *mlp_parts)
    sum_in = Scatter(plan, line, from_blocks(order, grads))
    gmiddle, sums = line.run(back, numbers, vec, ghidden, middle, top, *win_parts)
    sum_mlp.start(2)
    sum_in.start(3)
    gproject, sums_qkv, *grads = line.run(
        unattend, numbers, gmiddle, mixed, entry, project, probs, *first_parts
    )
    sum_first = Scatter(plan, line, from_blocks(order, grads))
    sum_mlp.start(1)
    sum_in.start(2)
    sum_first.start(3)
    grad_inputs, sums_one = line.run(enter, numbers, vec, x, gmiddle, gproject, *first_parts)
    flat_gains = jnp.concatenate([sums_one[0], sums[0]]).reshape(-1, gain_dev)
    flat_biases = jnp.concatenate(
        [sums_one[1], sums_qkv[0], sums_qkv[2], sums[2], sums[1], sums[3], grad_bias_in[0]]
    ).reshape(-1, bias_dev)
    flat_small = jnp.concatenate([flat_gains, flat_biases], 1).astype(BF)
    moved = jnp.dot(one_hot(order), flat_small, preferred_element_type=F32).astype(BF)
    moved = moved.reshape(4, plan.devices // 4, 1, -1)
    sum_small = Scatter(plan, line, [moved[i] for i in range(4)])
    sum_mlp.start(0)
    sum_in.start(1)
    sum_small.start(3)
    sum_small.start(2)
    sum_first.start(2)
    output = line.run(finish, numbers, vec, middle, active, *mlp_parts)
    sum_small.start(1)
    grad_mlp = sum_mlp.result()
    sum_in.start(0)
    sum_small.start(0)
    sum_first.start(1)
    grad_small = sum_small.result()
    grad_in = sum_in.result()
    sum_first.start(0)
    grad_first = sum_first.result()
    return (
        output.reshape(blocks, length, D),
        grad_inputs.reshape(blocks, length, D),
        grad_small[:, :gain_dev],
        grad_small[:, gain_dev:],
        grad_first[:, : 3 * D].reshape(1, -1),
        grad_first[:, 3 * D :].reshape(1, -1),
        grad_in.reshape(1, -1),
        grad_mlp.reshape(1, -1),
    )


def solution(mesh):
    plan = Plan(mesh)
    whole = P(AXES, None, None)
    flat = P(AXES, None)

    def body(*arrays):
        return per_device(plan, *arrays)

    return jax.shard_map(
        body,
        mesh=mesh,
        in_specs=(whole, flat, whole, flat, flat, flat, flat, flat, flat),
        out_specs=(whole, whole, flat, flat, flat, flat, flat, flat),
        check_vma=False,
    )
```

```python
import jax
import jax.numpy as jnp
from jax import lax
from jax.experimental import pallas as pl
from jax.experimental.pallas import tpu as pltpu
from jax.sharding import PartitionSpec as P

D = 1024
FF = 4096
HEADS = 16
HEAD_DIM = 64
SEQ = 256
AXES = ("dp", "fsdp")
BLOCKS = 32
GROUP = 4
WIDE = GROUP * HEAD_DIM
TILE = 512
CHUNK = 128
PIECE = FF // BLOCKS
BF = jnp.bfloat16
F32 = jnp.float32

eps = 1e-06
ANY = pl.BlockSpec(memory_space=pl.ANY)
VMEM = pl.BlockSpec(memory_space=pltpu.VMEM)
SMEM = pl.BlockSpec(memory_space=pltpu.SMEM)


class Plan:
    def __init__(self, mesh):
        outer, inner = mesh.shape["dp"], mesh.shape["fsdp"]
        ys = outer // 2
        xs = min(ys, inner)
        zs = inner // xs
        self.devices = outer * inner
        self.half = self.devices // 2

        def bits(size, unit):
            found = []
            while size > 1:
                size //= 2
                found.append(size * unit)
            return found

        xbits = bits(xs, 1)
        zbits = bits(zs, xs)
        self.core = inner
        ybits = bits(ys, 2 * inner)
        self.orders = (zbits + xbits + ybits, zbits + ybits + xbits)
        self.legs = [list(range(1)), list(range(1, len(zbits)))]
        for _ in range(2):
            start = self.legs[-1][-1] + 1
            self.legs.append(list(range(start, start + len(xbits))))

    def pairs(self, stage):
        return [
            (i, i ^ self.orders[1 if i & self.core else 0][stage]) for i in range(self.devices)
        ]

    def core_pairs(self):
        return [(i, i ^ self.core) for i in range(self.devices)]

    def masks(self, which):
        found = [0]
        for bit in self.orders[which]:
            found = found + [mask ^ bit for mask in found]
        return found

    def positions(self, me):
        tables = jnp.array(
            [
                self.masks(0) + [mask ^ self.core for mask in self.masks(1)],
                self.masks(1) + [mask ^ self.core for mask in self.masks(0)],
            ],
            jnp.int32,
        )
        mine = jnp.where((me & self.core) > 0, tables[1], tables[0])
        return mine ^ me


class Line:
    def __init__(self):
        self.last = []

    def tie(self, *arrays):
        if not self.last:
            return arrays
        tied = lax.optimization_barrier((arrays, tuple(self.last)))
        return tied[0]

    def run(self, step, *arrays):
        result = step(*self.tie(*arrays))
        self.last = [result[0] if isinstance(result, (list, tuple)) else result]
        return result

    def send(self, array, pairs, name="swap"):
        with jax.named_scope(name):
            return lax.ppermute(self.tie(array)[0], AXES, pairs)

    def wait(self, *arrays):
        self.last.extend(arrays)


class Gather:
    def __init__(self, plan, line, name, block):
        self.plan, self.line, self.name = plan, line, name
        self.held = block[None]
        self.coming = None

    def take(self):
        self.line.wait(self.coming)
        self.held = self.line.run(
            lambda held, coming: jnp.concatenate([held, coming], 0), self.held, self.coming
        )

    def start(self, leg):
        for stage in self.plan.legs[leg]:
            if stage != self.plan.legs[leg][0]:
                self.take()
            self.coming = self.line.send(
                self.held, self.plan.pairs(stage), f"gather_{self.name}_{stage}"
            )

    def swap_first(self):
        self.first = self.line.send(
            self.held, self.plan.core_pairs(), f"gather_{self.name}_swap_first"
        )

    def arrive(self):
        self.line.wait(self.coming)

    def swap_second(self):
        self.second = self.line.send(
            self.coming, self.plan.core_pairs(), f"gather_{self.name}_swap_second"
        )

    def parts(self):
        self.line.wait(self.first, self.second)
        return [self.held, self.coming, self.first, self.second]


def total(parts):
    if len(parts) == 2:
        return parts[0] + parts[1]
    result = parts[0].astype(F32)
    for part in parts[1:]:
        result = result + part.astype(F32)
    return result


class Scatter:
    def __init__(self, plan, line, name, parts):
        self.plan, self.line, self.name = plan, line, name
        keep_low, keep_high, send_low, send_high = parts
        self.high = [keep_high, line.send(send_high, plan.core_pairs(), f"sum_{name}_swap_high")]
        self.low = [keep_low, line.send(send_low, plan.core_pairs(), f"sum_{name}_swap_low")]
        self.side = []
        self.count = keep_low.shape[0]
        self.width = keep_low.shape[-1]

    def join(self, parts):
        half = self.plan.half
        self.side = [
            parts[:half],
            self.line.send(parts[half:], self.plan.core_pairs(), f"sum_{self.name}_swap_side"),
        ]

    def sum(self, low, high, parts):
        wide = total([part[low:high, :, : self.width] for part in parts])
        if not self.side:
            return wide
        offset = low if self.high is None else low + self.count
        narrow = [part[low:high, :, self.width :] for part in parts[2:]]
        narrow += [part[offset : offset + high - low] for part in self.side]
        return jnp.concatenate([wide, total(narrow)], -1)

    def start(self, leg):
        for stage in reversed(self.plan.legs[leg]):
            if self.high is not None:
                parts, low = self.high, 0
            else:
                self.count //= 2
                parts, low = self.low, self.count
            self.line.wait(parts[-1], *self.side)
            outgoing = self.line.run(
                lambda *parts: self.sum(low, low + self.count, parts).astype(BF), *parts
            )
            self.high = None
            self.low.append(
                self.line.send(outgoing, self.plan.pairs(stage), f"sum_{self.name}_{stage}")
            )

    def arrive(self):
        self.line.wait(self.low[-1])

    def result(self):
        self.arrive()
        return self.line.run(lambda *parts: self.sum(0, 1, parts)[0].astype(F32), *self.low)


def one_hot(order):
    return (order[:, None] == jnp.arange(order.shape[0])[None, :]).astype(BF)


def to_blocks(order, parts):
    if order.shape[0] == BLOCKS:
        return parts
    width = parts[0].shape[-1]
    joined = jnp.concatenate(parts, 0).reshape(order.shape[0], -1)
    spread = lax.dot_general(
        one_hot(order), joined, (((0,), (0,)), ((), ())), preferred_element_type=BF
    ).reshape(4, BLOCKS // 4, -1, width)
    return [spread[i] for i in range(4)]


def from_blocks(order, parts):
    count = order.shape[0]
    if count == BLOCKS:
        return parts
    width = parts[0].shape[-1]
    joined = jnp.concatenate(parts, 0).reshape(count, -1)
    moved = jnp.dot(one_hot(order), joined, preferred_element_type=BF)
    moved = moved.reshape(4, count // 4, -1, width)
    return [moved[i] for i in range(4)]


def params(limit):
    return pltpu.CompilerParams(vmem_limit_bytes=limit << 20)


def rows_of(ref, number, rows):
    return ref.at[pl.ds(pl.multiple_of(number * rows, rows), rows), :]


def fetches(order_ref, part_refs, held_ref, sems, start=0, width=None):
    each, rows, _ = part_refs[0].shape
    width = held_ref.shape[1] if width is None else width
    copies = []
    for place in range(BLOCKS):
        source = part_refs[place // each].at[place % each, :, pl.ds(start, width)]
        number = order_ref[place]
        copies.append(
            pltpu.make_async_copy(source, rows_of(held_ref, number, rows), sems.at[number])
        )
    return copies


def norm_parts(values):
    centre = values - jnp.mean(values, axis=-1, keepdims=True)
    inverse = lax.rsqrt(jnp.mean(centre * centre, axis=-1, keepdims=True) + eps)
    return centre * inverse, inverse


def norm_back(grad_norm, normed, inverse):
    return inverse * (
        grad_norm
        - jnp.mean(grad_norm, axis=-1, keepdims=True)
        - normed * jnp.mean(grad_norm * normed, axis=-1, keepdims=True)
    )


def span(index, size):
    if isinstance(index, int):
        return pl.ds(index * size, size)
    return pl.ds(pl.multiple_of(index * size, size), size)


def each(count):
    def run(body):
        for index in range(count):
            body(index)

    return run


def dot(a, b):
    return jnp.dot(a, b, preferred_element_type=F32)


def dot_nt(a, b):
    return lax.dot_general(a, b, (((1,), (1,)), ((), ())), preferred_element_type=F32)


def dot_tn(a, b):
    return lax.dot_general(a, b, (((0,), (0,)), ((), ())), preferred_element_type=F32)


def stacked(values):
    head = lax.broadcasted_iota(jnp.int32, values.shape, 1) // HEAD_DIM
    zero = jnp.zeros_like(values)
    return jnp.concatenate([jnp.where(head == h, values, zero) for h in range(GROUP)], 0)


def unstacked(values):
    rows = values.shape[0] // GROUP
    head = lax.broadcasted_iota(jnp.int32, (rows, values.shape[1]), 1) // HEAD_DIM
    result = values[:rows]
    for h in range(1, GROUP):
        result = jnp.where(head == h, values[h * rows : (h + 1) * rows], result)
    return result


def project_kernel(
    order_ref, vec_ref, x_ref, w0, w1, w2, w3, entry_ref, project_ref, held, sems
):
    copies = fetches(order_ref, (w0, w1, w2, w3), held, sems)
    for copy in copies:
        copy.start()

    @each(x_ref.shape[0] // CHUNK)
    def _(i):
        normed, _ = norm_parts(x_ref[span(i, CHUNK), :].astype(F32))
        entry_ref[span(i, CHUNK), :] = (normed * vec_ref[0:1, :] + vec_ref[2:3, :]).astype(BF)

    for copy in copies:
        copy.wait()

    @each(3 * D // TILE)
    def _(i):
        third = i // (D // TILE)
        column = span(i % (D // TILE), TILE)
        part = dot(entry_ref[...], held[:, span(i, TILE)])
        if third != 1:
            part = part + vec_ref[pl.ds(3 if third == 0 else 4, 1), column]
        project_ref[:, span(i, TILE)] = part.astype(BF)


def project_all(order, vec, x, *first):
    count = x.shape[0]
    shape = jax.ShapeDtypeStruct
    return pl.pallas_call(
        project_kernel,
        out_shape=[shape((count, D), BF), shape((count, 3 * D), BF)],
        in_specs=[SMEM] + [VMEM] * 2 + [ANY] * 4,
        out_specs=[VMEM] * 2,
        scratch_shapes=[pltpu.VMEM((D, 3 * D), BF), pltpu.SemaphoreType.DMA((BLOCKS,))],
        compiler_params=params(32),
        name="project",
    )(order, vec, x, *first)


def attend_kernel(project_ref, idr_ref, idc_ref, probs_ref, mixed_ref, probs, out_sems):
    groups = D // WIDE
    copies = []

    @each((mixed_ref.shape[0] // SEQ) * groups)
    def _(i):
        row, group = i // groups, i % groups
        rows = span(row, SEQ)
        queries = project_ref[rows, span(group, WIDE)] * BF(HEAD_DIM**-0.5)
        keys = project_ref[rows, span(groups + group, WIDE)]
        values = project_ref[rows, span(2 * groups + group, WIDE)]
        scores = dot_nt(stacked(queries), keys)
        same = idc_ref[rows, :] == idr_ref[pl.ds(row, 1), :]
        scores = jnp.where(same[None], scores.reshape(GROUP, SEQ, SEQ), -1e9)
        expo = jnp.exp(scores - jnp.max(scores, axis=-1, keepdims=True))
        low = (expo / jnp.sum(expo, axis=-1, keepdims=True)).astype(BF)
        low = low.reshape(GROUP * SEQ, SEQ)
        probs[i] = low
        copy = pltpu.make_async_copy(probs.at[i], probs_ref.at[i], out_sems.at[i])
        copy.start()
        copies.append(copy)
        mixed_ref[rows, span(group, WIDE)] = unstacked(dot(low, values)).astype(BF)

    for copy in copies:
        copy.wait()


def attend(project, ids):
    count = project.shape[0]
    steps = (count // SEQ) * (D // WIDE)
    shape = jax.ShapeDtypeStruct
    return pl.pallas_call(
        attend_kernel,
        out_shape=[shape((steps, GROUP * SEQ, SEQ), BF), shape((count, D), BF)],
        in_specs=[VMEM] * 3,
        out_specs=[ANY, VMEM],
        scratch_shapes=[
            pltpu.VMEM((steps, GROUP * SEQ, SEQ), BF),
            pltpu.SemaphoreType.DMA((steps,)),
        ],
        compiler_params=params(32),
        name="attend",
    )(project, ids, ids.reshape(count, 1))


def piece(number):
    return pl.ds(pl.multiple_of(number * PIECE, PIECE), PIECE)


def settle_kernel(
    order_ref, vec_ref, x_ref, mixed_ref, w0, w1, w2, w3, middle_ref, second_ref, held, sems
):
    copies = fetches(order_ref, (w0, w1, w2, w3), held, sems, FF)
    for copy in copies:
        copy.start()
    for copy in copies:
        copy.wait()

    @each(D // TILE)
    def _(i):
        columns = span(i, TILE)
        branch = dot(mixed_ref[...], held[:, columns]) + vec_ref[5:6, columns]
        middle_ref[:, columns] = x_ref[:, columns].astype(F32) + branch

    @pl.loop(0, x_ref.shape[0] // CHUNK)
    def _(i):
        normed, _ = norm_parts(middle_ref[span(i, CHUNK), :])
        second_ref[span(i, CHUNK), :] = (normed * vec_ref[1:2, :] + vec_ref[6:7, :]).astype(BF)


def settle(order, vec, x, mixed, *win):
    count = x.shape[0]
    shape = jax.ShapeDtypeStruct
    return pl.pallas_call(
        settle_kernel,
        out_shape=[shape((count, D), F32), shape((count, D), BF)],
        in_specs=[SMEM] + [VMEM] * 3 + [ANY] * 4,
        out_specs=[VMEM] * 2,
        scratch_shapes=[pltpu.VMEM((D, D), BF), pltpu.SemaphoreType.DMA((BLOCKS,))],
        compiler_params=params(32),
        name="settle",
    )(order, vec, x, mixed, *win)


def rise_kernel(
    order_ref, bias_ref, second_ref, top_ref, w0, w1, w2, w3,
    active_ref, slope_ref, g0, g1, g2, g3,
    held, active, slope, grads, sems, tile_sems,
):
    copies = fetches(order_ref, (w0, w1, w2, w3), held, sems)
    for copy in copies:
        copy.start()
    for copy in copies:
        copy.wait()
    outs = []
    places = TILE // PIECE

    @each(FF // TILE)
    def _(step):
        columns = span(step, TILE)
        numbers = [order_ref[step * places + j] for j in range(places)]
        weight = jnp.concatenate([held[:, piece(number)] for number in numbers], 1)
        bias = jnp.concatenate([bias_ref[:, piece(number)] for number in numbers], 1)
        hidden = dot(second_ref[...], weight) + bias
        cdf = 0.5 + 0.5 * lax.erf(hidden * (0.5**0.5))
        grow = cdf + hidden * jnp.exp(-0.5 * hidden * hidden) * 0.3989422804014327
        low = (hidden * cdf).astype(BF)
        active[:, columns] = low
        slope[:, columns] = grow.astype(BF)
        grad = dot_tn(low, top_ref[...]).astype(BF)
        block = pl.ds(step * places, places)
        grads[block] = grad.reshape(places, PIECE, D)
        apiece = g0.shape[0]
        target = (g0, g1, g2, g3)[step * places // apiece]
        target = target.at[pl.ds(step * places % apiece, places)]
        for number, (source, target) in enumerate(
            (
                (active.at[:, columns], active_ref.at[:, columns]),
                (slope.at[:, columns], slope_ref.at[:, columns]),
                (grads.at[block], target),
            )
        ):
            copy = pltpu.make_async_copy(source, target, tile_sems.at[step, number])
            copy.start()
            outs.append(copy)

    for copy in outs:
        copy.wait()


def rise(order, bias, second, top, *win):
    count = second.shape[0]
    shape = jax.ShapeDtypeStruct
    grad = shape((BLOCKS // 4, PIECE, D), BF)
    return pl.pallas_call(
        rise_kernel,
        out_shape=[shape((count, FF), BF)] * 2 + [grad] * 4,
        in_specs=[SMEM] + [VMEM] * 3 + [ANY] * 4,
        out_specs=[ANY] * 6,
        scratch_shapes=[
            pltpu.VMEM((D, FF), BF),
            pltpu.VMEM((count, FF), BF),
            pltpu.VMEM((count, FF), BF),
            pltpu.VMEM((BLOCKS, PIECE, D), BF),
            pltpu.SemaphoreType.DMA((BLOCKS,)),
            pltpu.SemaphoreType.DMA((FF // TILE, 3)),
        ],
        compiler_params=params(48),
        name="rise",
    )(order, bias, second, top, *win)


def part_fetches(part_refs, held_ref, sems):
    apiece = part_refs[0].shape[0]
    return [
        pltpu.make_async_copy(part, held_ref.at[pl.ds(i * apiece, apiece)], sems.at[i])
        for i, part in enumerate(part_refs)
    ]


def block_rows(order_ref, ref, part, apiece, rows):
    return jnp.concatenate(
        [ref[span(order_ref[part * apiece + j], rows), :] for j in range(apiece)], 0
    )


def fall_kernel(
    order_ref, vec_ref, top_ref, slope_ref, second_ref, middle_ref,
    m0, m1, m2, m3, w0, w1, w2, w3,
    gmiddle_ref, sums_ref, bias_ref, g0, g1, g2, g3,
    mheld, held, slope, ghidden, turned, middle, gsecond, grads,
    msems, sems, tile_sems, out_sems,
):
    copies = part_fetches((m0, m1, m2, m3), mheld, msems)
    apiece, rows, _ = g0.shape
    places = TILE // PIECE
    slopes = [
        pltpu.make_async_copy(
            slope_ref.at[:, span(i, FF // 4)], slope.at[:, span(i, FF // 4)], tile_sems.at[i]
        )
        for i in range(4)
    ]
    for i in range(4):
        copies[i].start()
        slopes[i].start()
    later = fetches(order_ref, (w0, w1, w2, w3), held, sems)
    later.append(pltpu.make_async_copy(middle_ref, middle, tile_sems.at[4]))
    for copy in later:
        copy.start()
    turned[...] = second_ref[...].T
    sums_ref[...] = jnp.zeros_like(sums_ref)

    @each(FF // TILE)
    def _(step):
        part = step * places // apiece
        if step * places % apiece == 0:
            copies[part].wait()
            slopes[part].wait()
        weight = mheld[pl.ds(step * places, places)].reshape(TILE, D)
        grad_active = dot_nt(top_ref[...], weight)
        grad = grad_active * slope[:, span(step, TILE)].astype(F32)
        low = grad.astype(BF)
        sums = jnp.sum(low.astype(F32), axis=0, keepdims=True)
        for j in range(places):
            number = order_ref[step * places + j]
            ghidden[:, piece(number)] = low[:, j * PIECE : (j + 1) * PIECE]
            bias_ref[:, piece(number)] = sums[:, j * PIECE : (j + 1) * PIECE]

    for copy in later:
        copy.wait()
    for i in range(D // WIDE):
        gsecond[:, span(i, WIDE)] = dot_nt(ghidden[...], held[span(i, WIDE), :])
    outs = []
    chunk = middle_ref.shape[0] // 4
    for part in (3, 2, 1, 0):
        left = block_rows(order_ref, turned, part, apiece, rows)
        for i in range(FF // TILE):
            grad = dot(left, ghidden[:, span(i, TILE)]).astype(BF)
            grads[part, :, :, span(i, TILE)] = grad.reshape(apiece, rows, TILE)
        copy = pltpu.make_async_copy(grads.at[part], (g0, g1, g2, g3)[part], out_sems.at[part])
        copy.start()
        outs.append(copy)
        places_of = span(part, chunk)
        normed, inverse = norm_parts(middle[places_of, :])
        grad = gsecond[places_of, :]
        top = top_ref[places_of, :].astype(F32)
        gmiddle = top + norm_back(grad * vec_ref[1:2, :], normed, inverse)
        gmiddle_ref[places_of, :] = gmiddle
        low = gmiddle.astype(BF).astype(F32)
        for row, value in enumerate((grad * normed, grad, low, top)):
            sums_ref[row : row + 1, :] += jnp.sum(value, axis=0, keepdims=True)
    for copy in outs:
        copy.wait()


def fall(order, vec, top, slope, second, middle, mlp, win):
    count = second.shape[0]
    shape = jax.ShapeDtypeStruct
    grad = shape((BLOCKS // 4, D // BLOCKS, FF), BF)
    return pl.pallas_call(
        fall_kernel,
        out_shape=[shape((count, D), F32), shape((8, D), F32), shape((1, FF), F32)] + [grad] * 4,
        in_specs=[SMEM, VMEM, VMEM, ANY, VMEM, ANY] + [ANY] * 8,
        out_specs=[VMEM] * 3 + [ANY] * 4,
        scratch_shapes=[
            pltpu.VMEM((BLOCKS, PIECE, D), BF),
            pltpu.VMEM((D, FF), BF),
            pltpu.VMEM((count, FF), BF),
            pltpu.VMEM((count, FF), BF),
            pltpu.VMEM((D, count), BF),
            pltpu.VMEM((count, D), F32),
            pltpu.VMEM((count, D), F32),
            pltpu.VMEM((4, *grad.shape), BF),
            pltpu.SemaphoreType.DMA((4,)),
            pltpu.SemaphoreType.DMA((BLOCKS,)),
            pltpu.SemaphoreType.DMA((5,)),
            pltpu.SemaphoreType.DMA((4,)),
        ],
        compiler_params=params(56),
        name="fall",
    )(order, vec, top, slope, second, middle, *mlp, *win)


def unattend_kernel(
    order_ref, vec_ref, x_ref, gmiddle_ref, project_ref, probs_ref, entry_ref, mixed_ref,
    w0, w1, w2, w3, f0, f1, f2, f3,
    ginputs_ref, sums_ref, g0, g1, g2, g3,
    oheld, held, project, probs, both, turned, branch, gmixed, gproject, gentry, grads,
    osems, sems, in_sems, probs_sems, out_sems,
):
    count = gmiddle_ref.shape[0]
    groups = D // WIDE
    ocopies = fetches(order_ref, (w0, w1, w2, w3), oheld, osems, FF)
    load = [
        pltpu.make_async_copy(project_ref, project, in_sems.at[0]),
        pltpu.make_async_copy(entry_ref, both.at[0], in_sems.at[1]),
        pltpu.make_async_copy(mixed_ref, both.at[1], in_sems.at[2]),
    ]
    pieces = [
        pltpu.make_async_copy(probs_ref.at[i], probs.at[i], probs_sems.at[i])
        for i in range((count // SEQ) * groups)
    ]
    copies = fetches(order_ref, (f0, f1, f2, f3), held, sems)
    for copy in ocopies + load + pieces + copies:
        copy.start()
    branch[...] = gmiddle_ref[...].astype(BF)
    sums_ref[...] = jnp.zeros_like(sums_ref)
    for copy in ocopies:
        copy.wait()

    @each(D // TILE)
    def _(i):
        gmixed[:, span(i, TILE)] = dot_nt(branch[...], oheld[span(i, TILE), :]).astype(BF)

    for copy in load:
        copy.wait()
    for i in range(2):
        turned[i] = both[i].T
    apiece, rows, _ = g0.shape

    @each((count // SEQ) * groups)
    def _(i):
        row, group = i // groups, i % groups
        where = span(row, SEQ)
        scale = HEAD_DIM**-0.5
        pieces[i].wait()
        queries = stacked(project[where, span(group, WIDE)] * BF(scale))
        keys = project[where, span(groups + group, WIDE)]
        values = project[where, span(2 * groups + group, WIDE)]
        gmix = stacked(gmixed[where, span(group, WIDE)])
        low = probs[i]
        gprobs = dot_nt(gmix, values)
        gvalues = dot_tn(low, gmix)
        weight = low.astype(F32)
        inner = jnp.sum(weight * gprobs, axis=-1, keepdims=True)
        gscores = (weight * (gprobs - inner)).astype(BF)
        gqueries = unstacked(dot(gscores, keys)) * scale
        gkeys = dot_tn(gscores, queries)
        for third, grad in enumerate((gqueries, gkeys, gvalues)):
            low = grad.astype(BF)
            gproject[where, span(third * groups + group, WIDE)] = low
            sums_ref[third : third + 1, span(group, WIDE)] += jnp.sum(
                low.astype(F32), axis=0, keepdims=True
            )

    for copy in copies:
        copy.wait()
    for i in range(D // WIDE):
        gentry[:, span(i, WIDE)] = dot_nt(gproject[...], held[span(i, WIDE), :])
    outs = []
    chunk = count // 4
    for part in (3, 2, 1, 0):
        left = block_rows(order_ref, turned.at[0], part, apiece, rows)
        for i in range(3 * D // TILE):
            grad = dot(left, gproject[:, span(i, TILE)]).astype(BF)
            grads[part, :, :, span(i, TILE)] = grad.reshape(apiece, rows, TILE)
        left = block_rows(order_ref, turned.at[1], part, apiece, rows)
        for i in range(D // TILE):
            grad = dot(left, branch[:, span(i, TILE)]).astype(BF)
            grads[part, :, :, span(3 * D // TILE + i, TILE)] = grad.reshape(apiece, rows, TILE)
        copy = pltpu.make_async_copy(grads.at[part], (g0, g1, g2, g3)[part], out_sems.at[part])
        copy.start()
        outs.append(copy)
        where = span(part, chunk)
        normed, inverse = norm_parts(x_ref[where, :].astype(F32))
        grad = gentry[where, :]
        back = norm_back(grad * vec_ref[0:1, :], normed, inverse)
        ginputs_ref[where, :] = gmiddle_ref[where, :] + back
        sums_ref[3:4, :] += jnp.sum(grad * normed, axis=0, keepdims=True)
        sums_ref[4:5, :] += jnp.sum(grad, axis=0, keepdims=True)
    for copy in outs:
        copy.wait()


def unattend(order, vec, x, gmiddle, project, probs, entry, mixed, win, first):
    count = gmiddle.shape[0]
    shape = jax.ShapeDtypeStruct
    grad = shape((BLOCKS // 4, D // BLOCKS, 4 * D), BF)
    return pl.pallas_call(
        unattend_kernel,
        out_shape=[shape((count, D), F32), shape((8, D), F32)] + [grad] * 4,
        in_specs=[SMEM] + [VMEM] * 3 + [ANY] * 12,
        out_specs=[VMEM] * 2 + [ANY] * 4,
        scratch_shapes=[
            pltpu.VMEM((D, D), BF),
            pltpu.VMEM((D, 3 * D), BF),
            pltpu.VMEM((count, 3 * D), BF),
            pltpu.VMEM(probs.shape, BF),
            pltpu.VMEM((2, count, D), BF),
            pltpu.VMEM((2, D, count), BF),
            pltpu.VMEM((count, D), BF),
            pltpu.VMEM((count, D), BF),
            pltpu.VMEM((count, 3 * D), BF),
            pltpu.VMEM((count, D), F32),
            pltpu.VMEM((4, *grad.shape), BF),
            pltpu.SemaphoreType.DMA((BLOCKS,)),
            pltpu.SemaphoreType.DMA((BLOCKS,)),
            pltpu.SemaphoreType.DMA((3,)),
            pltpu.SemaphoreType.DMA((probs.shape[0],)),
            pltpu.SemaphoreType.DMA((4,)),
        ],
        compiler_params=params(56),
        name="unattend",
    )(order, vec, x, gmiddle, project, probs, entry, mixed, *win, *first)


def finish_kernel(
    vec_ref, middle_ref, active_ref, w0, w1, w2, w3,
    out_ref, held, active, sems, tile_sems,
):
    copies = [
        pltpu.make_async_copy(
            active_ref.at[:, span(half, FF // 2)], active.at[half], tile_sems.at[half]
        )
        for half in range(2)
    ]
    fetch = part_fetches((w0, w1, w2, w3), held, sems)
    for copy in fetch + copies:
        copy.start()
    for copy in fetch + copies:
        copy.wait()

    @each(D // WIDE)
    def _(i):
        columns = span(i, WIDE)
        weight = held[:, :, columns].reshape(FF, WIDE)
        result = dot(active[0], weight[: FF // 2])
        result = result + dot(active[1], weight[FF // 2 :]) + vec_ref[7:8, columns]
        out_ref[:, columns] = (middle_ref[:, columns] + result).astype(BF)


def finish(vec, middle, active, *mlp):
    count = middle.shape[0]
    return pl.pallas_call(
        finish_kernel,
        out_shape=jax.ShapeDtypeStruct((count, D), BF),
        in_specs=[VMEM, VMEM, ANY] + [ANY] * 4,
        out_specs=VMEM,
        scratch_shapes=[
            pltpu.VMEM((BLOCKS, PIECE, D), BF),
            pltpu.VMEM((2, count, FF // 2), BF),
            pltpu.SemaphoreType.DMA((4,)),
            pltpu.SemaphoreType.DMA((2,)),
        ],
        compiler_params=params(32),
        name="finish",
    )(vec, middle, active, *mlp)


def per_device(plan, inputs, image_ids, cotangent, gains, biases, w_qkv, w_out, w_in, w_mlp):
    me = lax.axis_index(AXES)
    order = plan.positions(me)
    gain_dev, bias_dev = gains.shape[1], biases.shape[1]
    small_dev = gain_dev + bias_dev
    rows = D // plan.devices
    blocks, length = image_ids.shape
    count = blocks * length
    x = inputs.reshape(count, D)
    numbers = order if plan.devices == BLOCKS else jnp.arange(BLOCKS, dtype=jnp.int32)
    line = Line()
    side = 128

    small = jnp.concatenate([gains, biases], 1)
    small = jnp.pad(small, ((0, 0), (0, rows * side - small_dev))).reshape(rows, side)
    first = Gather(plan, line, "qkv", jnp.concatenate([w_qkv.reshape(rows, 3 * D), small], 1))
    first.start(0)
    win = Gather(
        plan, line, "in", jnp.concatenate([w_in.reshape(rows, FF), w_out.reshape(rows, D)], 1)
    )
    mlp = Gather(plan, line, "mlp", w_mlp.reshape(FF // plan.devices, D))
    top = jnp.where(image_ids.reshape(count, 1) >= 0, cotangent.reshape(count, D), BF(0))
    first.take()
    first.start(1)
    win.start(0)
    first.take()
    win.take()
    first.start(2)
    win.start(1)
    first.take()
    win.take()
    first.start(3)
    first.swap_first()
    mlp.start(0)
    first.arrive()
    mlp.take()
    first.swap_second()
    win.start(2)
    mlp.start(1)
    first_parts = first.parts()

    def unpack(*parts):
        placed = jnp.concatenate([part[:, :, 3 * D :] for part in parts], 0)
        placed = placed.reshape(-1, rows * side)[:, :small_dev]
        spread = lax.dot_general(
            one_hot(order), placed, (((0,), (0,)), ((), ())), preferred_element_type=F32
        )
        return jnp.concatenate(
            [spread[:, :gain_dev].reshape(-1), spread[:, gain_dev:].reshape(-1)]
        ).reshape(-1, D)

    vec = line.run(unpack, *first_parts)
    line.wait(*first_parts)
    bias_in = vec[8:12].reshape(1, FF)
    vec = vec[:8]
    if plan.devices != BLOCKS:
        first_parts = [part[:, :, : 3 * D] for part in first_parts]
    first_parts = to_blocks(order, first_parts)
    entry, project = line.run(project_all, numbers, vec, x, *first_parts)
    win.take()
    mlp.take()
    win.start(3)
    win.swap_first()
    probs, mixed = line.run(attend, project, image_ids)
    win.arrive()
    line.wait(win.first)
    win.swap_second()
    mlp.start(2)
    win_parts = to_blocks(order, win.parts())
    middle, second = line.run(settle, numbers, vec, x, mixed, *win_parts)
    mlp.take()
    mlp.start(3)
    mlp.swap_first()
    active, slope, *grads = line.run(rise, numbers, bias_in, second, top, *win_parts)
    line.wait(mlp.first)
    mlp.arrive()
    sum_mlp = Scatter(plan, line, "mlp", from_blocks(order, grads))
    mlp.swap_second()
    sum_mlp.start(3)
    mlp_parts = to_blocks(order, mlp.parts())
    gmiddle, sums, grad_bias_in, *grads = line.run(
        fall, numbers, vec, top, slope, second, middle, mlp_parts, win_parts
    )
    sum_mlp.arrive()
    sum_in = Scatter(plan, line, "in", from_blocks(order, grads))
    sum_mlp.start(2)
    sum_in.start(3)
    grad_inputs, sums_one, *grads = line.run(
        unattend, numbers, vec, x, gmiddle, project, probs, entry, mixed, win_parts, first_parts
    )
    sum_mlp.arrive()
    sum_in.arrive()
    sum_first = Scatter(plan, line, "first", from_blocks(order, grads))
    sum_in.start(2)
    sum_mlp.start(1)

    def pack(sums_one, sums, grad_bias_in):
        flat_gains = jnp.concatenate([sums_one[3], sums[0]]).reshape(-1, gain_dev)
        flat_biases = jnp.concatenate(
            [sums_one[4], sums_one[0], sums_one[2], sums[2], sums[1], sums[3], grad_bias_in[0]]
        ).reshape(-1, bias_dev)
        flat_small = jnp.concatenate([flat_gains, flat_biases], 1).astype(BF)
        moved = jnp.dot(one_hot(order), flat_small, preferred_element_type=F32).astype(BF)
        moved = jnp.pad(moved, ((0, 0), (0, rows * side - small_dev)))
        return moved.reshape(plan.devices, rows, side)

    sum_first.join(pack(sums_one, sums, grad_bias_in))
    sum_in.arrive()
    sum_first.start(3)
    sum_in.start(1)
    output = line.run(finish, vec, middle, active, *mlp_parts)
    sum_mlp.start(0)
    sum_in.start(0)
    sum_first.start(2)
    grad_mlp = sum_mlp.result()
    grad_in = sum_in.result()
    sum_first.start(1)
    sum_first.start(0)
    grad_first = sum_first.result()
    grad_small = grad_first[:, 4 * D :].reshape(1, -1)[:, :small_dev]
    return (
        output.reshape(blocks, length, D),
        grad_inputs.reshape(blocks, length, D),
        grad_small[:, :gain_dev],
        grad_small[:, gain_dev:],
        grad_first[:, : 3 * D].reshape(1, -1),
        grad_first[:, 3 * D : 4 * D].reshape(1, -1),
        grad_in.reshape(1, -1),
        grad_mlp.reshape(1, -1),
    )


def solution(mesh):
    plan = Plan(mesh)
    whole = P(AXES, None, None)
    flat = P(AXES, None)

    def body(*arrays):
        return per_device(plan, *arrays)

    return jax.shard_map(
        body,
        mesh=mesh,
        in_specs=(whole, flat, whole, flat, flat, flat, flat, flat, flat),
        out_specs=(whole, whole, flat, flat, flat, flat, flat, flat),
        check_vma=False,
    )
```

```python
import jax
import jax.numpy as jnp
from jax import lax
from jax.experimental import pallas as pl
from jax.experimental.pallas import tpu as pltpu
from jax.sharding import PartitionSpec as P

D = 1024
FF = 4096
HEADS = 16
HEAD_DIM = 64
SEQ = 256
AXES = ("dp", "fsdp")
BLOCKS = 32
GROUP = 4
WIDE = GROUP * HEAD_DIM
TILE = 512
CHUNK = 128
PIECE = FF // BLOCKS
BF = jnp.bfloat16
F32 = jnp.float32

eps = 1e-06
ANY = pl.BlockSpec(memory_space=pl.ANY)
VMEM = pl.BlockSpec(memory_space=pltpu.VMEM)
SMEM = pl.BlockSpec(memory_space=pltpu.SMEM)


class Plan:
    def __init__(self, mesh, late=False):
        outer, inner = mesh.shape["dp"], mesh.shape["fsdp"]
        ys = outer // 2
        xs = min(ys, inner)
        zs = inner // xs
        self.devices = outer * inner
        self.half = self.devices // 2

        def bits(size, unit):
            found = []
            while size > 1:
                size //= 2
                found.append(size * unit)
            return found

        xbits = bits(xs, 1)
        zbits = bits(zs, xs)
        self.core = inner
        ybits = bits(ys, 2 * inner)
        self.late = late
        z_legs, xy_legs = [1, len(zbits) - 1], [len(xbits)] * 2
        if late:
            self.orders = (xbits + ybits + zbits, ybits + xbits + zbits)
            lengths = xy_legs + z_legs
        else:
            self.orders = (zbits + xbits + ybits, zbits + ybits + xbits)
            lengths = z_legs + xy_legs
        self.legs = []
        for length in lengths:
            start = self.legs[-1][-1] + 1 if self.legs else 0
            self.legs.append(list(range(start, start + length)))

    def pairs(self, stage):
        return [
            (i, i ^ self.orders[1 if i & self.core else 0][stage]) for i in range(self.devices)
        ]

    def core_pairs(self):
        return [(i, i ^ self.core) for i in range(self.devices)]

    def masks(self, which):
        found = [0]
        for bit in self.orders[which]:
            found = found + [mask ^ bit for mask in found]
        return found

    def positions(self, me):
        tables = jnp.array(
            [
                self.masks(0) + [mask ^ self.core for mask in self.masks(1)],
                self.masks(1) + [mask ^ self.core for mask in self.masks(0)],
            ],
            jnp.int32,
        )
        mine = jnp.where((me & self.core) > 0, tables[1], tables[0])
        return mine ^ me


class Line:
    def __init__(self):
        self.last = []

    def tie(self, *arrays):
        if not self.last:
            return arrays
        tied = lax.optimization_barrier((arrays, tuple(self.last)))
        return tied[0]

    def run(self, step, *arrays):
        result = step(*self.tie(*arrays))
        self.last = [result[0] if isinstance(result, (list, tuple)) else result]
        return result

    def send(self, array, pairs, name="swap"):
        with jax.named_scope(name):
            return lax.ppermute(self.tie(array)[0], AXES, pairs)

    def wait(self, *arrays):
        self.last.extend(arrays)


class Gather:
    def __init__(self, plan, line, name, block):
        self.plan, self.line, self.name = plan, line, name
        self.held = block[None]
        self.coming = None

    def take(self):
        self.line.wait(self.coming)
        self.held = self.line.run(
            lambda held, coming: jnp.concatenate([held, coming], 0), self.held, self.coming
        )

    def start(self, leg):
        for stage in self.plan.legs[leg]:
            if stage != self.plan.legs[leg][0]:
                self.take()
            self.coming = self.line.send(
                self.held, self.plan.pairs(stage), f"gather_{self.name}_{stage}"
            )

    def swap_first(self):
        self.first = self.line.send(
            self.held, self.plan.core_pairs(), f"gather_{self.name}_swap_first"
        )

    def arrive(self):
        self.line.wait(self.coming)

    def swap_second(self):
        self.second = self.line.send(
            self.coming, self.plan.core_pairs(), f"gather_{self.name}_swap_second"
        )

    def parts(self):
        self.line.wait(self.first, self.second)
        return [self.held, self.coming, self.first, self.second]


def total(parts):
    if len(parts) == 2:
        return parts[0] + parts[1]
    result = parts[0].astype(F32)
    for part in parts[1:]:
        result = result + part.astype(F32)
    return result


class Scatter:
    def __init__(self, plan, line, name, parts):
        self.plan, self.line, self.name = plan, line, name
        keep_low, keep_high, send_low, send_high = parts
        self.high = [keep_high, line.send(send_high, plan.core_pairs(), f"sum_{name}_swap_high")]
        self.low = [keep_low, line.send(send_low, plan.core_pairs(), f"sum_{name}_swap_low")]
        self.side = []
        self.count = keep_low.shape[0]
        self.width = keep_low.shape[-1]

    def join(self, parts):
        half = self.plan.half
        self.side = [
            parts[:half],
            self.line.send(parts[half:], self.plan.core_pairs(), f"sum_{self.name}_swap_side"),
        ]

    def sum(self, low, high, parts):
        wide = total([part[low:high, :, : self.width] for part in parts])
        if not self.side:
            return wide
        offset = low if self.high is None else low + self.count
        narrow = [part[low:high, :, self.width :] for part in parts[2:]]
        narrow += [part[offset : offset + high - low] for part in self.side]
        return jnp.concatenate([wide, total(narrow)], -1)

    def start(self, leg):
        for stage in reversed(self.plan.legs[leg]):
            if self.high is not None:
                parts, low = self.high, 0
            else:
                self.count //= 2
                parts, low = self.low, self.count
            self.line.wait(parts[-1], *self.side)
            outgoing = self.line.run(
                lambda *parts: self.sum(low, low + self.count, parts).astype(BF), *parts
            )
            self.high = None
            self.low.append(
                self.line.send(outgoing, self.plan.pairs(stage), f"sum_{self.name}_{stage}")
            )

    def arrive(self):
        self.line.wait(self.low[-1])

    def result(self):
        self.arrive()
        return self.line.run(lambda *parts: self.sum(0, 1, parts)[0].astype(F32), *self.low)


def one_hot(order):
    return (order[:, None] == jnp.arange(order.shape[0])[None, :]).astype(BF)


def to_blocks(order, parts):
    if order.shape[0] == BLOCKS:
        return parts
    width = parts[0].shape[-1]
    joined = jnp.concatenate(parts, 0).reshape(order.shape[0], -1)
    spread = lax.dot_general(
        one_hot(order), joined, (((0,), (0,)), ((), ())), preferred_element_type=BF
    ).reshape(4, BLOCKS // 4, -1, width)
    return [spread[i] for i in range(4)]


def from_blocks(order, parts):
    count = order.shape[0]
    if count == BLOCKS:
        return parts
    width = parts[0].shape[-1]
    joined = jnp.concatenate(parts, 0).reshape(count, -1)
    moved = jnp.dot(one_hot(order), joined, preferred_element_type=BF)
    moved = moved.reshape(4, count // 4, -1, width)
    return [moved[i] for i in range(4)]


def params(limit):
    return pltpu.CompilerParams(vmem_limit_bytes=limit << 20)


def rows_of(ref, number, rows):
    return ref.at[pl.ds(pl.multiple_of(number * rows, rows), rows), :]


def fetches(order_ref, part_refs, held_ref, sems, start=0, width=None):
    each, rows, _ = part_refs[0].shape
    width = held_ref.shape[1] if width is None else width
    copies = []
    for place in range(BLOCKS):
        source = part_refs[place // each].at[place % each, :, pl.ds(start, width)]
        number = order_ref[place]
        copies.append(
            pltpu.make_async_copy(source, rows_of(held_ref, number, rows), sems.at[number])
        )
    return copies


def norm_parts(values):
    centre = values - jnp.mean(values, axis=-1, keepdims=True)
    inverse = lax.rsqrt(jnp.mean(centre * centre, axis=-1, keepdims=True) + eps)
    return centre * inverse, inverse


def norm_back(grad_norm, normed, inverse):
    return inverse * (
        grad_norm
        - jnp.mean(grad_norm, axis=-1, keepdims=True)
        - normed * jnp.mean(grad_norm * normed, axis=-1, keepdims=True)
    )


def span(index, size):
    if isinstance(index, int):
        return pl.ds(index * size, size)
    return pl.ds(pl.multiple_of(index * size, size), size)


def each(count):
    def run(body):
        for index in range(count):
            body(index)

    return run


def dot(a, b):
    return jnp.dot(a, b, preferred_element_type=F32)


def dot_nt(a, b):
    return lax.dot_general(a, b, (((1,), (1,)), ((), ())), preferred_element_type=F32)


def dot_tn(a, b):
    return lax.dot_general(a, b, (((0,), (0,)), ((), ())), preferred_element_type=F32)


def stacked(values):
    head = lax.broadcasted_iota(jnp.int32, values.shape, 1) // HEAD_DIM
    zero = jnp.zeros_like(values)
    return jnp.concatenate([jnp.where(head == h, values, zero) for h in range(GROUP)], 0)


def unstacked(values):
    rows = values.shape[0] // GROUP
    head = lax.broadcasted_iota(jnp.int32, (rows, values.shape[1]), 1) // HEAD_DIM
    result = values[:rows]
    for h in range(1, GROUP):
        result = jnp.where(head == h, values[h * rows : (h + 1) * rows], result)
    return result


def project_kernel(
    order_ref, vec_ref, x_ref, w0, w1, w2, w3, entry_ref, project_ref, held, sems
):
    copies = fetches(order_ref, (w0, w1, w2, w3), held, sems)
    for copy in copies:
        copy.start()

    @each(x_ref.shape[0] // CHUNK)
    def _(i):
        normed, _ = norm_parts(x_ref[span(i, CHUNK), :].astype(F32))
        entry_ref[span(i, CHUNK), :] = (normed * vec_ref[0:1, :] + vec_ref[2:3, :]).astype(BF)

    for copy in copies:
        copy.wait()

    @each(3 * D // TILE)
    def _(i):
        third = i // (D // TILE)
        column = span(i % (D // TILE), TILE)
        part = dot(entry_ref[...], held[:, span(i, TILE)])
        if third != 1:
            part = part + vec_ref[pl.ds(3 if third == 0 else 4, 1), column]
        project_ref[:, span(i, TILE)] = part.astype(BF)


def project_all(order, vec, x, *first):
    count = x.shape[0]
    shape = jax.ShapeDtypeStruct
    return pl.pallas_call(
        project_kernel,
        out_shape=[shape((count, D), BF), shape((count, 3 * D), BF)],
        in_specs=[SMEM] + [VMEM] * 2 + [ANY] * 4,
        out_specs=[VMEM] * 2,
        scratch_shapes=[pltpu.VMEM((D, 3 * D), BF), pltpu.SemaphoreType.DMA((BLOCKS,))],
        compiler_params=params(32),
        name="project",
    )(order, vec, x, *first)


def attend_kernel(project_ref, idr_ref, idc_ref, probs_ref, mixed_ref, probs, out_sems):
    groups = D // WIDE
    copies = []

    @each((mixed_ref.shape[0] // SEQ) * groups)
    def _(i):
        row, group = i // groups, i % groups
        rows = span(row, SEQ)
        queries = project_ref[rows, span(group, WIDE)] * BF(HEAD_DIM**-0.5)
        keys = project_ref[rows, span(groups + group, WIDE)]
        values = project_ref[rows, span(2 * groups + group, WIDE)]
        scores = dot_nt(stacked(queries), keys)
        same = idc_ref[rows, :] == idr_ref[pl.ds(row, 1), :]
        scores = jnp.where(same[None], scores.reshape(GROUP, SEQ, SEQ), -1e9)
        expo = jnp.exp(scores - jnp.max(scores, axis=-1, keepdims=True))
        low = (expo / jnp.sum(expo, axis=-1, keepdims=True)).astype(BF)
        low = low.reshape(GROUP * SEQ, SEQ)
        probs[i] = low
        copy = pltpu.make_async_copy(probs.at[i], probs_ref.at[i], out_sems.at[i])
        copy.start()
        copies.append(copy)
        mixed_ref[rows, span(group, WIDE)] = unstacked(dot(low, values)).astype(BF)

    for copy in copies:
        copy.wait()


def attend(project, ids):
    count = project.shape[0]
    steps = (count // SEQ) * (D // WIDE)
    shape = jax.ShapeDtypeStruct
    return pl.pallas_call(
        attend_kernel,
        out_shape=[shape((steps, GROUP * SEQ, SEQ), BF), shape((count, D), BF)],
        in_specs=[VMEM] * 3,
        out_specs=[ANY, VMEM],
        scratch_shapes=[
            pltpu.VMEM((steps, GROUP * SEQ, SEQ), BF),
            pltpu.SemaphoreType.DMA((steps,)),
        ],
        compiler_params=params(32),
        name="attend",
    )(project, ids, ids.reshape(count, 1))


def piece(number):
    return pl.ds(pl.multiple_of(number * PIECE, PIECE), PIECE)


def settle_kernel(
    order_ref, vec_ref, x_ref, mixed_ref, w0, w1, w2, w3, middle_ref, second_ref, held, sems
):
    copies = fetches(order_ref, (w0, w1, w2, w3), held, sems, FF)
    for copy in copies:
        copy.start()
    for copy in copies:
        copy.wait()

    @each(D // TILE)
    def _(i):
        columns = span(i, TILE)
        branch = dot(mixed_ref[...], held[:, columns]) + vec_ref[5:6, columns]
        middle_ref[:, columns] = x_ref[:, columns].astype(F32) + branch

    @pl.loop(0, x_ref.shape[0] // CHUNK)
    def _(i):
        normed, _ = norm_parts(middle_ref[span(i, CHUNK), :])
        second_ref[span(i, CHUNK), :] = (normed * vec_ref[1:2, :] + vec_ref[6:7, :]).astype(BF)


def settle(order, vec, x, mixed, *win):
    count = x.shape[0]
    shape = jax.ShapeDtypeStruct
    return pl.pallas_call(
        settle_kernel,
        out_shape=[shape((count, D), F32), shape((count, D), BF)],
        in_specs=[SMEM] + [VMEM] * 3 + [ANY] * 4,
        out_specs=[VMEM] * 2,
        scratch_shapes=[pltpu.VMEM((D, D), BF), pltpu.SemaphoreType.DMA((BLOCKS,))],
        compiler_params=params(32),
        name="settle",
    )(order, vec, x, mixed, *win)


def rise_kernel(
    order_ref, bias_ref, second_ref, top_ref, w0, w1, w2, w3,
    active_ref, slope_ref, g0, g1, g2, g3,
    held, active, slope, grads, sems, tile_sems,
):
    copies = fetches(order_ref, (w0, w1, w2, w3), held, sems)
    for copy in copies:
        copy.start()
    for copy in copies:
        copy.wait()
    outs = []
    places = TILE // PIECE

    @each(FF // TILE)
    def _(step):
        columns = span(step, TILE)
        numbers = [order_ref[step * places + j] for j in range(places)]
        weight = jnp.concatenate([held[:, piece(number)] for number in numbers], 1)
        bias = jnp.concatenate([bias_ref[:, piece(number)] for number in numbers], 1)
        hidden = dot(second_ref[...], weight) + bias
        cdf = 0.5 + 0.5 * lax.erf(hidden * (0.5**0.5))
        grow = cdf + hidden * jnp.exp(-0.5 * hidden * hidden) * 0.3989422804014327
        low = (hidden * cdf).astype(BF)
        active[:, columns] = low
        slope[:, columns] = grow.astype(BF)
        grad = dot_tn(low, top_ref[...]).astype(BF)
        block = pl.ds(step * places, places)
        grads[block] = grad.reshape(places, PIECE, D)
        apiece = g0.shape[0]
        target = (g0, g1, g2, g3)[step * places // apiece]
        target = target.at[pl.ds(step * places % apiece, places)]
        for number, (source, target) in enumerate(
            (
                (active.at[:, columns], active_ref.at[:, columns]),
                (slope.at[:, columns], slope_ref.at[:, columns]),
                (grads.at[block], target),
            )
        ):
            copy = pltpu.make_async_copy(source, target, tile_sems.at[step, number])
            copy.start()
            outs.append(copy)

    for copy in outs:
        copy.wait()


def rise(order, bias, second, top, *win):
    count = second.shape[0]
    shape = jax.ShapeDtypeStruct
    grad = shape((BLOCKS // 4, PIECE, D), BF)
    return pl.pallas_call(
        rise_kernel,
        out_shape=[shape((count, FF), BF)] * 2 + [grad] * 4,
        in_specs=[SMEM] + [VMEM] * 3 + [ANY] * 4,
        out_specs=[ANY] * 6,
        scratch_shapes=[
            pltpu.VMEM((D, FF), BF),
            pltpu.VMEM((count, FF), BF),
            pltpu.VMEM((count, FF), BF),
            pltpu.VMEM((BLOCKS, PIECE, D), BF),
            pltpu.SemaphoreType.DMA((BLOCKS,)),
            pltpu.SemaphoreType.DMA((FF // TILE, 3)),
        ],
        compiler_params=params(48),
        name="rise",
    )(order, bias, second, top, *win)


def mlp_fetches(spot_ref, early_refs, late_refs, held_ref, sems):
    apiece, _, width = early_refs[0].shape
    early = [
        pltpu.make_async_copy(
            part, held_ref.at[pl.ds(i * apiece, apiece), :, pl.ds(0, width)], sems.at[BLOCKS + i]
        )
        for i, part in enumerate(early_refs)
    ]
    late = [
        pltpu.make_async_copy(
            late_refs[place // apiece].at[place % apiece],
            held_ref.at[spot_ref[place], :, pl.ds(width, width)],
            sems.at[spot_ref[place]],
        )
        for place in range(BLOCKS)
    ]
    return early, late


def start(copies):
    for copy in copies:
        copy.start()


def wait(copies):
    for copy in copies:
        copy.wait()


def block_rows(order_ref, ref, part, apiece, rows):
    return jnp.concatenate(
        [ref[span(order_ref[part * apiece + j], rows), :] for j in range(apiece)], 0
    )


def fall_kernel(
    order_ref, spot_ref, top_ref, slope_ref, second_ref,
    m0, m1, m2, m3, l0, l1, l2, l3,
    ghidden_ref, bias_ref, g0, g1, g2, g3,
    mheld, slope, ghidden, turned, grads, msems, tile_sems, out_sems,
):
    copies, late = mlp_fetches(spot_ref, (m0, m1, m2, m3), (l0, l1, l2, l3), mheld, msems)
    apiece, rows, _ = g0.shape
    places = TILE // PIECE
    slopes = [
        pltpu.make_async_copy(
            slope_ref.at[:, span(i, FF // 4)], slope.at[:, span(i, FF // 4)], tile_sems.at[i]
        )
        for i in range(4)
    ]
    for i in range(4):
        copies[i].start()
        slopes[i].start()
        if i == 0:
            for copy in late:
                copy.start()
    turned[...] = second_ref[...].T

    @each(FF // TILE)
    def _(step):
        part = step * places // apiece
        if step * places % apiece == 0:
            copies[part].wait()
            slopes[part].wait()
        for place in range(step * places, (step + 1) * places):
            pltpu.make_async_copy(
                l0.at[0], mheld.at[place, :, pl.ds(D // 2, D // 2)], msems.at[place]
            ).wait()
        weight = mheld[pl.ds(step * places, places)].reshape(TILE, D)
        grad_active = dot_nt(top_ref[...], weight)
        grad = grad_active * slope[:, span(step, TILE)].astype(F32)
        low = grad.astype(BF)
        sums = jnp.sum(low.astype(F32), axis=0, keepdims=True)
        for j in range(places):
            number = order_ref[step * places + j]
            ghidden[:, piece(number)] = low[:, j * PIECE : (j + 1) * PIECE]
            bias_ref[:, piece(number)] = sums[:, j * PIECE : (j + 1) * PIECE]

    outs = [pltpu.make_async_copy(ghidden, ghidden_ref, out_sems.at[4])]
    start(outs)
    for part in (3, 2, 1, 0):
        left = block_rows(order_ref, turned, part, apiece, rows)
        for i in range(FF // TILE):
            grad = dot(left, ghidden[:, span(i, TILE)]).astype(BF)
            grads[part, :, :, span(i, TILE)] = grad.reshape(apiece, rows, TILE)
        copy = pltpu.make_async_copy(grads.at[part], (g0, g1, g2, g3)[part], out_sems.at[part])
        copy.start()
        outs.append(copy)
    for copy in outs:
        copy.wait()


def fall(order, spot, top, slope, second, *mlp):
    count = second.shape[0]
    shape = jax.ShapeDtypeStruct
    grad = shape((BLOCKS // 4, D // BLOCKS, FF), BF)
    return pl.pallas_call(
        fall_kernel,
        out_shape=[shape((count, FF), BF), shape((1, FF), F32)] + [grad] * 4,
        in_specs=[SMEM, SMEM, VMEM, ANY, VMEM] + [ANY] * 8,
        out_specs=[ANY, VMEM] + [ANY] * 4,
        scratch_shapes=[
            pltpu.VMEM((BLOCKS, PIECE, D), BF),
            pltpu.VMEM((count, FF), BF),
            pltpu.VMEM((count, FF), BF),
            pltpu.VMEM((D, count), BF),
            pltpu.VMEM((4, *grad.shape), BF),
            pltpu.SemaphoreType.DMA((BLOCKS + 4,)),
            pltpu.SemaphoreType.DMA((4,)),
            pltpu.SemaphoreType.DMA((5,)),
        ],
        compiler_params=params(40),
        name="fall",
    )(order, spot, top, slope, second, *mlp)


def back_kernel(
    order_ref, vec_ref, ghidden_ref, top_ref, middle_ref, w0, w1, w2, w3,
    gmiddle_ref, sums_ref,
    held, ghidden, middle, gsecond, gmiddle, sems, in_sems, out_sems,
):
    later = [
        pltpu.make_async_copy(ghidden_ref, ghidden, in_sems.at[0]),
        *fetches(order_ref, (w0, w1, w2, w3), held, sems),
        pltpu.make_async_copy(middle_ref, middle, in_sems.at[1]),
    ]
    start(later)
    sums_ref[...] = jnp.zeros_like(sums_ref)
    outs = []
    for copy in later:
        copy.wait()
    chunk = middle_ref.shape[0] // 2
    for half in range(2):
        where = span(half, chunk)
        for i in range(D // TILE):
            gsecond[where, span(i, TILE)] = dot_nt(ghidden[where, :], held[span(i, TILE), :])
        normed, inverse = norm_parts(middle[where, :])
        grad = gsecond[where, :]
        top = top_ref[where, :].astype(F32)
        total_grad = top + norm_back(grad * vec_ref[1:2, :], normed, inverse)
        gmiddle[where, :] = total_grad
        copy = pltpu.make_async_copy(
            gmiddle.at[where, :], gmiddle_ref.at[where, :], out_sems.at[half]
        )
        copy.start()
        outs.append(copy)
        low = total_grad.astype(BF).astype(F32)
        for row, value in enumerate((grad * normed, grad, low, top)):
            sums_ref[row : row + 1, :] += jnp.sum(value, axis=0, keepdims=True)
    wait(outs)


def back(order, vec, ghidden, top, middle, *win):
    count = middle.shape[0]
    shape = jax.ShapeDtypeStruct
    return pl.pallas_call(
        back_kernel,
        out_shape=[shape((count, D), F32), shape((8, D), F32)],
        in_specs=[SMEM, VMEM, ANY, VMEM, ANY] + [ANY] * 4,
        out_specs=[ANY, VMEM],
        scratch_shapes=[
            pltpu.VMEM((D, FF), BF),
            pltpu.VMEM((count, FF), BF),
            pltpu.VMEM((count, D), F32),
            pltpu.VMEM((count, D), F32),
            pltpu.VMEM((count, D), F32),
            pltpu.SemaphoreType.DMA((BLOCKS,)),
            pltpu.SemaphoreType.DMA((2,)),
            pltpu.SemaphoreType.DMA((2,)),
        ],
        compiler_params=params(32),
        name="back",
    )(order, vec, ghidden, top, middle, *win)


def unattend_kernel(
    order_ref, vec_ref, x_ref, gmiddle_ref, project_ref, probs_ref, entry_ref, mixed_ref,
    w0, w1, w2, w3, f0, f1, f2, f3,
    ginputs_ref, sums_ref, g0, g1, g2, g3,
    oheld, held, project, probs, both, turned, branch, gmixed, gproject, gentry, ginputs, grads,
    osems, sems, in_sems, probs_sems, out_sems,
):
    count = gmiddle_ref.shape[0]
    groups = D // WIDE
    ocopies = fetches(order_ref, (w0, w1, w2, w3), oheld, osems, FF)
    load = [
        pltpu.make_async_copy(project_ref, project, in_sems.at[0]),
        pltpu.make_async_copy(entry_ref, both.at[0], in_sems.at[1]),
        pltpu.make_async_copy(mixed_ref, both.at[1], in_sems.at[2]),
    ]
    pieces = [
        pltpu.make_async_copy(probs_ref.at[i], probs.at[i], probs_sems.at[i])
        for i in range((count // SEQ) * groups)
    ]
    copies = fetches(order_ref, (f0, f1, f2, f3), held, sems)
    start([load[2], *ocopies])
    branch[...] = gmiddle_ref[...].astype(BF)
    sums_ref[...] = jnp.zeros_like(sums_ref)
    apiece, rows, _ = g0.shape
    load[2].wait()
    start([load[0]])
    turned[1] = both[1].T
    for part in (3, 2, 1, 0):
        left = block_rows(order_ref, turned.at[1], part, apiece, rows)
        for i in range(D // TILE):
            grad = dot(left, branch[:, span(i, TILE)]).astype(BF)
            grads[part, :, :, span(3 * D // TILE + i, TILE)] = grad.reshape(apiece, rows, TILE)
    wait(ocopies)
    start(pieces[:2])

    @each(D // TILE)
    def _(i):
        gmixed[:, span(i, TILE)] = dot_nt(branch[...], oheld[span(i, TILE), :]).astype(BF)

    load[0].wait()

    @each((count // SEQ) * groups)
    def _(i):
        row, group = i // groups, i % groups
        where = span(row, SEQ)
        scale = HEAD_DIM**-0.5
        pieces[i].wait()
        if i % 2 == 0:
            start(pieces[i + 2 : i + 4] if i + 2 < len(pieces) else [load[1], *copies])
        queries = stacked(project[where, span(group, WIDE)] * BF(scale))
        keys = project[where, span(groups + group, WIDE)]
        values = project[where, span(2 * groups + group, WIDE)]
        gmix = stacked(gmixed[where, span(group, WIDE)])
        low = probs[i]
        gprobs = dot_nt(gmix, values)
        gvalues = dot_tn(low, gmix)
        weight = low.astype(F32)
        inner = jnp.sum(weight * gprobs, axis=-1, keepdims=True)
        gscores = (weight * (gprobs - inner)).astype(BF)
        gqueries = unstacked(dot(gscores, keys)) * scale
        gkeys = dot_tn(gscores, queries)
        for third, grad in enumerate((gqueries, gkeys, gvalues)):
            low = grad.astype(BF)
            gproject[where, span(third * groups + group, WIDE)] = low
            sums_ref[third : third + 1, span(group, WIDE)] += jnp.sum(
                low.astype(F32), axis=0, keepdims=True
            )

    load[1].wait()
    turned[0] = both[0].T
    outs = []
    for part in (3, 2, 1, 0):
        left = block_rows(order_ref, turned.at[0], part, apiece, rows)
        for i in range(3 * D // TILE):
            grad = dot(left, gproject[:, span(i, TILE)]).astype(BF)
            grads[part, :, :, span(i, TILE)] = grad.reshape(apiece, rows, TILE)
        copy = pltpu.make_async_copy(grads.at[part], (g0, g1, g2, g3)[part], out_sems.at[part])
        copy.start()
        outs.append(copy)
    for copy in copies:
        copy.wait()
    chunk = count // 2
    for half in range(2):
        where = span(half, chunk)
        for i in range(D // TILE):
            gentry[where, span(i, TILE)] = dot_nt(gproject[where, :], held[span(i, TILE), :])
        normed, inverse = norm_parts(x_ref[where, :].astype(F32))
        grad = gentry[where, :]
        back = norm_back(grad * vec_ref[0:1, :], normed, inverse)
        ginputs[where, :] = gmiddle_ref[where, :] + back
        copy = pltpu.make_async_copy(
            ginputs.at[where, :], ginputs_ref.at[where, :], out_sems.at[4 + half]
        )
        copy.start()
        outs.append(copy)
        sums_ref[3:4, :] += jnp.sum(grad * normed, axis=0, keepdims=True)
        sums_ref[4:5, :] += jnp.sum(grad, axis=0, keepdims=True)
    for copy in outs:
        copy.wait()


def unattend(order, vec, x, gmiddle, project, probs, entry, mixed, win, first):
    count = gmiddle.shape[0]
    shape = jax.ShapeDtypeStruct
    grad = shape((BLOCKS // 4, D // BLOCKS, 4 * D), BF)
    return pl.pallas_call(
        unattend_kernel,
        out_shape=[shape((count, D), F32), shape((8, D), F32)] + [grad] * 4,
        in_specs=[SMEM] + [VMEM] * 3 + [ANY] * 12,
        out_specs=[ANY, VMEM] + [ANY] * 4,
        scratch_shapes=[
            pltpu.VMEM((D, D), BF),
            pltpu.VMEM((D, 3 * D), BF),
            pltpu.VMEM((count, 3 * D), BF),
            pltpu.VMEM(probs.shape, BF),
            pltpu.VMEM((2, count, D), BF),
            pltpu.VMEM((2, D, count), BF),
            pltpu.VMEM((count, D), BF),
            pltpu.VMEM((count, D), BF),
            pltpu.VMEM((count, 3 * D), BF),
            pltpu.VMEM((count, D), F32),
            pltpu.VMEM((count, D), F32),
            pltpu.VMEM((4, *grad.shape), BF),
            pltpu.SemaphoreType.DMA((BLOCKS,)),
            pltpu.SemaphoreType.DMA((BLOCKS,)),
            pltpu.SemaphoreType.DMA((3,)),
            pltpu.SemaphoreType.DMA((probs.shape[0],)),
            pltpu.SemaphoreType.DMA((6,)),
        ],
        compiler_params=params(56),
        name="unattend",
    )(order, vec, x, gmiddle, project, probs, entry, mixed, *win, *first)


def finish_kernel(
    spot_ref, vec_ref, middle_ref, active_ref, m0, m1, m2, m3, l0, l1, l2, l3,
    out_ref, held, active, sems, tile_sems,
):
    copies = [
        pltpu.make_async_copy(
            active_ref.at[:, span(half, FF // 2)], active.at[half], tile_sems.at[half]
        )
        for half in range(2)
    ]
    early, late = mlp_fetches(spot_ref, (m0, m1, m2, m3), (l0, l1, l2, l3), held, sems)
    fetch = early + late
    for copy in fetch + copies:
        copy.start()
    for copy in fetch + copies:
        copy.wait()

    @each(D // WIDE)
    def _(i):
        columns = span(i, WIDE)
        weight = held[:, :, columns].reshape(FF, WIDE)
        result = dot(active[0], weight[: FF // 2])
        result = result + dot(active[1], weight[FF // 2 :]) + vec_ref[7:8, columns]
        out_ref[:, columns] = (middle_ref[:, columns] + result).astype(BF)


def finish(spot, vec, middle, active, *mlp):
    count = middle.shape[0]
    return pl.pallas_call(
        finish_kernel,
        out_shape=jax.ShapeDtypeStruct((count, D), BF),
        in_specs=[SMEM, VMEM, VMEM, ANY] + [ANY] * 8,
        out_specs=VMEM,
        scratch_shapes=[
            pltpu.VMEM((BLOCKS, PIECE, D), BF),
            pltpu.VMEM((2, count, FF // 2), BF),
            pltpu.SemaphoreType.DMA((BLOCKS + 4,)),
            pltpu.SemaphoreType.DMA((2,)),
        ],
        compiler_params=params(32),
        name="finish",
    )(spot, vec, middle, active, *mlp)


def per_device(plan, late_plan, inputs, image_ids, cotangent, gains, biases, w_qkv, w_out, w_in, w_mlp):
    me = lax.axis_index(AXES)
    order = plan.positions(me)
    gain_dev, bias_dev = gains.shape[1], biases.shape[1]
    small_dev = gain_dev + bias_dev
    rows = D // plan.devices
    blocks, length = image_ids.shape
    count = blocks * length
    x = inputs.reshape(count, D)
    numbers = order if plan.devices == BLOCKS else jnp.arange(BLOCKS, dtype=jnp.int32)
    late_order = late_plan.positions(me)
    spot = jnp.arange(BLOCKS, dtype=jnp.int32)
    if plan.devices == BLOCKS:
        spot = jnp.sum(jnp.where(late_order[:, None] == order[None], spot[None], 0), axis=1)
    line = Line()
    side = 128

    small = jnp.concatenate([gains, biases], 1)
    small = jnp.pad(small, ((0, 0), (0, rows * side - small_dev))).reshape(rows, side)
    first = Gather(plan, line, "qkv", jnp.concatenate([w_qkv.reshape(rows, 3 * D), small], 1))
    win = Gather(
        plan, line, "in", jnp.concatenate([w_in.reshape(rows, FF), w_out.reshape(rows, D)], 1)
    )
    mlp_block = w_mlp.reshape(FF // plan.devices, D)
    mlp = Gather(plan, line, "mlp", mlp_block[:, : D // 2])
    late = Gather(late_plan, line, "late", mlp_block[:, D // 2 :])
    top = jnp.where(image_ids.reshape(count, 1) >= 0, cotangent.reshape(count, D), BF(0))
    first.start(0)
    late.start(0)
    first.take()
    late.take()
    first.start(1)
    win.start(0)
    late.start(1)
    first.take()
    win.take()
    late.take()
    first.start(2)
    first.take()
    first.start(3)
    first.swap_first()
    win.start(1)
    first.arrive()
    win.take()
    first.swap_second()
    win.start(2)
    mlp.start(0)
    first_parts = first.parts()

    def unpack(*parts):
        placed = jnp.concatenate([part[:, :, 3 * D :] for part in parts], 0)
        placed = placed.reshape(-1, rows * side)[:, :small_dev]
        spread = lax.dot_general(
            one_hot(order), placed, (((0,), (0,)), ((), ())), preferred_element_type=F32
        )
        return jnp.concatenate(
            [spread[:, :gain_dev].reshape(-1), spread[:, gain_dev:].reshape(-1)]
        ).reshape(-1, D)

    vec = line.run(unpack, *first_parts)
    line.wait(*first_parts)
    bias_in = vec[8:12].reshape(1, FF)
    vec = vec[:8]
    if plan.devices != BLOCKS:
        first_parts = [part[:, :, : 3 * D] for part in first_parts]
    first_parts = to_blocks(order, first_parts)
    entry, project = line.run(project_all, numbers, vec, x, *first_parts)
    line.wait(mlp.coming)
    win.take()
    win.start(3)
    win.swap_first()
    mlp.take()
    mlp.start(1)
    late.start(2)
    probs, mixed = line.run(attend, project, image_ids)
    line.wait(mlp.coming, late.coming)
    win.arrive()
    line.wait(win.first)
    win.swap_second()
    mlp.take()
    mlp.start(2)
    win_parts = to_blocks(order, win.parts())
    middle, second = line.run(settle, numbers, vec, x, mixed, *win_parts)
    line.wait(mlp.coming)
    late.take()
    late.start(3)
    late.swap_first()
    mlp.take()
    mlp.start(3)
    mlp.swap_first()
    active, slope, *grads = line.run(rise, numbers, bias_in, second, top, *win_parts)
    line.wait(mlp.first, late.first)
    mlp.arrive()
    late.arrive()
    sum_mlp = Scatter(plan, line, "mlp", from_blocks(order, grads))
    mlp.swap_second()
    late.swap_second()
    sum_mlp.start(3)
    mlp_parts = to_blocks(order, mlp.parts()) + to_blocks(late_order, late.parts())
    ghidden, grad_bias_in, *grads = line.run(fall, numbers, spot, top, slope, second, *mlp_parts)
    sum_mlp.arrive()
    sum_in = Scatter(plan, line, "in", from_blocks(order, grads))
    sum_mlp.start(2)
    sum_in.start(3)
    gmiddle, sums = line.run(back, numbers, vec, ghidden, top, middle, *win_parts)
    grad_inputs, sums_one, *grads = line.run(
        unattend, numbers, vec, x, gmiddle, project, probs, entry, mixed, win_parts, first_parts
    )
    sum_mlp.arrive()
    sum_in.arrive()
    sum_first = Scatter(plan, line, "first", from_blocks(order, grads))

    def pack(sums_one, sums, grad_bias_in):
        flat_gains = jnp.concatenate([sums_one[3], sums[0]]).reshape(-1, gain_dev)
        flat_biases = jnp.concatenate(
            [sums_one[4], sums_one[0], sums_one[2], sums[2], sums[1], sums[3], grad_bias_in[0]]
        ).reshape(-1, bias_dev)
        flat_small = jnp.concatenate([flat_gains, flat_biases], 1).astype(BF)
        moved = jnp.dot(one_hot(order), flat_small, preferred_element_type=F32).astype(BF)
        moved = jnp.pad(moved, ((0, 0), (0, rows * side - small_dev)))
        return moved.reshape(plan.devices, rows, side)

    sum_first.join(pack(sums_one, sums, grad_bias_in))
    sum_in.start(2)
    sum_first.start(3)
    sum_mlp.start(1)
    output = line.run(finish, spot, vec, middle, active, *mlp_parts)
    sum_mlp.arrive()
    sum_in.start(1)
    sum_mlp.start(0)
    sum_in.arrive()
    sum_mlp.arrive()
    sum_first.start(2)
    sum_in.start(0)
    grad_mlp = sum_mlp.result()
    sum_in.arrive()
    sum_first.start(1)
    grad_in = sum_in.result()
    sum_first.start(0)
    grad_first = sum_first.result()
    grad_small = grad_first[:, 4 * D :].reshape(1, -1)[:, :small_dev]
    return (
        output.reshape(blocks, length, D),
        grad_inputs.reshape(blocks, length, D),
        grad_small[:, :gain_dev],
        grad_small[:, gain_dev:],
        grad_first[:, : 3 * D].reshape(1, -1),
        grad_first[:, 3 * D : 4 * D].reshape(1, -1),
        grad_in.reshape(1, -1),
        grad_mlp.reshape(1, -1),
    )


def solution(mesh):
    plan, late_plan = Plan(mesh), Plan(mesh, late=True)
    whole = P(AXES, None, None)
    flat = P(AXES, None)

    def body(*arrays):
        return per_device(plan, late_plan, *arrays)

    return jax.shard_map(
        body,
        mesh=mesh,
        in_specs=(whole, flat, whole, flat, flat, flat, flat, flat, flat),
        out_specs=(whole, whole, flat, flat, flat, flat, flat, flat),
        check_vma=False,
    )
```

```python
import jax
import jax.numpy as jnp
from jax import lax
from jax.experimental import pallas as pl
from jax.experimental.pallas import tpu as pltpu
from jax.sharding import PartitionSpec as P

D = 1024
FF = 4096
HEADS = 16
HEAD_DIM = 64
SEQ = 256
AXES = ("dp", "fsdp")
BLOCKS = 32
GROUP = 4
WIDE = GROUP * HEAD_DIM
TILE = 512
CHUNK = 128
PIECE = FF // BLOCKS
BF = jnp.bfloat16
F32 = jnp.float32

eps = 1e-06
ANY = pl.BlockSpec(memory_space=pl.ANY)
HBM = pl.BlockSpec(memory_space=pltpu.HBM)
VMEM = pl.BlockSpec(memory_space=pltpu.VMEM)
SMEM = pl.BlockSpec(memory_space=pltpu.SMEM)


class Plan:
    def __init__(self, mesh, late=False):
        outer, inner = mesh.shape["dp"], mesh.shape["fsdp"]
        ys = outer // 2
        xs = min(ys, inner)
        zs = inner // xs
        self.devices = outer * inner
        self.half = self.devices // 2

        def bits(size, unit):
            found = []
            while size > 1:
                size //= 2
                found.append(size * unit)
            return found

        xbits = bits(xs, 1)
        zbits = bits(zs, xs)
        self.core = inner
        ybits = bits(ys, 2 * inner)
        self.late = late
        z_legs, xy_legs = [1, len(zbits) - 1], [len(xbits)] * 2
        if late:
            self.orders = (xbits + ybits + zbits, ybits + xbits + zbits)
            lengths = xy_legs + z_legs
        else:
            self.orders = (zbits + xbits + ybits, zbits + ybits + xbits)
            lengths = z_legs + xy_legs
        self.legs = []
        for length in lengths:
            start = self.legs[-1][-1] + 1 if self.legs else 0
            self.legs.append(list(range(start, start + length)))

    def pairs(self, stage):
        return [
            (i, i ^ self.orders[1 if i & self.core else 0][stage]) for i in range(self.devices)
        ]

    def core_pairs(self):
        return [(i, i ^ self.core) for i in range(self.devices)]

    def masks(self, which):
        found = [0]
        for bit in self.orders[which]:
            found = found + [mask ^ bit for mask in found]
        return found

    def positions(self, me):
        tables = jnp.array(
            [
                self.masks(0) + [mask ^ self.core for mask in self.masks(1)],
                self.masks(1) + [mask ^ self.core for mask in self.masks(0)],
            ],
            jnp.int32,
        )
        mine = jnp.where((me & self.core) > 0, tables[1], tables[0])
        return mine ^ me


class Line:
    def __init__(self):
        self.last = []

    def tie(self, *arrays):
        if not self.last:
            return arrays
        tied = lax.optimization_barrier((arrays, tuple(self.last)))
        return tied[0]

    def run(self, step, *arrays):
        result = step(*self.tie(*arrays))
        self.last = [result[0] if isinstance(result, (list, tuple)) else result]
        return result

    def send(self, array, pairs, name="swap"):
        with jax.named_scope(name):
            return lax.ppermute(self.tie(array)[0], AXES, pairs)

    def wait(self, *arrays):
        self.last.extend(arrays)


class Gather:
    def __init__(self, plan, line, name, block):
        self.plan, self.line, self.name = plan, line, name
        self.held = block[None]
        self.coming = None

    def take(self):
        self.line.wait(self.coming)
        self.held = self.line.run(
            lambda held, coming: jnp.concatenate([held, coming], 0), self.held, self.coming
        )

    def start(self, leg):
        for stage in self.plan.legs[leg]:
            if stage != self.plan.legs[leg][0]:
                self.take()
            self.coming = self.line.send(
                self.held, self.plan.pairs(stage), f"gather_{self.name}_{stage}"
            )

    def swap_first(self):
        self.first = self.line.send(
            self.held, self.plan.core_pairs(), f"gather_{self.name}_swap_first"
        )

    def arrive(self):
        self.line.wait(self.coming)

    def swap_second(self):
        self.second = self.line.send(
            self.coming, self.plan.core_pairs(), f"gather_{self.name}_swap_second"
        )

    def parts(self):
        self.line.wait(self.first, self.second)
        return [self.held, self.coming, self.first, self.second]


def total(parts):
    if len(parts) == 2:
        return parts[0] + parts[1]
    result = parts[0].astype(F32)
    for part in parts[1:]:
        result = result + part.astype(F32)
    return result


class Scatter:
    def __init__(self, plan, line, name, parts):
        self.plan, self.line, self.name = plan, line, name
        keep_low, keep_high, send_low, send_high = parts
        self.high = [keep_high, line.send(send_high, plan.core_pairs(), f"sum_{name}_swap_high")]
        self.low = [keep_low, line.send(send_low, plan.core_pairs(), f"sum_{name}_swap_low")]
        self.side = []
        self.count = keep_low.shape[0]
        self.width = keep_low.shape[-1]
        self.owned = []

    def join(self, parts):
        half = self.plan.half
        self.side = [
            parts[:half],
            self.line.send(parts[half:], self.plan.core_pairs(), f"sum_{self.name}_swap_side"),
        ]

    def sum(self, low, high, parts):
        wide = total([part[low:high, :, : self.width] for part in parts])
        if not self.side:
            return wide
        offset = low if self.high is None else low + self.count
        narrow = [part[low:high, :, self.width :] for part in parts[2:]]
        narrow += [part[offset : offset + high - low] for part in self.side]
        return jnp.concatenate([wide, total(narrow)], -1)

    def start(self, leg):
        for stage in reversed(self.plan.legs[leg]):
            if self.high is not None:
                parts, low = self.high, 0
            else:
                self.count //= 2
                parts, low = self.low, self.count
            self.line.wait(parts[-1], *self.side)
            outgoing = self.line.run(
                lambda *parts: self.sum(low, low + self.count, parts).astype(BF), *parts
            )
            self.high = None
            self.low.append(
                self.line.send(outgoing, self.plan.pairs(stage), f"sum_{self.name}_{stage}")
            )

    def last(self):
        self.line.wait(self.low[-1])
        stages = self.plan.legs[0] + self.plan.legs[1]
        outgoing = self.line.run(
            lambda *parts: [
                self.sum(index, index + 1, parts).astype(BF) for index in range(1, self.count)
            ],
            *self.low,
        )
        for index in range(1, self.count):
            masks = [0, 0]
            for bit, stage in enumerate(stages):
                if index >> bit & 1:
                    masks = [mask ^ order[stage] for mask, order in zip(masks, self.plan.orders)]
            pairs = [(i, i ^ masks[1 if i & self.plan.core else 0]) for i in range(self.plan.devices)]
            self.owned.append(
                self.line.send(outgoing[index - 1], pairs, f"sum_{self.name}_last_{index}")
            )

    def arrive(self):
        self.line.wait(self.low[-1], *self.owned)

    def result(self):
        before = self.line.last
        self.arrive()
        count = len(self.low)

        def add(*parts):
            summed = self.sum(0, 1, parts[:count]).astype(F32)
            for part in parts[count:]:
                summed = summed + part.astype(F32)
            return summed[0]

        result = self.line.run(add, *self.low, *self.owned)
        self.line.last = before
        return result


def one_hot(order):
    return (order[:, None] == jnp.arange(order.shape[0])[None, :]).astype(BF)


def to_blocks(order, parts):
    if order.shape[0] == BLOCKS:
        return parts
    width = parts[0].shape[-1]
    joined = jnp.concatenate(parts, 0).reshape(order.shape[0], -1)
    spread = lax.dot_general(
        one_hot(order), joined, (((0,), (0,)), ((), ())), preferred_element_type=BF
    ).reshape(4, BLOCKS // 4, -1, width)
    return [spread[i] for i in range(4)]


def from_blocks(order, parts):
    count = order.shape[0]
    if count == BLOCKS:
        return parts
    width = parts[0].shape[-1]
    joined = jnp.concatenate(parts, 0).reshape(count, -1)
    moved = jnp.dot(one_hot(order), joined, preferred_element_type=BF)
    moved = moved.reshape(4, count // 4, -1, width)
    return [moved[i] for i in range(4)]


def params(limit):
    return pltpu.CompilerParams(vmem_limit_bytes=limit << 20)


def rows_of(ref, number, rows):
    return ref.at[pl.ds(pl.multiple_of(number * rows, rows), rows), :]


def fetches(order_ref, part_refs, held_ref, sems, start=0, width=None):
    each, rows, _ = part_refs[0].shape
    width = held_ref.shape[1] if width is None else width
    copies = []
    for place in range(BLOCKS):
        source = part_refs[place // each].at[place % each, :, pl.ds(start, width)]
        number = order_ref[place]
        copies.append(
            pltpu.make_async_copy(source, rows_of(held_ref, number, rows), sems.at[number])
        )
    return copies


def norm_parts(values):
    centre = values - jnp.mean(values, axis=-1, keepdims=True)
    inverse = lax.rsqrt(jnp.mean(centre * centre, axis=-1, keepdims=True) + eps)
    return centre * inverse, inverse


def norm_back(grad_norm, normed, inverse):
    return inverse * (
        grad_norm
        - jnp.mean(grad_norm, axis=-1, keepdims=True)
        - normed * jnp.mean(grad_norm * normed, axis=-1, keepdims=True)
    )


def span(index, size):
    if isinstance(index, int):
        return pl.ds(index * size, size)
    return pl.ds(pl.multiple_of(index * size, size), size)


def each(count):
    def run(body):
        for index in range(count):
            body(index)

    return run


def dot(a, b):
    return jnp.dot(a, b, preferred_element_type=F32)


def dot_nt(a, b):
    return lax.dot_general(a, b, (((1,), (1,)), ((), ())), preferred_element_type=F32)


def dot_tn(a, b):
    return lax.dot_general(a, b, (((0,), (0,)), ((), ())), preferred_element_type=F32)


def stacked(values):
    head = lax.broadcasted_iota(jnp.int32, values.shape, 1) // HEAD_DIM
    zero = jnp.zeros_like(values)
    return jnp.concatenate([jnp.where(head == h, values, zero) for h in range(GROUP)], 0)


def unstacked(values):
    rows = values.shape[0] // GROUP
    head = lax.broadcasted_iota(jnp.int32, (rows, values.shape[1]), 1) // HEAD_DIM
    result = values[:rows]
    for h in range(1, GROUP):
        result = jnp.where(head == h, values[h * rows : (h + 1) * rows], result)
    return result


def project_kernel(
    order_ref, vec_ref, x_ref, w0, w1, w2, w3, entry_ref, project_ref, held, sems
):
    copies = fetches(order_ref, (w0, w1, w2, w3), held, sems)
    for copy in copies:
        copy.start()

    @each(x_ref.shape[0] // CHUNK)
    def _(i):
        normed, _ = norm_parts(x_ref[span(i, CHUNK), :].astype(F32))
        entry_ref[span(i, CHUNK), :] = (normed * vec_ref[0:1, :] + vec_ref[2:3, :]).astype(BF)

    for copy in copies:
        copy.wait()

    @each(3 * D // TILE)
    def _(i):
        third = i // (D // TILE)
        column = span(i % (D // TILE), TILE)
        part = dot(entry_ref[...], held[:, span(i, TILE)])
        if third != 1:
            part = part + vec_ref[pl.ds(3 if third == 0 else 4, 1), column]
        project_ref[:, span(i, TILE)] = part.astype(BF)


def project_all(order, vec, x, *first):
    count = x.shape[0]
    shape = jax.ShapeDtypeStruct
    return pl.pallas_call(
        project_kernel,
        out_shape=[shape((count, D), BF), shape((count, 3 * D), BF)],
        in_specs=[SMEM] + [VMEM] * 2 + [ANY] * 4,
        out_specs=[VMEM] * 2,
        scratch_shapes=[pltpu.VMEM((D, 3 * D), BF), pltpu.SemaphoreType.DMA((BLOCKS,))],
        compiler_params=params(32),
        name="project",
    )(order, vec, x, *first)


def attend_kernel(project_ref, idr_ref, idc_ref, probs_ref, mixed_ref, probs, out_sems):
    groups = D // WIDE
    copies = []

    @each((mixed_ref.shape[0] // SEQ) * groups)
    def _(i):
        row, group = i // groups, i % groups
        rows = span(row, SEQ)
        queries = project_ref[rows, span(group, WIDE)] * BF(HEAD_DIM**-0.5)
        keys = project_ref[rows, span(groups + group, WIDE)]
        values = project_ref[rows, span(2 * groups + group, WIDE)]
        scores = dot_nt(stacked(queries), keys)
        same = idc_ref[rows, :] == idr_ref[pl.ds(row, 1), :]
        scores = jnp.where(same[None], scores.reshape(GROUP, SEQ, SEQ), -1e9)
        expo = jnp.exp(scores - jnp.max(scores, axis=-1, keepdims=True))
        low = (expo / jnp.sum(expo, axis=-1, keepdims=True)).astype(BF)
        low = low.reshape(GROUP * SEQ, SEQ)
        probs[i] = low
        copy = pltpu.make_async_copy(probs.at[i], probs_ref.at[i], out_sems.at[i])
        copy.start()
        copies.append(copy)
        mixed_ref[rows, span(group, WIDE)] = unstacked(dot(low, values)).astype(BF)

    for copy in copies:
        copy.wait()


def attend(project, ids):
    count = project.shape[0]
    steps = (count // SEQ) * (D // WIDE)
    shape = jax.ShapeDtypeStruct
    return pl.pallas_call(
        attend_kernel,
        out_shape=[shape((steps, GROUP * SEQ, SEQ), BF), shape((count, D), BF)],
        in_specs=[VMEM] * 3,
        out_specs=[ANY, VMEM],
        scratch_shapes=[
            pltpu.VMEM((steps, GROUP * SEQ, SEQ), BF),
            pltpu.SemaphoreType.DMA((steps,)),
        ],
        compiler_params=params(32),
        name="attend",
    )(project, ids, ids.reshape(count, 1))


def piece(number):
    return pl.ds(pl.multiple_of(number * PIECE, PIECE), PIECE)


def settle_kernel(
    order_ref, vec_ref, x_ref, mixed_ref, w0, w1, w2, w3, middle_ref, second_ref, held, sems
):
    copies = fetches(order_ref, (w0, w1, w2, w3), held, sems, FF)
    for copy in copies:
        copy.start()
    for copy in copies:
        copy.wait()

    @each(D // TILE)
    def _(i):
        columns = span(i, TILE)
        branch = dot(mixed_ref[...], held[:, columns]) + vec_ref[5:6, columns]
        middle_ref[:, columns] = x_ref[:, columns].astype(F32) + branch

    @pl.loop(0, x_ref.shape[0] // CHUNK)
    def _(i):
        normed, _ = norm_parts(middle_ref[span(i, CHUNK), :])
        second_ref[span(i, CHUNK), :] = (normed * vec_ref[1:2, :] + vec_ref[6:7, :]).astype(BF)


def settle(order, vec, x, mixed, *win):
    count = x.shape[0]
    shape = jax.ShapeDtypeStruct
    return pl.pallas_call(
        settle_kernel,
        out_shape=[shape((count, D), F32), shape((count, D), BF)],
        in_specs=[SMEM] + [VMEM] * 3 + [ANY] * 4,
        out_specs=[VMEM] * 2,
        scratch_shapes=[pltpu.VMEM((D, D), BF), pltpu.SemaphoreType.DMA((BLOCKS,))],
        compiler_params=params(32),
        name="settle",
    )(order, vec, x, mixed, *win)


def rise_kernel(
    order_ref, bias_ref, second_ref, top_ref, w0, w1, w2, w3,
    active_ref, slope_ref, g0, g1, g2, g3,
    held, active, slope, grads, sems, tile_sems,
):
    copies = fetches(order_ref, (w0, w1, w2, w3), held, sems)
    for copy in copies:
        copy.start()
    for copy in copies:
        copy.wait()
    outs = []
    places = TILE // PIECE

    @each(FF // TILE)
    def _(step):
        columns = span(step, TILE)
        numbers = [order_ref[step * places + j] for j in range(places)]
        weight = jnp.concatenate([held[:, piece(number)] for number in numbers], 1)
        bias = jnp.concatenate([bias_ref[:, piece(number)] for number in numbers], 1)
        hidden = dot(second_ref[...], weight) + bias
        cdf = 0.5 + 0.5 * lax.erf(hidden * (0.5**0.5))
        grow = cdf + hidden * jnp.exp(-0.5 * hidden * hidden) * 0.3989422804014327
        low = (hidden * cdf).astype(BF)
        active[:, columns] = low
        slope[:, columns] = grow.astype(BF)
        grad = dot_tn(low, top_ref[...]).astype(BF)
        block = pl.ds(step * places, places)
        grads[block] = grad.reshape(places, PIECE, D)
        apiece = g0.shape[0]
        target = (g0, g1, g2, g3)[step * places // apiece]
        target = target.at[pl.ds(step * places % apiece, places)]
        for number, (source, target) in enumerate(
            (
                (active.at[:, columns], active_ref.at[:, columns]),
                (slope.at[:, columns], slope_ref.at[:, columns]),
                (grads.at[block], target),
            )
        ):
            copy = pltpu.make_async_copy(source, target, tile_sems.at[step, number])
            copy.start()
            outs.append(copy)

    for copy in outs:
        copy.wait()


def rise(order, bias, second, top, *win):
    count = second.shape[0]
    shape = jax.ShapeDtypeStruct
    grad = shape((BLOCKS // 4, PIECE, D), BF)
    return pl.pallas_call(
        rise_kernel,
        out_shape=[shape((count, FF), BF)] * 2 + [grad] * 4,
        in_specs=[SMEM] + [VMEM] * 3 + [ANY] * 4,
        out_specs=[ANY] * 6,
        scratch_shapes=[
            pltpu.VMEM((D, FF), BF),
            pltpu.VMEM((count, FF), BF),
            pltpu.VMEM((count, FF), BF),
            pltpu.VMEM((BLOCKS, PIECE, D), BF),
            pltpu.SemaphoreType.DMA((BLOCKS,)),
            pltpu.SemaphoreType.DMA((FF // TILE, 3)),
        ],
        compiler_params=params(48),
        name="rise",
    )(order, bias, second, top, *win)


def mlp_fetches(spot_ref, early_refs, late_refs, held_ref, sems):
    apiece, _, width = early_refs[0].shape
    early = [
        pltpu.make_async_copy(
            part, held_ref.at[pl.ds(i * apiece, apiece), :, pl.ds(0, width)], sems.at[BLOCKS + i]
        )
        for i, part in enumerate(early_refs)
    ]
    late = [
        pltpu.make_async_copy(
            late_refs[place // apiece].at[place % apiece],
            held_ref.at[spot_ref[place], :, pl.ds(width, width)],
            sems.at[spot_ref[place]],
        )
        for place in range(BLOCKS)
    ]
    return early, late


def start(copies):
    for copy in copies:
        copy.start()


def wait(copies):
    for copy in copies:
        copy.wait()


def block_rows(order_ref, ref, part, apiece, rows):
    return jnp.concatenate(
        [ref[span(order_ref[part * apiece + j], rows), :] for j in range(apiece)], 0
    )


def fall_kernel(
    order_ref, spot_ref, top_ref, slope_ref, second_ref,
    m0, m1, m2, m3, l0, l1, l2, l3,
    ghidden_ref, bias_ref, g0, g1, g2, g3,
    mheld, slope, ghidden, turned, grads, msems, tile_sems, out_sems,
):
    copies, late = mlp_fetches(spot_ref, (m0, m1, m2, m3), (l0, l1, l2, l3), mheld, msems)
    apiece, rows, _ = g0.shape
    places = TILE // PIECE
    slopes = [
        pltpu.make_async_copy(
            slope_ref.at[:, span(i, FF // 4)], slope.at[:, span(i, FF // 4)], tile_sems.at[i]
        )
        for i in range(4)
    ]
    for i in range(4):
        copies[i].start()
        slopes[i].start()
        if i == 0:
            for copy in late:
                copy.start()
    turned[...] = second_ref[...].T

    @each(FF // TILE)
    def _(step):
        part = step * places // apiece
        if step * places % apiece == 0:
            copies[part].wait()
            slopes[part].wait()
        for place in range(step * places, (step + 1) * places):
            pltpu.make_async_copy(
                l0.at[0], mheld.at[place, :, pl.ds(D // 2, D // 2)], msems.at[place]
            ).wait()
        weight = mheld[pl.ds(step * places, places)].reshape(TILE, D)
        grad_active = dot_nt(top_ref[...], weight)
        grad = grad_active * slope[:, span(step, TILE)].astype(F32)
        low = grad.astype(BF)
        sums = jnp.sum(low.astype(F32), axis=0, keepdims=True)
        for j in range(places):
            number = order_ref[step * places + j]
            ghidden[:, piece(number)] = low[:, j * PIECE : (j + 1) * PIECE]
            bias_ref[:, piece(number)] = sums[:, j * PIECE : (j + 1) * PIECE]

    outs = [pltpu.make_async_copy(ghidden, ghidden_ref, out_sems.at[4])]
    start(outs)
    for part in (3, 2, 1, 0):
        left = block_rows(order_ref, turned, part, apiece, rows)
        for i in range(FF // TILE):
            grad = dot(left, ghidden[:, span(i, TILE)]).astype(BF)
            grads[part, :, :, span(i, TILE)] = grad.reshape(apiece, rows, TILE)
        copy = pltpu.make_async_copy(grads.at[part], (g0, g1, g2, g3)[part], out_sems.at[part])
        copy.start()
        outs.append(copy)
    for copy in outs:
        copy.wait()


def fall(order, spot, top, slope, second, *mlp):
    count = second.shape[0]
    shape = jax.ShapeDtypeStruct
    grad = shape((BLOCKS // 4, D // BLOCKS, FF), BF)
    return pl.pallas_call(
        fall_kernel,
        out_shape=[shape((count, FF), BF), shape((1, FF), F32)] + [grad] * 4,
        in_specs=[SMEM, SMEM, VMEM, ANY, VMEM] + [ANY] * 8,
        out_specs=[HBM, VMEM] + [ANY] * 4,
        scratch_shapes=[
            pltpu.VMEM((BLOCKS, PIECE, D), BF),
            pltpu.VMEM((count, FF), BF),
            pltpu.VMEM((count, FF), BF),
            pltpu.VMEM((D, count), BF),
            pltpu.VMEM((4, *grad.shape), BF),
            pltpu.SemaphoreType.DMA((BLOCKS + 4,)),
            pltpu.SemaphoreType.DMA((4,)),
            pltpu.SemaphoreType.DMA((5,)),
        ],
        compiler_params=params(40),
        name="fall",
    )(order, spot, top, slope, second, *mlp)


def back_kernel(
    order_ref, vec_ref, ghidden_ref, top_ref, middle_ref, w0, w1, w2, w3,
    gmiddle_ref, branch_ref, sums_ref,
    held, ghidden, middle, gsecond, gmiddle, branch, sems, in_sems, out_sems,
):
    later = [
        pltpu.make_async_copy(ghidden_ref, ghidden, in_sems.at[0]),
        *fetches(order_ref, (w0, w1, w2, w3), held, sems),
        pltpu.make_async_copy(middle_ref, middle, in_sems.at[1]),
    ]
    start(later)
    sums_ref[...] = jnp.zeros_like(sums_ref)
    outs = []
    for copy in later:
        copy.wait()
    chunk = middle_ref.shape[0] // 2
    for half in range(2):
        where = span(half, chunk)
        for i in range(D // TILE):
            gsecond[where, span(i, TILE)] = dot_nt(ghidden[where, :], held[span(i, TILE), :])
        normed, inverse = norm_parts(middle[where, :])
        grad = gsecond[where, :]
        top = top_ref[where, :].astype(F32)
        total_grad = top + norm_back(grad * vec_ref[1:2, :], normed, inverse)
        gmiddle[where, :] = total_grad
        copy = pltpu.make_async_copy(
            gmiddle.at[where, :], gmiddle_ref.at[where, :], out_sems.at[half]
        )
        copy.start()
        outs.append(copy)
        branch[where, :] = total_grad.astype(BF)
        low = total_grad.astype(BF).astype(F32)
        for row, value in enumerate((grad * normed, grad, low, top)):
            sums_ref[row : row + 1, :] += jnp.sum(value, axis=0, keepdims=True)
    outs.append(pltpu.make_async_copy(branch, branch_ref, out_sems.at[2]))
    outs[-1].start()
    wait(outs)


def back(order, vec, ghidden, top, middle, *win):
    count = middle.shape[0]
    shape = jax.ShapeDtypeStruct
    return pl.pallas_call(
        back_kernel,
        out_shape=[shape((count, D), F32), shape((count, D), BF), shape((8, D), F32)],
        in_specs=[SMEM, VMEM, HBM, VMEM, HBM] + [ANY] * 4,
        out_specs=[HBM, HBM, VMEM],
        scratch_shapes=[
            pltpu.VMEM((D, FF), BF),
            pltpu.VMEM((count, FF), BF),
            pltpu.VMEM((count, D), F32),
            pltpu.VMEM((count, D), F32),
            pltpu.VMEM((count, D), F32),
            pltpu.VMEM((count, D), BF),
            pltpu.SemaphoreType.DMA((BLOCKS,)),
            pltpu.SemaphoreType.DMA((2,)),
            pltpu.SemaphoreType.DMA((3,)),
        ],
        compiler_params=params(32),
        name="back",
    )(order, vec, ghidden, top, middle, *win)


def unattend_kernel(
    order_ref, vec_ref, x_ref, gmiddle_ref, branch_ref, project_ref, probs_ref, entry_ref, mixed_ref,
    w0, w1, w2, w3, f0, f1, f2, f3,
    ginputs_ref, sums_ref, g0, g1, g2, g3,
    oheld, held, project, probs, both, turned, gmiddle, branch, gmixed, gproject, gentry, ginputs, grads,
    osems, sems, in_sems, probs_sems, out_sems,
):
    count = x_ref.shape[0]
    groups = D // WIDE
    ocopies = fetches(order_ref, (w0, w1, w2, w3), oheld, osems, FF)
    load = [
        pltpu.make_async_copy(project_ref, project, in_sems.at[0]),
        pltpu.make_async_copy(entry_ref, both.at[0], in_sems.at[1]),
        pltpu.make_async_copy(mixed_ref, both.at[1], in_sems.at[2]),
        pltpu.make_async_copy(branch_ref, branch, in_sems.at[3]),
        pltpu.make_async_copy(gmiddle_ref, gmiddle, in_sems.at[4]),
    ]
    pieces = [
        pltpu.make_async_copy(probs_ref.at[i], probs.at[i], probs_sems.at[i])
        for i in range((count // SEQ) * groups)
    ]
    copies = fetches(order_ref, (f0, f1, f2, f3), held, sems)
    start([load[2], load[3], *ocopies])
    sums_ref[...] = jnp.zeros_like(sums_ref)
    apiece, rows, _ = g0.shape
    load[2].wait()
    start([load[0]])
    turned[1] = both[1].T
    load[3].wait()
    for part in (3, 2, 1, 0):
        left = block_rows(order_ref, turned.at[1], part, apiece, rows)
        for i in range(D // TILE):
            grad = dot(left, branch[:, span(i, TILE)]).astype(BF)
            grads[part, :, :, span(3 * D // TILE + i, TILE)] = grad.reshape(apiece, rows, TILE)
    wait(ocopies)
    start(pieces[:2])

    @each(D // TILE)
    def _(i):
        gmixed[:, span(i, TILE)] = dot_nt(branch[...], oheld[span(i, TILE), :]).astype(BF)

    load[0].wait()

    @each((count // SEQ) * groups)
    def _(i):
        row, group = i // groups, i % groups
        where = span(row, SEQ)
        scale = HEAD_DIM**-0.5
        pieces[i].wait()
        if i % 2 == 0:
            start(pieces[i + 2 : i + 4] if i + 2 < len(pieces) else [load[1], load[4], *copies])
        queries = stacked(project[where, span(group, WIDE)] * BF(scale))
        keys = project[where, span(groups + group, WIDE)]
        values = project[where, span(2 * groups + group, WIDE)]
        gmix = stacked(gmixed[where, span(group, WIDE)])
        low = probs[i]
        gprobs = dot_nt(gmix, values)
        gvalues = dot_tn(low, gmix)
        weight = low.astype(F32)
        inner = jnp.sum(weight * gprobs, axis=-1, keepdims=True)
        gscores = (weight * (gprobs - inner)).astype(BF)
        gqueries = unstacked(dot(gscores, keys)) * scale
        gkeys = dot_tn(gscores, queries)
        for third, grad in enumerate((gqueries, gkeys, gvalues)):
            low = grad.astype(BF)
            gproject[where, span(third * groups + group, WIDE)] = low
            sums_ref[third : third + 1, span(group, WIDE)] += jnp.sum(
                low.astype(F32), axis=0, keepdims=True
            )

    load[1].wait()
    turned[0] = both[0].T
    outs = []
    for part in (3, 2, 1, 0):
        left = block_rows(order_ref, turned.at[0], part, apiece, rows)
        for i in range(3 * D // TILE):
            grad = dot(left, gproject[:, span(i, TILE)]).astype(BF)
            grads[part, :, :, span(i, TILE)] = grad.reshape(apiece, rows, TILE)
        copy = pltpu.make_async_copy(grads.at[part], (g0, g1, g2, g3)[part], out_sems.at[part])
        copy.start()
        outs.append(copy)
    wait(copies)
    load[4].wait()
    chunk = count // 2
    for half in range(2):
        where = span(half, chunk)
        for i in range(D // TILE):
            gentry[where, span(i, TILE)] = dot_nt(gproject[where, :], held[span(i, TILE), :])
        normed, inverse = norm_parts(x_ref[where, :].astype(F32))
        grad = gentry[where, :]
        back = norm_back(grad * vec_ref[0:1, :], normed, inverse)
        ginputs[where, :] = gmiddle[where, :] + back
        copy = pltpu.make_async_copy(
            ginputs.at[where, :], ginputs_ref.at[where, :], out_sems.at[4 + half]
        )
        copy.start()
        outs.append(copy)
        sums_ref[3:4, :] += jnp.sum(grad * normed, axis=0, keepdims=True)
        sums_ref[4:5, :] += jnp.sum(grad, axis=0, keepdims=True)
    for copy in outs:
        copy.wait()


def unattend(order, vec, x, gmiddle, branch, project, probs, entry, mixed, win, first):
    count = gmiddle.shape[0]
    shape = jax.ShapeDtypeStruct
    grad = shape((BLOCKS // 4, D // BLOCKS, 4 * D), BF)
    return pl.pallas_call(
        unattend_kernel,
        out_shape=[shape((count, D), F32), shape((8, D), F32)] + [grad] * 4,
        in_specs=[SMEM] + [VMEM] * 2 + [HBM] * 6 + [ANY] * 8,
        out_specs=[ANY, VMEM] + [ANY] * 4,
        scratch_shapes=[
            pltpu.VMEM((D, D), BF),
            pltpu.VMEM((D, 3 * D), BF),
            pltpu.VMEM((count, 3 * D), BF),
            pltpu.VMEM(probs.shape, BF),
            pltpu.VMEM((2, count, D), BF),
            pltpu.VMEM((2, D, count), BF),
            pltpu.VMEM((count, D), F32),
            pltpu.VMEM((count, D), BF),
            pltpu.VMEM((count, D), BF),
            pltpu.VMEM((count, 3 * D), BF),
            pltpu.VMEM((count, D), F32),
            pltpu.VMEM((count, D), F32),
            pltpu.VMEM((4, *grad.shape), BF),
            pltpu.SemaphoreType.DMA((BLOCKS,)),
            pltpu.SemaphoreType.DMA((BLOCKS,)),
            pltpu.SemaphoreType.DMA((5,)),
            pltpu.SemaphoreType.DMA((probs.shape[0],)),
            pltpu.SemaphoreType.DMA((6,)),
        ],
        compiler_params=params(56),
        name="unattend",
    )(order, vec, x, gmiddle, branch, project, probs, entry, mixed, *win, *first)


def finish_kernel(
    spot_ref, vec_ref, middle_ref, active_ref, m0, m1, m2, m3, l0, l1, l2, l3,
    out_ref, held, active, sems, tile_sems,
):
    copies = [
        pltpu.make_async_copy(
            active_ref.at[:, span(half, FF // 2)], active.at[half], tile_sems.at[half]
        )
        for half in range(2)
    ]
    early, late = mlp_fetches(spot_ref, (m0, m1, m2, m3), (l0, l1, l2, l3), held, sems)
    fetch = early + late
    for copy in fetch + copies:
        copy.start()
    for copy in fetch + copies:
        copy.wait()

    @each(D // WIDE)
    def _(i):
        columns = span(i, WIDE)
        weight = held[:, :, columns].reshape(FF, WIDE)
        result = dot(active[0], weight[: FF // 2])
        result = result + dot(active[1], weight[FF // 2 :]) + vec_ref[7:8, columns]
        out_ref[:, columns] = (middle_ref[:, columns] + result).astype(BF)


def finish(spot, vec, middle, active, *mlp):
    count = middle.shape[0]
    return pl.pallas_call(
        finish_kernel,
        out_shape=jax.ShapeDtypeStruct((count, D), BF),
        in_specs=[SMEM, VMEM, VMEM, ANY] + [ANY] * 8,
        out_specs=VMEM,
        scratch_shapes=[
            pltpu.VMEM((BLOCKS, PIECE, D), BF),
            pltpu.VMEM((2, count, FF // 2), BF),
            pltpu.SemaphoreType.DMA((BLOCKS + 4,)),
            pltpu.SemaphoreType.DMA((2,)),
        ],
        compiler_params=params(32),
        name="finish",
    )(spot, vec, middle, active, *mlp)


def per_device(plan, late_plan, inputs, image_ids, cotangent, gains, biases, w_qkv, w_out, w_in, w_mlp):
    me = lax.axis_index(AXES)
    order = plan.positions(me)
    gain_dev, bias_dev = gains.shape[1], biases.shape[1]
    small_dev = gain_dev + bias_dev
    rows = D // plan.devices
    blocks, length = image_ids.shape
    count = blocks * length
    x = inputs.reshape(count, D)
    numbers = order if plan.devices == BLOCKS else jnp.arange(BLOCKS, dtype=jnp.int32)
    late_order = late_plan.positions(me)
    spot = jnp.arange(BLOCKS, dtype=jnp.int32)
    if plan.devices == BLOCKS:
        spot = jnp.sum(jnp.where(late_order[:, None] == order[None], spot[None], 0), axis=1)
    line = Line()
    side = 128

    small = jnp.concatenate([gains, biases], 1)
    small = jnp.pad(small, ((0, 0), (0, rows * side - small_dev))).reshape(rows, side)
    first = Gather(plan, line, "qkv", jnp.concatenate([w_qkv.reshape(rows, 3 * D), small], 1))
    win = Gather(
        plan, line, "in", jnp.concatenate([w_in.reshape(rows, FF), w_out.reshape(rows, D)], 1)
    )
    mlp_block = w_mlp.reshape(FF // plan.devices, D)
    mlp = Gather(plan, line, "mlp", mlp_block[:, : D // 2])
    late = Gather(late_plan, line, "late", mlp_block[:, D // 2 :])
    top = jnp.where(image_ids.reshape(count, 1) >= 0, cotangent.reshape(count, D), BF(0))
    first.start(0)
    late.start(0)
    first.take()
    late.take()
    first.start(1)
    win.start(0)
    late.start(1)
    first.take()
    win.take()
    late.take()
    first.start(2)
    first.take()
    first.start(3)
    first.swap_first()
    win.start(1)
    first.arrive()
    win.take()
    first.swap_second()
    win.start(2)
    mlp.start(0)
    first_parts = first.parts()

    def unpack(*parts):
        placed = jnp.concatenate([part[:, :, 3 * D :] for part in parts], 0)
        placed = placed.reshape(-1, rows * side)[:, :small_dev]
        spread = lax.dot_general(
            one_hot(order), placed, (((0,), (0,)), ((), ())), preferred_element_type=F32
        )
        return jnp.concatenate(
            [spread[:, :gain_dev].reshape(-1), spread[:, gain_dev:].reshape(-1)]
        ).reshape(-1, D)

    vec = line.run(unpack, *first_parts)
    line.wait(*first_parts)
    bias_in = vec[8:12].reshape(1, FF)
    vec = vec[:8]
    if plan.devices != BLOCKS:
        first_parts = [part[:, :, : 3 * D] for part in first_parts]
    first_parts = to_blocks(order, first_parts)
    entry, project = line.run(project_all, numbers, vec, x, *first_parts)
    line.wait(mlp.coming)
    win.take()
    win.start(3)
    win.swap_first()
    mlp.take()
    mlp.start(1)
    late.start(2)
    probs, mixed = line.run(attend, project, image_ids)
    line.wait(mlp.coming, late.coming)
    win.arrive()
    line.wait(win.first)
    win.swap_second()
    mlp.take()
    mlp.start(2)
    win_parts = to_blocks(order, win.parts())
    middle, second = line.run(settle, numbers, vec, x, mixed, *win_parts)
    line.wait(mlp.coming)
    late.take()
    late.start(3)
    late.swap_first()
    mlp.take()
    mlp.start(3)
    mlp.swap_first()
    active, slope, *grads = line.run(rise, numbers, bias_in, second, top, *win_parts)
    line.wait(mlp.first, late.first)
    mlp.arrive()
    late.arrive()
    sum_mlp = Scatter(plan, line, "mlp", from_blocks(order, grads))
    mlp.swap_second()
    late.swap_second()
    sum_mlp.start(3)
    mlp_parts = to_blocks(order, mlp.parts()) + to_blocks(late_order, late.parts())
    ghidden, grad_bias_in, *grads = line.run(fall, numbers, spot, top, slope, second, *mlp_parts)
    sum_in = Scatter(plan, line, "in", from_blocks(order, grads))
    sum_mlp.start(2)
    sum_in.start(3)
    gmiddle, branch, sums = line.run(back, numbers, vec, ghidden, top, middle, *win_parts)
    grad_inputs, sums_one, *grads = line.run(
        unattend, numbers, vec, x, gmiddle, branch, project, probs, entry, mixed, win_parts, first_parts
    )
    sum_mlp.arrive()
    sum_in.arrive()
    sum_first = Scatter(plan, line, "first", from_blocks(order, grads))

    def pack(sums_one, sums, grad_bias_in):
        flat_gains = jnp.concatenate([sums_one[3], sums[0]]).reshape(-1, gain_dev)
        flat_biases = jnp.concatenate(
            [sums_one[4], sums_one[0], sums_one[2], sums[2], sums[1], sums[3], grad_bias_in[0]]
        ).reshape(-1, bias_dev)
        flat_small = jnp.concatenate([flat_gains, flat_biases], 1).astype(BF)
        moved = jnp.dot(one_hot(order), flat_small, preferred_element_type=F32).astype(BF)
        moved = jnp.pad(moved, ((0, 0), (0, rows * side - small_dev)))
        return moved.reshape(plan.devices, rows, side)

    sum_first.join(pack(sums_one, sums, grad_bias_in))
    sum_in.start(2)
    sum_first.start(3)
    sum_mlp.start(1)
    output = line.run(finish, spot, vec, middle, active, *mlp_parts)
    sum_mlp.arrive()
    sum_in.start(1)
    sum_mlp.start(0)
    sum_in.arrive()
    sum_mlp.arrive()
    sum_first.start(2)
    sum_in.start(0)
    grad_mlp = sum_mlp.result()
    sum_in.arrive()
    sum_first.last()
    grad_in = sum_in.result()
    grad_first = sum_first.result()
    grad_small = grad_first[:, 4 * D :].reshape(1, -1)[:, :small_dev]
    return (
        output.reshape(blocks, length, D),
        grad_inputs.reshape(blocks, length, D),
        grad_small[:, :gain_dev],
        grad_small[:, gain_dev:],
        grad_first[:, : 3 * D].reshape(1, -1),
        grad_first[:, 3 * D : 4 * D].reshape(1, -1),
        grad_in.reshape(1, -1),
        grad_mlp.reshape(1, -1),
    )


def solution(mesh):
    plan, late_plan = Plan(mesh), Plan(mesh, late=True)
    whole = P(AXES, None, None)
    flat = P(AXES, None)

    def body(*arrays):
        return per_device(plan, late_plan, *arrays)

    return jax.shard_map(
        body,
        mesh=mesh,
        in_specs=(whole, flat, whole, flat, flat, flat, flat, flat, flat),
        out_specs=(whole, whole, flat, flat, flat, flat, flat, flat),
        check_vma=False,
    )
```

```python
import jax
import jax.numpy as jnp
from jax import lax
from jax.experimental import pallas as pl
from jax.experimental.pallas import tpu as pltpu
from jax.sharding import PartitionSpec as P

D = 1024
FF = 4096
HEADS = 16
HEAD_DIM = 64
SEQ = 256
AXES = ("dp", "fsdp")
BLOCKS = 32
GROUP = 4
WIDE = GROUP * HEAD_DIM
TILE = 512
CHUNK = 128
PIECE = FF // BLOCKS
BF = jnp.bfloat16
F32 = jnp.float32

eps = 1e-06
ANY = pl.BlockSpec(memory_space=pl.ANY)
HBM = pl.BlockSpec(memory_space=pltpu.HBM)
VMEM = pl.BlockSpec(memory_space=pltpu.VMEM)
SMEM = pl.BlockSpec(memory_space=pltpu.SMEM)


class Plan:
    def __init__(self, mesh, late=False):
        outer, inner = mesh.shape["dp"], mesh.shape["fsdp"]
        ys = outer // 2
        xs = min(ys, inner)
        zs = inner // xs
        self.devices = outer * inner
        self.half = self.devices // 2

        def bits(size, unit):
            found = []
            while size > 1:
                size //= 2
                found.append(size * unit)
            return found

        xbits = bits(xs, 1)
        zbits = bits(zs, xs)
        self.core = inner
        ybits = bits(ys, 2 * inner)
        self.late = late
        z_legs, xy_legs = [1, len(zbits) - 1], [len(xbits)] * 2
        if late:
            self.orders = (xbits + ybits + zbits, ybits + xbits + zbits)
            lengths = xy_legs + z_legs
        else:
            self.orders = (zbits + xbits + ybits, zbits + ybits + xbits)
            lengths = z_legs + xy_legs
        self.legs = []
        for length in lengths:
            start = self.legs[-1][-1] + 1 if self.legs else 0
            self.legs.append(list(range(start, start + length)))

    def pairs(self, stage):
        return [
            (i, i ^ self.orders[1 if i & self.core else 0][stage]) for i in range(self.devices)
        ]

    def core_pairs(self):
        return [(i, i ^ self.core) for i in range(self.devices)]

    def masks(self, which):
        found = [0]
        for bit in self.orders[which]:
            found = found + [mask ^ bit for mask in found]
        return found

    def positions(self, me):
        tables = jnp.array(
            [
                self.masks(0) + [mask ^ self.core for mask in self.masks(1)],
                self.masks(1) + [mask ^ self.core for mask in self.masks(0)],
            ],
            jnp.int32,
        )
        mine = jnp.where((me & self.core) > 0, tables[1], tables[0])
        return mine ^ me


class Line:
    def __init__(self):
        self.last = []

    def tie(self, *arrays):
        if not self.last:
            return arrays
        tied = lax.optimization_barrier((arrays, tuple(self.last)))
        return tied[0]

    def run(self, step, *arrays):
        result = step(*self.tie(*arrays))
        self.last = [result[0] if isinstance(result, (list, tuple)) else result]
        return result

    def send(self, array, pairs, name="swap"):
        with jax.named_scope(name):
            return lax.ppermute(self.tie(array)[0], AXES, pairs)

    def wait(self, *arrays):
        self.last.extend(arrays)


class Gather:
    def __init__(self, plan, line, name, block):
        self.plan, self.line, self.name = plan, line, name
        self.held = block[None]
        self.coming = None

    def take(self):
        self.line.wait(self.coming)
        self.held = self.line.run(
            lambda held, coming: jnp.concatenate([held, coming], 0), self.held, self.coming
        )

    def start(self, leg):
        for stage in self.plan.legs[leg]:
            if stage != self.plan.legs[leg][0]:
                self.take()
            self.coming = self.line.send(
                self.held, self.plan.pairs(stage), f"gather_{self.name}_{stage}"
            )

    def swap_first(self):
        self.first = self.line.send(
            self.held, self.plan.core_pairs(), f"gather_{self.name}_swap_first"
        )

    def arrive(self):
        self.line.wait(self.coming)

    def swap_second(self):
        self.second = self.line.send(
            self.coming, self.plan.core_pairs(), f"gather_{self.name}_swap_second"
        )

    def parts(self):
        self.line.wait(self.first, self.second)
        return [self.held, self.coming, self.first, self.second]


def total(parts):
    if len(parts) == 2:
        return parts[0] + parts[1]
    result = parts[0].astype(F32)
    for part in parts[1:]:
        result = result + part.astype(F32)
    return result


class Scatter:
    def __init__(self, plan, line, name, parts):
        self.plan, self.line, self.name = plan, line, name
        keep_low, keep_high, send_low, send_high = parts
        self.high = [keep_high, line.send(send_high, plan.core_pairs(), f"sum_{name}_swap_high")]
        self.low = [keep_low, line.send(send_low, plan.core_pairs(), f"sum_{name}_swap_low")]
        self.side = []
        self.count = keep_low.shape[0]
        self.width = keep_low.shape[-1]
        self.owned = []

    def join(self, parts):
        half = self.plan.half
        self.side = [
            parts[:half],
            self.line.send(parts[half:], self.plan.core_pairs(), f"sum_{self.name}_swap_side"),
        ]

    def sum(self, low, high, parts):
        wide = total([part[low:high, :, : self.width] for part in parts])
        if not self.side:
            return wide
        offset = low if self.high is None else low + self.count
        narrow = [part[low:high, :, self.width :] for part in parts[2:]]
        narrow += [part[offset : offset + high - low] for part in self.side]
        return jnp.concatenate([wide, total(narrow)], -1)

    def start(self, leg):
        for stage in reversed(self.plan.legs[leg]):
            if self.high is not None:
                parts, low = self.high, 0
            else:
                self.count //= 2
                parts, low = self.low, self.count
            self.line.wait(parts[-1], *self.side)
            outgoing = self.line.run(
                lambda *parts: self.sum(low, low + self.count, parts).astype(BF), *parts
            )
            self.high = None
            self.low.append(
                self.line.send(outgoing, self.plan.pairs(stage), f"sum_{self.name}_{stage}")
            )

    def last(self):
        self.line.wait(self.low[-1])
        stages = self.plan.legs[0] + self.plan.legs[1]
        outgoing = self.line.run(
            lambda *parts: [
                self.sum(index, index + 1, parts).astype(BF) for index in range(1, self.count)
            ],
            *self.low,
        )
        for index in range(1, self.count):
            masks = [0, 0]
            for bit, stage in enumerate(stages):
                if index >> bit & 1:
                    masks = [mask ^ order[stage] for mask, order in zip(masks, self.plan.orders)]
            pairs = [(i, i ^ masks[1 if i & self.plan.core else 0]) for i in range(self.plan.devices)]
            self.owned.append(
                self.line.send(outgoing[index - 1], pairs, f"sum_{self.name}_last_{index}")
            )

    def arrive(self):
        self.line.wait(self.low[-1], *self.owned)

    def result(self):
        before = self.line.last
        self.arrive()
        count = len(self.low)

        def add(*parts):
            summed = self.sum(0, 1, parts[:count]).astype(F32)
            for part in parts[count:]:
                summed = summed + part.astype(F32)
            return summed[0]

        result = self.line.run(add, *self.low, *self.owned)
        self.line.last = before
        return result


def one_hot(order):
    return (order[:, None] == jnp.arange(order.shape[0])[None, :]).astype(BF)


def to_blocks(order, parts):
    if order.shape[0] == BLOCKS:
        return parts
    width = parts[0].shape[-1]
    joined = jnp.concatenate(parts, 0).reshape(order.shape[0], -1)
    spread = lax.dot_general(
        one_hot(order), joined, (((0,), (0,)), ((), ())), preferred_element_type=BF
    ).reshape(4, BLOCKS // 4, -1, width)
    return [spread[i] for i in range(4)]


def from_blocks(order, parts):
    count = order.shape[0]
    if count == BLOCKS:
        return parts
    width = parts[0].shape[-1]
    joined = jnp.concatenate(parts, 0).reshape(count, -1)
    moved = jnp.dot(one_hot(order), joined, preferred_element_type=BF)
    moved = moved.reshape(4, count // 4, -1, width)
    return [moved[i] for i in range(4)]


def params(limit):
    return pltpu.CompilerParams(vmem_limit_bytes=limit << 20)


def rows_of(ref, number, rows):
    return ref.at[pl.ds(pl.multiple_of(number * rows, rows), rows), :]


def fetches(order_ref, part_refs, held_ref, sems, start=0, width=None):
    each, rows, _ = part_refs[0].shape
    width = held_ref.shape[1] if width is None else width
    copies = []
    for place in range(BLOCKS):
        source = part_refs[place // each].at[place % each, :, pl.ds(start, width)]
        number = order_ref[place]
        copies.append(
            pltpu.make_async_copy(source, rows_of(held_ref, number, rows), sems.at[number])
        )
    return copies


def norm_parts(values):
    centre = values - jnp.mean(values, axis=-1, keepdims=True)
    inverse = lax.rsqrt(jnp.mean(centre * centre, axis=-1, keepdims=True) + eps)
    return centre * inverse, inverse


def norm_back(grad_norm, normed, inverse):
    return inverse * (
        grad_norm
        - jnp.mean(grad_norm, axis=-1, keepdims=True)
        - normed * jnp.mean(grad_norm * normed, axis=-1, keepdims=True)
    )


def span(index, size):
    if isinstance(index, int):
        return pl.ds(index * size, size)
    return pl.ds(pl.multiple_of(index * size, size), size)


def each(count):
    def run(body):
        for index in range(count):
            body(index)

    return run


def dot(a, b):
    return jnp.dot(a, b, preferred_element_type=F32)


def dot_nt(a, b):
    return lax.dot_general(a, b, (((1,), (1,)), ((), ())), preferred_element_type=F32)


def dot_tn(a, b):
    return lax.dot_general(a, b, (((0,), (0,)), ((), ())), preferred_element_type=F32)


def stacked(values):
    head = lax.broadcasted_iota(jnp.int32, values.shape, 1) // HEAD_DIM
    zero = jnp.zeros_like(values)
    return jnp.concatenate([jnp.where(head == h, values, zero) for h in range(GROUP)], 0)


def unstacked(values):
    rows = values.shape[0] // GROUP
    head = lax.broadcasted_iota(jnp.int32, (rows, values.shape[1]), 1) // HEAD_DIM
    result = values[:rows]
    for h in range(1, GROUP):
        result = jnp.where(head == h, values[h * rows : (h + 1) * rows], result)
    return result


def project_kernel(
    order_ref, vec_ref, x_ref, w0, w1, w2, w3, entry_ref, project_ref, held, sems
):
    copies = fetches(order_ref, (w0, w1, w2, w3), held, sems)
    for copy in copies:
        copy.start()

    @each(x_ref.shape[0] // CHUNK)
    def _(i):
        normed, _ = norm_parts(x_ref[span(i, CHUNK), :].astype(F32))
        entry_ref[span(i, CHUNK), :] = (normed * vec_ref[0:1, :] + vec_ref[2:3, :]).astype(BF)

    for copy in copies:
        copy.wait()

    @each(3 * D // TILE)
    def _(i):
        third = i // (D // TILE)
        column = span(i % (D // TILE), TILE)
        part = dot(entry_ref[...], held[:, span(i, TILE)])
        if third != 1:
            part = part + vec_ref[pl.ds(3 if third == 0 else 4, 1), column]
        project_ref[:, span(i, TILE)] = part.astype(BF)


def project_all(order, vec, x, *first):
    count = x.shape[0]
    shape = jax.ShapeDtypeStruct
    return pl.pallas_call(
        project_kernel,
        out_shape=[shape((count, D), BF), shape((count, 3 * D), BF)],
        in_specs=[SMEM] + [VMEM] * 2 + [ANY] * 4,
        out_specs=[VMEM] * 2,
        scratch_shapes=[pltpu.VMEM((D, 3 * D), BF), pltpu.SemaphoreType.DMA((BLOCKS,))],
        compiler_params=params(32),
        name="project",
    )(order, vec, x, *first)


def attend_kernel(project_ref, idr_ref, idc_ref, probs_ref, mixed_ref, probs, out_sems):
    groups = D // WIDE
    copies = []

    @each((mixed_ref.shape[0] // SEQ) * groups)
    def _(i):
        row, group = i // groups, i % groups
        rows = span(row, SEQ)
        queries = project_ref[rows, span(group, WIDE)] * BF(HEAD_DIM**-0.5)
        keys = project_ref[rows, span(groups + group, WIDE)]
        values = project_ref[rows, span(2 * groups + group, WIDE)]
        scores = dot_nt(stacked(queries), keys)
        same = idc_ref[rows, :] == idr_ref[pl.ds(row, 1), :]
        scores = jnp.where(same[None], scores.reshape(GROUP, SEQ, SEQ), -1e9)
        expo = jnp.exp(scores - jnp.max(scores, axis=-1, keepdims=True))
        low = (expo / jnp.sum(expo, axis=-1, keepdims=True)).astype(BF)
        low = low.reshape(GROUP * SEQ, SEQ)
        probs[i] = low
        copy = pltpu.make_async_copy(probs.at[i], probs_ref.at[i], out_sems.at[i])
        copy.start()
        copies.append(copy)
        mixed_ref[rows, span(group, WIDE)] = unstacked(dot(low, values)).astype(BF)

    for copy in copies:
        copy.wait()


def attend(project, ids):
    count = project.shape[0]
    steps = (count // SEQ) * (D // WIDE)
    shape = jax.ShapeDtypeStruct
    return pl.pallas_call(
        attend_kernel,
        out_shape=[shape((steps, GROUP * SEQ, SEQ), BF), shape((count, D), BF)],
        in_specs=[VMEM] * 3,
        out_specs=[ANY, VMEM],
        scratch_shapes=[
            pltpu.VMEM((steps, GROUP * SEQ, SEQ), BF),
            pltpu.SemaphoreType.DMA((steps,)),
        ],
        compiler_params=params(32),
        name="attend",
    )(project, ids, ids.reshape(count, 1))


def piece(number):
    return pl.ds(pl.multiple_of(number * PIECE, PIECE), PIECE)


def settle_kernel(
    order_ref, vec_ref, x_ref, mixed_ref, w0, w1, w2, w3, middle_ref, second_ref, held, sems
):
    copies = fetches(order_ref, (w0, w1, w2, w3), held, sems, FF)
    for copy in copies:
        copy.start()
    for copy in copies:
        copy.wait()

    @each(D // TILE)
    def _(i):
        columns = span(i, TILE)
        branch = dot(mixed_ref[...], held[:, columns]) + vec_ref[5:6, columns]
        middle_ref[:, columns] = x_ref[:, columns].astype(F32) + branch

    @pl.loop(0, x_ref.shape[0] // CHUNK)
    def _(i):
        normed, _ = norm_parts(middle_ref[span(i, CHUNK), :])
        second_ref[span(i, CHUNK), :] = (normed * vec_ref[1:2, :] + vec_ref[6:7, :]).astype(BF)


def settle(order, vec, x, mixed, *win):
    count = x.shape[0]
    shape = jax.ShapeDtypeStruct
    return pl.pallas_call(
        settle_kernel,
        out_shape=[shape((count, D), F32), shape((count, D), BF)],
        in_specs=[SMEM] + [VMEM] * 3 + [ANY] * 4,
        out_specs=[VMEM] * 2,
        scratch_shapes=[pltpu.VMEM((D, D), BF), pltpu.SemaphoreType.DMA((BLOCKS,))],
        compiler_params=params(32),
        name="settle",
    )(order, vec, x, mixed, *win)


def rise_kernel(
    order_ref, bias_ref, second_ref, top_ref, w0, w1, w2, w3,
    active_ref, slope_ref, g0, g1, g2, g3,
    held, active, slope, grads, sems, tile_sems,
):
    copies = fetches(order_ref, (w0, w1, w2, w3), held, sems)
    for copy in copies:
        copy.start()
    for copy in copies:
        copy.wait()
    outs = []
    places = TILE // PIECE

    @each(FF // TILE)
    def _(step):
        columns = span(step, TILE)
        numbers = [order_ref[step * places + j] for j in range(places)]
        weight = jnp.concatenate([held[:, piece(number)] for number in numbers], 1)
        bias = jnp.concatenate([bias_ref[:, piece(number)] for number in numbers], 1)
        hidden = dot(second_ref[...], weight) + bias
        cdf = 0.5 + 0.5 * lax.erf(hidden * (0.5**0.5))
        grow = cdf + hidden * jnp.exp(-0.5 * hidden * hidden) * 0.3989422804014327
        low = (hidden * cdf).astype(BF)
        active[:, columns] = low
        slope[:, columns] = grow.astype(BF)
        grad = dot_tn(low, top_ref[...]).astype(BF)
        block = pl.ds(step * places, places)
        grads[block] = grad.reshape(places, PIECE, D)
        apiece = g0.shape[0]
        target = (g0, g1, g2, g3)[step * places // apiece]
        target = target.at[pl.ds(step * places % apiece, places)]
        for number, (source, target) in enumerate(
            (
                (active.at[:, columns], active_ref.at[:, columns]),
                (slope.at[:, columns], slope_ref.at[:, columns]),
                (grads.at[block], target),
            )
        ):
            copy = pltpu.make_async_copy(source, target, tile_sems.at[step, number])
            copy.start()
            outs.append(copy)

    for copy in outs:
        copy.wait()


def rise(order, bias, second, top, *win):
    count = second.shape[0]
    shape = jax.ShapeDtypeStruct
    grad = shape((BLOCKS // 4, PIECE, D), BF)
    return pl.pallas_call(
        rise_kernel,
        out_shape=[shape((count, FF), BF)] * 2 + [grad] * 4,
        in_specs=[SMEM] + [VMEM] * 3 + [ANY] * 4,
        out_specs=[ANY] * 6,
        scratch_shapes=[
            pltpu.VMEM((D, FF), BF),
            pltpu.VMEM((count, FF), BF),
            pltpu.VMEM((count, FF), BF),
            pltpu.VMEM((BLOCKS, PIECE, D), BF),
            pltpu.SemaphoreType.DMA((BLOCKS,)),
            pltpu.SemaphoreType.DMA((FF // TILE, 3)),
        ],
        compiler_params=params(48),
        name="rise",
    )(order, bias, second, top, *win)


def mlp_fetches(spot_ref, early_refs, late_refs, held_ref, sems):
    apiece, _, width = early_refs[0].shape
    early = [
        pltpu.make_async_copy(
            part, held_ref.at[pl.ds(i * apiece, apiece), :, pl.ds(0, width)], sems.at[BLOCKS + i]
        )
        for i, part in enumerate(early_refs)
    ]
    late = [
        pltpu.make_async_copy(
            late_refs[place // apiece].at[place % apiece],
            held_ref.at[spot_ref[place], :, pl.ds(width, width)],
            sems.at[spot_ref[place]],
        )
        for place in range(BLOCKS)
    ]
    return early, late


def start(copies):
    for copy in copies:
        copy.start()


def wait(copies):
    for copy in copies:
        copy.wait()


def block_rows(order_ref, ref, part, apiece, rows):
    return jnp.concatenate(
        [ref[span(order_ref[part * apiece + j], rows), :] for j in range(apiece)], 0
    )


def fall_kernel(
    order_ref, spot_ref, top_ref, slope_ref, second_ref,
    m0, m1, m2, m3, l0, l1, l2, l3,
    ghidden_ref, bias_ref, g0, g1, g2, g3,
    mheld, slope, ghidden, turned, grads, msems, tile_sems, out_sems,
):
    copies, late = mlp_fetches(spot_ref, (m0, m1, m2, m3), (l0, l1, l2, l3), mheld, msems)
    apiece, rows, _ = g0.shape
    places = TILE // PIECE
    slopes = [
        pltpu.make_async_copy(
            slope_ref.at[:, span(i, FF // 4)], slope.at[:, span(i, FF // 4)], tile_sems.at[i]
        )
        for i in range(4)
    ]
    for i in range(4):
        copies[i].start()
        slopes[i].start()
        if i == 0:
            for copy in late:
                copy.start()
    turned[...] = second_ref[...].T

    @each(FF // TILE)
    def _(step):
        part = step * places // apiece
        if step * places % apiece == 0:
            copies[part].wait()
            slopes[part].wait()
        for place in range(step * places, (step + 1) * places):
            pltpu.make_async_copy(
                l0.at[0], mheld.at[place, :, pl.ds(D // 2, D // 2)], msems.at[place]
            ).wait()
        weight = mheld[pl.ds(step * places, places)].reshape(TILE, D)
        grad_active = dot_nt(top_ref[...], weight)
        grad = grad_active * slope[:, span(step, TILE)].astype(F32)
        low = grad.astype(BF)
        sums = jnp.sum(low.astype(F32), axis=0, keepdims=True)
        for j in range(places):
            number = order_ref[step * places + j]
            ghidden[:, piece(number)] = low[:, j * PIECE : (j + 1) * PIECE]
            bias_ref[:, piece(number)] = sums[:, j * PIECE : (j + 1) * PIECE]

    outs = [pltpu.make_async_copy(ghidden, ghidden_ref, out_sems.at[4])]
    start(outs)
    for part in (3, 2, 1, 0):
        left = block_rows(order_ref, turned, part, apiece, rows)
        for i in range(FF // TILE):
            grad = dot(left, ghidden[:, span(i, TILE)]).astype(BF)
            grads[part, :, :, span(i, TILE)] = grad.reshape(apiece, rows, TILE)
        copy = pltpu.make_async_copy(grads.at[part], (g0, g1, g2, g3)[part], out_sems.at[part])
        copy.start()
        outs.append(copy)
    for copy in outs:
        copy.wait()


def fall(order, spot, top, slope, second, *mlp):
    count = second.shape[0]
    shape = jax.ShapeDtypeStruct
    grad = shape((BLOCKS // 4, D // BLOCKS, FF), BF)
    return pl.pallas_call(
        fall_kernel,
        out_shape=[shape((count, FF), BF), shape((1, FF), F32)] + [grad] * 4,
        in_specs=[SMEM, SMEM, VMEM, ANY, VMEM] + [ANY] * 8,
        out_specs=[HBM, VMEM] + [ANY] * 4,
        scratch_shapes=[
            pltpu.VMEM((BLOCKS, PIECE, D), BF),
            pltpu.VMEM((count, FF), BF),
            pltpu.VMEM((count, FF), BF),
            pltpu.VMEM((D, count), BF),
            pltpu.VMEM((4, *grad.shape), BF),
            pltpu.SemaphoreType.DMA((BLOCKS + 4,)),
            pltpu.SemaphoreType.DMA((4,)),
            pltpu.SemaphoreType.DMA((5,)),
        ],
        compiler_params=params(40),
        name="fall",
    )(order, spot, top, slope, second, *mlp)


def back_kernel(
    order_ref, vec_ref, ghidden_ref, top_ref, middle_ref, w0, w1, w2, w3,
    gmiddle_ref, branch_ref, sums_ref,
    held, ghidden, middle, gsecond, gmiddle, branch, sems, in_sems, out_sems,
):
    wide = FF // 2
    loads = [
        [
            pltpu.make_async_copy(
                ghidden_ref.at[:, span(k, wide)], ghidden.at[k], in_sems.at[k]
            ),
            *fetches(order_ref, (w0, w1, w2, w3), held.at[k], sems.at[k], k * wide, wide),
        ]
        for k in range(2)
    ]
    loads[1].append(pltpu.make_async_copy(middle_ref, middle, in_sems.at[2]))
    start(loads[0])
    start(loads[1])
    sums_ref[...] = jnp.zeros_like(sums_ref)
    outs = []
    wait(loads[0])
    for i in range(D // TILE):
        gsecond[:, span(i, TILE)] = dot_nt(ghidden[0], held[0, span(i, TILE), :])
    wait(loads[1])
    chunk = middle_ref.shape[0] // 2
    for half in range(2):
        where = span(half, chunk)
        for i in range(D // TILE):
            gsecond[where, span(i, TILE)] += dot_nt(ghidden[1, where, :], held[1, span(i, TILE), :])
        normed, inverse = norm_parts(middle[where, :])
        grad = gsecond[where, :]
        top = top_ref[where, :].astype(F32)
        total_grad = top + norm_back(grad * vec_ref[1:2, :], normed, inverse)
        gmiddle[where, :] = total_grad
        copy = pltpu.make_async_copy(
            gmiddle.at[where, :], gmiddle_ref.at[where, :], out_sems.at[half]
        )
        copy.start()
        outs.append(copy)
        branch[where, :] = total_grad.astype(BF)
        low = total_grad.astype(BF).astype(F32)
        for row, value in enumerate((grad * normed, grad, low, top)):
            sums_ref[row : row + 1, :] += jnp.sum(value, axis=0, keepdims=True)
    outs.append(pltpu.make_async_copy(branch, branch_ref, out_sems.at[2]))
    outs[-1].start()
    wait(outs)


def back(order, vec, ghidden, top, middle, *win):
    count = middle.shape[0]
    shape = jax.ShapeDtypeStruct
    return pl.pallas_call(
        back_kernel,
        out_shape=[shape((count, D), F32), shape((count, D), BF), shape((8, D), F32)],
        in_specs=[SMEM, VMEM, HBM, VMEM, HBM] + [ANY] * 4,
        out_specs=[HBM, HBM, VMEM],
        scratch_shapes=[
            pltpu.VMEM((2, D, FF // 2), BF),
            pltpu.VMEM((2, count, FF // 2), BF),
            pltpu.VMEM((count, D), F32),
            pltpu.VMEM((count, D), F32),
            pltpu.VMEM((count, D), F32),
            pltpu.VMEM((count, D), BF),
            pltpu.SemaphoreType.DMA((2, BLOCKS)),
            pltpu.SemaphoreType.DMA((3,)),
            pltpu.SemaphoreType.DMA((3,)),
        ],
        compiler_params=params(52),
        name="back",
    )(order, vec, ghidden, top, middle, *win)


def unattend_kernel(
    order_ref, vec_ref, x_ref, gmiddle_ref, branch_ref, project_ref, probs_ref, entry_ref, mixed_ref,
    w0, w1, w2, w3, f0, f1, f2, f3,
    ginputs_ref, sums_ref, g0, g1, g2, g3,
    oheld, held, project, probs, both, turned, gmiddle, branch, gmixed, gproject, gentry, ginputs, grads,
    osems, sems, in_sems, probs_sems, out_sems,
):
    count = x_ref.shape[0]
    groups = D // WIDE
    ocopies = fetches(order_ref, (w0, w1, w2, w3), oheld, osems, FF)
    load = [
        pltpu.make_async_copy(project_ref, project, in_sems.at[0]),
        pltpu.make_async_copy(entry_ref, both.at[0], in_sems.at[1]),
        pltpu.make_async_copy(mixed_ref, both.at[1], in_sems.at[2]),
        pltpu.make_async_copy(branch_ref, branch, in_sems.at[3]),
        pltpu.make_async_copy(gmiddle_ref, gmiddle, in_sems.at[4]),
    ]
    pieces = [
        pltpu.make_async_copy(probs_ref.at[i], probs.at[i], probs_sems.at[i])
        for i in range((count // SEQ) * groups)
    ]
    copies = fetches(order_ref, (f0, f1, f2, f3), held, sems)
    start([load[2], load[3], *ocopies])
    sums_ref[...] = jnp.zeros_like(sums_ref)
    apiece, rows, _ = g0.shape
    load[2].wait()
    start([load[0]])
    turned[1] = both[1].T
    load[3].wait()
    for part in (3, 2, 1, 0):
        left = block_rows(order_ref, turned.at[1], part, apiece, rows)
        for i in range(D // TILE):
            grad = dot(left, branch[:, span(i, TILE)]).astype(BF)
            grads[part, :, :, span(3 * D // TILE + i, TILE)] = grad.reshape(apiece, rows, TILE)
    wait(ocopies)
    start(pieces[:2])

    @each(D // TILE)
    def _(i):
        gmixed[:, span(i, TILE)] = dot_nt(branch[...], oheld[span(i, TILE), :]).astype(BF)

    load[0].wait()

    @each((count // SEQ) * groups)
    def _(i):
        row, group = i // groups, i % groups
        where = span(row, SEQ)
        scale = HEAD_DIM**-0.5
        pieces[i].wait()
        if i % 2 == 0:
            start(pieces[i + 2 : i + 4] if i + 2 < len(pieces) else [load[1], load[4], *copies])
        queries = stacked(project[where, span(group, WIDE)] * BF(scale))
        keys = project[where, span(groups + group, WIDE)]
        values = project[where, span(2 * groups + group, WIDE)]
        gmix = stacked(gmixed[where, span(group, WIDE)])
        low = probs[i]
        gprobs = dot_nt(gmix, values)
        gvalues = dot_tn(low, gmix)
        weight = low.astype(F32)
        inner = jnp.sum(weight * gprobs, axis=-1, keepdims=True)
        gscores = (weight * (gprobs - inner)).astype(BF)
        gqueries = unstacked(dot(gscores, keys)) * scale
        gkeys = dot_tn(gscores, queries)
        for third, grad in enumerate((gqueries, gkeys, gvalues)):
            low = grad.astype(BF)
            gproject[where, span(third * groups + group, WIDE)] = low
            sums_ref[third : third + 1, span(group, WIDE)] += jnp.sum(
                low.astype(F32), axis=0, keepdims=True
            )

    load[1].wait()
    turned[0] = both[0].T
    outs = []
    for part in (3, 2, 1, 0):
        left = block_rows(order_ref, turned.at[0], part, apiece, rows)
        for i in range(3 * D // TILE):
            grad = dot(left, gproject[:, span(i, TILE)]).astype(BF)
            grads[part, :, :, span(i, TILE)] = grad.reshape(apiece, rows, TILE)
        copy = pltpu.make_async_copy(grads.at[part], (g0, g1, g2, g3)[part], out_sems.at[part])
        copy.start()
        outs.append(copy)
    wait(copies)
    load[4].wait()
    chunk = count // 2
    for half in range(2):
        where = span(half, chunk)
        for i in range(D // TILE):
            gentry[where, span(i, TILE)] = dot_nt(gproject[where, :], held[span(i, TILE), :])
        normed, inverse = norm_parts(x_ref[where, :].astype(F32))
        grad = gentry[where, :]
        back = norm_back(grad * vec_ref[0:1, :], normed, inverse)
        ginputs[where, :] = gmiddle[where, :] + back
        copy = pltpu.make_async_copy(
            ginputs.at[where, :], ginputs_ref.at[where, :], out_sems.at[4 + half]
        )
        copy.start()
        outs.append(copy)
        sums_ref[3:4, :] += jnp.sum(grad * normed, axis=0, keepdims=True)
        sums_ref[4:5, :] += jnp.sum(grad, axis=0, keepdims=True)
    for copy in outs:
        copy.wait()


def unattend(order, vec, x, gmiddle, branch, project, probs, entry, mixed, win, first):
    count = gmiddle.shape[0]
    shape = jax.ShapeDtypeStruct
    grad = shape((BLOCKS // 4, D // BLOCKS, 4 * D), BF)
    return pl.pallas_call(
        unattend_kernel,
        out_shape=[shape((count, D), F32), shape((8, D), F32)] + [grad] * 4,
        in_specs=[SMEM] + [VMEM] * 2 + [HBM] * 6 + [ANY] * 8,
        out_specs=[ANY, VMEM] + [ANY] * 4,
        scratch_shapes=[
            pltpu.VMEM((D, D), BF),
            pltpu.VMEM((D, 3 * D), BF),
            pltpu.VMEM((count, 3 * D), BF),
            pltpu.VMEM(probs.shape, BF),
            pltpu.VMEM((2, count, D), BF),
            pltpu.VMEM((2, D, count), BF),
            pltpu.VMEM((count, D), F32),
            pltpu.VMEM((count, D), BF),
            pltpu.VMEM((count, D), BF),
            pltpu.VMEM((count, 3 * D), BF),
            pltpu.VMEM((count, D), F32),
            pltpu.VMEM((count, D), F32),
            pltpu.VMEM((4, *grad.shape), BF),
            pltpu.SemaphoreType.DMA((BLOCKS,)),
            pltpu.SemaphoreType.DMA((BLOCKS,)),
            pltpu.SemaphoreType.DMA((5,)),
            pltpu.SemaphoreType.DMA((probs.shape[0],)),
            pltpu.SemaphoreType.DMA((6,)),
        ],
        compiler_params=params(56),
        name="unattend",
    )(order, vec, x, gmiddle, branch, project, probs, entry, mixed, *win, *first)


def finish_kernel(
    spot_ref, vec_ref, middle_ref, active_ref, m0, m1, m2, m3, l0, l1, l2, l3,
    out_ref, held, active, sems, tile_sems,
):
    copies = [
        pltpu.make_async_copy(
            active_ref.at[:, span(half, FF // 2)], active.at[half], tile_sems.at[half]
        )
        for half in range(2)
    ]
    early, late = mlp_fetches(spot_ref, (m0, m1, m2, m3), (l0, l1, l2, l3), held, sems)
    fetch = early + late
    for copy in fetch + copies:
        copy.start()
    for copy in fetch + copies:
        copy.wait()

    @each(D // WIDE)
    def _(i):
        columns = span(i, WIDE)
        weight = held[:, :, columns].reshape(FF, WIDE)
        result = dot(active[0], weight[: FF // 2])
        result = result + dot(active[1], weight[FF // 2 :]) + vec_ref[7:8, columns]
        out_ref[:, columns] = (middle_ref[:, columns] + result).astype(BF)


def finish(spot, vec, middle, active, *mlp):
    count = middle.shape[0]
    return pl.pallas_call(
        finish_kernel,
        out_shape=jax.ShapeDtypeStruct((count, D), BF),
        in_specs=[SMEM, VMEM, VMEM, ANY] + [ANY] * 8,
        out_specs=VMEM,
        scratch_shapes=[
            pltpu.VMEM((BLOCKS, PIECE, D), BF),
            pltpu.VMEM((2, count, FF // 2), BF),
            pltpu.SemaphoreType.DMA((BLOCKS + 4,)),
            pltpu.SemaphoreType.DMA((2,)),
        ],
        compiler_params=params(32),
        name="finish",
    )(spot, vec, middle, active, *mlp)


def per_device(plan, late_plan, inputs, image_ids, cotangent, gains, biases, w_qkv, w_out, w_in, w_mlp):
    me = lax.axis_index(AXES)
    order = plan.positions(me)
    gain_dev, bias_dev = gains.shape[1], biases.shape[1]
    small_dev = gain_dev + bias_dev
    rows = D // plan.devices
    blocks, length = image_ids.shape
    count = blocks * length
    x = inputs.reshape(count, D)
    numbers = order if plan.devices == BLOCKS else jnp.arange(BLOCKS, dtype=jnp.int32)
    late_order = late_plan.positions(me)
    spot = jnp.arange(BLOCKS, dtype=jnp.int32)
    if plan.devices == BLOCKS:
        spot = jnp.sum(jnp.where(late_order[:, None] == order[None], spot[None], 0), axis=1)
    line = Line()
    side = 128

    small = jnp.concatenate([gains, biases], 1)
    small = jnp.pad(small, ((0, 0), (0, rows * side - small_dev))).reshape(rows, side)
    first = Gather(plan, line, "qkv", jnp.concatenate([w_qkv.reshape(rows, 3 * D), small], 1))
    win = Gather(
        plan, line, "in", jnp.concatenate([w_in.reshape(rows, FF), w_out.reshape(rows, D)], 1)
    )
    mlp_block = w_mlp.reshape(FF // plan.devices, D)
    mlp = Gather(plan, line, "mlp", mlp_block[:, : D // 2])
    late = Gather(late_plan, line, "late", mlp_block[:, D // 2 :])
    top = jnp.where(image_ids.reshape(count, 1) >= 0, cotangent.reshape(count, D), BF(0))
    first.start(0)
    late.start(0)
    first.take()
    late.take()
    first.start(1)
    win.start(0)
    late.start(1)
    first.take()
    win.take()
    late.take()
    first.start(2)
    first.take()
    first.start(3)
    first.swap_first()
    win.start(1)
    first.arrive()
    win.take()
    first.swap_second()
    win.start(2)
    mlp.start(0)
    first_parts = first.parts()

    def unpack(*parts):
        placed = jnp.concatenate([part[:, :, 3 * D :] for part in parts], 0)
        placed = placed.reshape(-1, rows * side)[:, :small_dev]
        spread = lax.dot_general(
            one_hot(order), placed, (((0,), (0,)), ((), ())), preferred_element_type=F32
        )
        return jnp.concatenate(
            [spread[:, :gain_dev].reshape(-1), spread[:, gain_dev:].reshape(-1)]
        ).reshape(-1, D)

    vec = line.run(unpack, *first_parts)
    line.wait(*first_parts)
    bias_in = vec[8:12].reshape(1, FF)
    vec = vec[:8]
    if plan.devices != BLOCKS:
        first_parts = [part[:, :, : 3 * D] for part in first_parts]
    first_parts = to_blocks(order, first_parts)
    entry, project = line.run(project_all, numbers, vec, x, *first_parts)
    line.wait(mlp.coming)
    win.take()
    win.start(3)
    win.swap_first()
    mlp.take()
    mlp.start(1)
    late.start(2)
    probs, mixed = line.run(attend, project, image_ids)
    line.wait(mlp.coming, late.coming)
    win.arrive()
    line.wait(win.first)
    win.swap_second()
    mlp.take()
    mlp.start(2)
    win_parts = to_blocks(order, win.parts())
    middle, second = line.run(settle, numbers, vec, x, mixed, *win_parts)
    line.wait(mlp.coming)
    late.take()
    late.start(3)
    late.swap_first()
    mlp.take()
    mlp.start(3)
    mlp.swap_first()
    active, slope, *grads = line.run(rise, numbers, bias_in, second, top, *win_parts)
    line.wait(mlp.first, late.first)
    mlp.arrive()
    late.arrive()
    sum_mlp = Scatter(plan, line, "mlp", from_blocks(order, grads))
    mlp.swap_second()
    late.swap_second()
    sum_mlp.start(3)
    mlp_parts = to_blocks(order, mlp.parts()) + to_blocks(late_order, late.parts())
    ghidden, grad_bias_in, *grads = line.run(fall, numbers, spot, top, slope, second, *mlp_parts)
    sum_in = Scatter(plan, line, "in", from_blocks(order, grads))
    gmiddle, branch, sums = line.run(back, numbers, vec, ghidden, top, middle, *win_parts)
    line.wait(sum_in.high[-1])
    sum_mlp.arrive()
    sum_in.start(3)
    sum_mlp.start(2)
    grad_inputs, sums_one, *grads = line.run(
        unattend, numbers, vec, x, gmiddle, branch, project, probs, entry, mixed, win_parts, first_parts
    )
    sum_mlp.arrive()
    sum_in.arrive()
    sum_first = Scatter(plan, line, "first", from_blocks(order, grads))

    def pack(sums_one, sums, grad_bias_in):
        flat_gains = jnp.concatenate([sums_one[3], sums[0]]).reshape(-1, gain_dev)
        flat_biases = jnp.concatenate(
            [sums_one[4], sums_one[0], sums_one[2], sums[2], sums[1], sums[3], grad_bias_in[0]]
        ).reshape(-1, bias_dev)
        flat_small = jnp.concatenate([flat_gains, flat_biases], 1).astype(BF)
        moved = jnp.dot(one_hot(order), flat_small, preferred_element_type=F32).astype(BF)
        moved = jnp.pad(moved, ((0, 0), (0, rows * side - small_dev)))
        return moved.reshape(plan.devices, rows, side)

    sum_first.join(pack(sums_one, sums, grad_bias_in))
    sum_in.start(2)
    sum_first.start(3)
    sum_mlp.start(1)
    output = line.run(finish, spot, vec, middle, active, *mlp_parts)
    sum_mlp.arrive()
    sum_in.start(1)
    sum_mlp.start(0)
    sum_in.arrive()
    sum_mlp.arrive()
    sum_first.start(2)
    sum_in.start(0)
    grad_mlp = sum_mlp.result()
    sum_in.arrive()
    sum_first.last()
    grad_in = sum_in.result()
    grad_first = sum_first.result()
    grad_small = grad_first[:, 4 * D :].reshape(1, -1)[:, :small_dev]
    return (
        output.reshape(blocks, length, D),
        grad_inputs.reshape(blocks, length, D),
        grad_small[:, :gain_dev],
        grad_small[:, gain_dev:],
        grad_first[:, : 3 * D].reshape(1, -1),
        grad_first[:, 3 * D : 4 * D].reshape(1, -1),
        grad_in.reshape(1, -1),
        grad_mlp.reshape(1, -1),
    )


def solution(mesh):
    plan, late_plan = Plan(mesh), Plan(mesh, late=True)
    whole = P(AXES, None, None)
    flat = P(AXES, None)

    def body(*arrays):
        return per_device(plan, late_plan, *arrays)

    return jax.shard_map(
        body,
        mesh=mesh,
        in_specs=(whole, flat, whole, flat, flat, flat, flat, flat, flat),
        out_specs=(whole, whole, flat, flat, flat, flat, flat, flat),
        check_vma=False,
    )
```

```python
import jax
import jax.numpy as jnp
from jax import lax
from jax.experimental import pallas as pl
from jax.experimental.pallas import tpu as pltpu
from jax.sharding import PartitionSpec as P

D = 1024
FF = 4096
HEADS = 16
HEAD_DIM = 64
SEQ = 256
AXES = ("dp", "fsdp")
BLOCKS = 32
GROUP = 4
WIDE = GROUP * HEAD_DIM
TILE = 512
CHUNK = 128
PIECE = FF // BLOCKS
BF = jnp.bfloat16
F32 = jnp.float32

eps = 1e-06
ANY = pl.BlockSpec(memory_space=pl.ANY)
HBM = pl.BlockSpec(memory_space=pltpu.HBM)
VMEM = pl.BlockSpec(memory_space=pltpu.VMEM)
SMEM = pl.BlockSpec(memory_space=pltpu.SMEM)


class Plan:
    def __init__(self, mesh, late=False):
        outer, inner = mesh.shape["dp"], mesh.shape["fsdp"]
        ys = outer // 2
        xs = min(ys, inner)
        zs = inner // xs
        self.devices = outer * inner
        self.half = self.devices // 2

        def bits(size, unit):
            found = []
            while size > 1:
                size //= 2
                found.append(size * unit)
            return found

        xbits = bits(xs, 1)
        zbits = bits(zs, xs)
        self.core = inner
        ybits = bits(ys, 2 * inner)
        self.late = late
        z_legs, xy_legs = [1, len(zbits) - 1], [len(xbits)] * 2
        if late:
            self.orders = (xbits + ybits + zbits, ybits + xbits + zbits)
            lengths = xy_legs + z_legs
        else:
            self.orders = (zbits + xbits + ybits, zbits + ybits + xbits)
            lengths = z_legs + xy_legs
        self.legs = []
        for length in lengths:
            start = self.legs[-1][-1] + 1 if self.legs else 0
            self.legs.append(list(range(start, start + length)))

    def pairs(self, stage):
        return [
            (i, i ^ self.orders[1 if i & self.core else 0][stage]) for i in range(self.devices)
        ]

    def core_pairs(self):
        return [(i, i ^ self.core) for i in range(self.devices)]

    def masks(self, which):
        found = [0]
        for bit in self.orders[which]:
            found = found + [mask ^ bit for mask in found]
        return found

    def positions(self, me):
        tables = jnp.array(
            [
                self.masks(0) + [mask ^ self.core for mask in self.masks(1)],
                self.masks(1) + [mask ^ self.core for mask in self.masks(0)],
            ],
            jnp.int32,
        )
        mine = jnp.where((me & self.core) > 0, tables[1], tables[0])
        return mine ^ me


class Line:
    def __init__(self):
        self.last = []

    def tie(self, *arrays):
        if not self.last:
            return arrays
        tied = lax.optimization_barrier((arrays, tuple(self.last)))
        return tied[0]

    def run(self, step, *arrays):
        result = step(*self.tie(*arrays))
        self.last = [result[0] if isinstance(result, (list, tuple)) else result]
        return result

    def send(self, array, pairs, name="swap"):
        with jax.named_scope(name):
            return lax.ppermute(self.tie(array)[0], AXES, pairs)

    def wait(self, *arrays):
        self.last.extend(arrays)


class Gather:
    def __init__(self, plan, line, name, block):
        self.plan, self.line, self.name = plan, line, name
        self.held = block[None]
        self.coming = None

    def take(self):
        self.line.wait(self.coming)
        self.held = self.line.run(
            lambda held, coming: jnp.concatenate([held, coming], 0), self.held, self.coming
        )

    def start(self, leg):
        for stage in self.plan.legs[leg]:
            if stage != self.plan.legs[leg][0]:
                self.take()
            self.coming = self.line.send(
                self.held, self.plan.pairs(stage), f"gather_{self.name}_{stage}"
            )

    def swap_first(self):
        self.first = self.line.send(
            self.held, self.plan.core_pairs(), f"gather_{self.name}_swap_first"
        )

    def arrive(self):
        self.line.wait(self.coming)

    def swap_second(self):
        self.second = self.line.send(
            self.coming, self.plan.core_pairs(), f"gather_{self.name}_swap_second"
        )

    def parts(self):
        self.line.wait(self.first, self.second)
        return [self.held, self.coming, self.first, self.second]


def total(parts):
    if len(parts) == 2:
        return parts[0] + parts[1]
    result = parts[0].astype(F32)
    for part in parts[1:]:
        result = result + part.astype(F32)
    return result


class Scatter:
    def __init__(self, plan, line, name, parts):
        self.plan, self.line, self.name = plan, line, name
        keep_low, keep_high, send_low, send_high = parts
        self.high = [keep_high, line.send(send_high, plan.core_pairs(), f"sum_{name}_swap_high")]
        self.low = [keep_low, line.send(send_low, plan.core_pairs(), f"sum_{name}_swap_low")]
        self.side = []
        self.count = keep_low.shape[0]
        self.width = keep_low.shape[-1]
        self.owned = []

    def join(self, parts):
        half = self.plan.half
        self.side = [
            parts[:half],
            self.line.send(parts[half:], self.plan.core_pairs(), f"sum_{self.name}_swap_side"),
        ]

    def sum(self, low, high, parts):
        wide = total([part[low:high, :, : self.width] for part in parts])
        if not self.side:
            return wide
        offset = low if self.high is None else low + self.count
        narrow = [part[low:high, :, self.width :] for part in parts[2:]]
        narrow += [part[offset : offset + high - low] for part in self.side]
        return jnp.concatenate([wide, total(narrow)], -1)

    def start(self, leg):
        for stage in reversed(self.plan.legs[leg]):
            if self.high is not None:
                parts, low = self.high, 0
            else:
                self.count //= 2
                parts, low = self.low, self.count
            self.line.wait(parts[-1], *self.side)
            outgoing = self.line.run(
                lambda *parts: self.sum(low, low + self.count, parts).astype(BF), *parts
            )
            self.high = None
            self.low.append(
                self.line.send(outgoing, self.plan.pairs(stage), f"sum_{self.name}_{stage}")
            )

    def last(self):
        self.line.wait(self.low[-1])
        stages = self.plan.legs[0] + self.plan.legs[1]
        outgoing = self.line.run(
            lambda *parts: [
                self.sum(index, index + 1, parts).astype(BF) for index in range(1, self.count)
            ],
            *self.low,
        )
        for index in range(1, self.count):
            masks = [0, 0]
            for bit, stage in enumerate(stages):
                if index >> bit & 1:
                    masks = [mask ^ order[stage] for mask, order in zip(masks, self.plan.orders)]
            pairs = [(i, i ^ masks[1 if i & self.plan.core else 0]) for i in range(self.plan.devices)]
            self.owned.append(
                self.line.send(outgoing[index - 1], pairs, f"sum_{self.name}_last_{index}")
            )

    def arrive(self):
        self.line.wait(self.low[-1], *self.owned)

    def result(self):
        before = self.line.last
        self.arrive()
        count = len(self.low)

        def add(*parts):
            summed = self.sum(0, 1, parts[:count]).astype(F32)
            for part in parts[count:]:
                summed = summed + part.astype(F32)
            return summed[0]

        result = self.line.run(add, *self.low, *self.owned)
        self.line.last = before
        return result


def one_hot(order):
    return (order[:, None] == jnp.arange(order.shape[0])[None, :]).astype(BF)


def to_blocks(order, parts):
    if order.shape[0] == BLOCKS:
        return parts
    width = parts[0].shape[-1]
    joined = jnp.concatenate(parts, 0).reshape(order.shape[0], -1)
    spread = lax.dot_general(
        one_hot(order), joined, (((0,), (0,)), ((), ())), preferred_element_type=BF
    ).reshape(4, BLOCKS // 4, -1, width)
    return [spread[i] for i in range(4)]


def from_blocks(order, parts):
    count = order.shape[0]
    if count == BLOCKS:
        return parts
    width = parts[0].shape[-1]
    joined = jnp.concatenate(parts, 0).reshape(count, -1)
    moved = jnp.dot(one_hot(order), joined, preferred_element_type=BF)
    moved = moved.reshape(4, count // 4, -1, width)
    return [moved[i] for i in range(4)]


def params(limit):
    return pltpu.CompilerParams(vmem_limit_bytes=limit << 20)


def rows_of(ref, number, rows):
    return ref.at[pl.ds(pl.multiple_of(number * rows, rows), rows), :]


def fetches(order_ref, part_refs, held_ref, sems, start=0, width=None):
    each, rows, _ = part_refs[0].shape
    width = held_ref.shape[1] if width is None else width
    copies = []
    for place in range(BLOCKS):
        source = part_refs[place // each].at[place % each, :, pl.ds(start, width)]
        number = order_ref[place]
        copies.append(
            pltpu.make_async_copy(source, rows_of(held_ref, number, rows), sems.at[number])
        )
    return copies


def norm_parts(values):
    centre = values - jnp.mean(values, axis=-1, keepdims=True)
    inverse = lax.rsqrt(jnp.mean(centre * centre, axis=-1, keepdims=True) + eps)
    return centre * inverse, inverse


def norm_back(grad_norm, normed, inverse):
    return inverse * (
        grad_norm
        - jnp.mean(grad_norm, axis=-1, keepdims=True)
        - normed * jnp.mean(grad_norm * normed, axis=-1, keepdims=True)
    )


def span(index, size):
    if isinstance(index, int):
        return pl.ds(index * size, size)
    return pl.ds(pl.multiple_of(index * size, size), size)


def each(count):
    def run(body):
        for index in range(count):
            body(index)

    return run


def dot(a, b):
    return jnp.dot(a, b, preferred_element_type=F32)


def dot_nt(a, b):
    return lax.dot_general(a, b, (((1,), (1,)), ((), ())), preferred_element_type=F32)


def dot_tn(a, b):
    return lax.dot_general(a, b, (((0,), (0,)), ((), ())), preferred_element_type=F32)


def stacked(values):
    head = lax.broadcasted_iota(jnp.int32, values.shape, 1) // HEAD_DIM
    zero = jnp.zeros_like(values)
    return jnp.concatenate([jnp.where(head == h, values, zero) for h in range(GROUP)], 0)


def unstacked(values):
    rows = values.shape[0] // GROUP
    head = lax.broadcasted_iota(jnp.int32, (rows, values.shape[1]), 1) // HEAD_DIM
    result = values[:rows]
    for h in range(1, GROUP):
        result = jnp.where(head == h, values[h * rows : (h + 1) * rows], result)
    return result


def project_kernel(
    order_ref, vec_ref, x_ref, w0, w1, w2, w3, entry_ref, project_ref, held, sems
):
    copies = fetches(order_ref, (w0, w1, w2, w3), held, sems)
    for copy in copies:
        copy.start()

    @each(x_ref.shape[0] // CHUNK)
    def _(i):
        normed, _ = norm_parts(x_ref[span(i, CHUNK), :].astype(F32))
        entry_ref[span(i, CHUNK), :] = (normed * vec_ref[0:1, :] + vec_ref[2:3, :]).astype(BF)

    for copy in copies:
        copy.wait()

    @each(3 * D // TILE)
    def _(i):
        third = i // (D // TILE)
        column = span(i % (D // TILE), TILE)
        part = dot(entry_ref[...], held[:, span(i, TILE)])
        if third != 1:
            part = part + vec_ref[pl.ds(3 if third == 0 else 4, 1), column]
        project_ref[:, span(i, TILE)] = part.astype(BF)


def project_all(order, vec, x, *first):
    count = x.shape[0]
    shape = jax.ShapeDtypeStruct
    return pl.pallas_call(
        project_kernel,
        out_shape=[shape((count, D), BF), shape((count, 3 * D), BF)],
        in_specs=[SMEM] + [VMEM] * 2 + [ANY] * 4,
        out_specs=[VMEM] * 2,
        scratch_shapes=[pltpu.VMEM((D, 3 * D), BF), pltpu.SemaphoreType.DMA((BLOCKS,))],
        compiler_params=params(32),
        name="project",
    )(order, vec, x, *first)


def attend_kernel(project_ref, idr_ref, idc_ref, probs_ref, mixed_ref, probs, out_sems):
    groups = D // WIDE
    copies = []

    @each((mixed_ref.shape[0] // SEQ) * groups)
    def _(i):
        row, group = i // groups, i % groups
        rows = span(row, SEQ)
        queries = project_ref[rows, span(group, WIDE)] * BF(HEAD_DIM**-0.5)
        keys = project_ref[rows, span(groups + group, WIDE)]
        values = project_ref[rows, span(2 * groups + group, WIDE)]
        scores = dot_nt(stacked(queries), keys)
        same = idc_ref[rows, :] == idr_ref[pl.ds(row, 1), :]
        scores = jnp.where(same[None], scores.reshape(GROUP, SEQ, SEQ), -1e9)
        expo = jnp.exp(scores - jnp.max(scores, axis=-1, keepdims=True))
        low = (expo / jnp.sum(expo, axis=-1, keepdims=True)).astype(BF)
        low = low.reshape(GROUP * SEQ, SEQ)
        probs[i] = low
        copy = pltpu.make_async_copy(probs.at[i], probs_ref.at[i], out_sems.at[i])
        copy.start()
        copies.append(copy)
        mixed_ref[rows, span(group, WIDE)] = unstacked(dot(low, values)).astype(BF)

    for copy in copies:
        copy.wait()


def attend(project, ids):
    count = project.shape[0]
    steps = (count // SEQ) * (D // WIDE)
    shape = jax.ShapeDtypeStruct
    return pl.pallas_call(
        attend_kernel,
        out_shape=[shape((steps, GROUP * SEQ, SEQ), BF), shape((count, D), BF)],
        in_specs=[VMEM] * 3,
        out_specs=[ANY, VMEM],
        scratch_shapes=[
            pltpu.VMEM((steps, GROUP * SEQ, SEQ), BF),
            pltpu.SemaphoreType.DMA((steps,)),
        ],
        compiler_params=params(32),
        name="attend",
    )(project, ids, ids.reshape(count, 1))


def piece(number):
    return pl.ds(pl.multiple_of(number * PIECE, PIECE), PIECE)


def settle_kernel(
    order_ref, vec_ref, x_ref, mixed_ref, w0, w1, w2, w3, middle_ref, second_ref, held, sems
):
    copies = fetches(order_ref, (w0, w1, w2, w3), held, sems, FF)
    for copy in copies:
        copy.start()
    for copy in copies:
        copy.wait()

    @each(D // TILE)
    def _(i):
        columns = span(i, TILE)
        branch = dot(mixed_ref[...], held[:, columns]) + vec_ref[5:6, columns]
        middle_ref[:, columns] = x_ref[:, columns].astype(F32) + branch

    @pl.loop(0, x_ref.shape[0] // CHUNK)
    def _(i):
        normed, _ = norm_parts(middle_ref[span(i, CHUNK), :])
        second_ref[span(i, CHUNK), :] = (normed * vec_ref[1:2, :] + vec_ref[6:7, :]).astype(BF)


def settle(order, vec, x, mixed, *win):
    count = x.shape[0]
    shape = jax.ShapeDtypeStruct
    return pl.pallas_call(
        settle_kernel,
        out_shape=[shape((count, D), F32), shape((count, D), BF)],
        in_specs=[SMEM] + [VMEM] * 3 + [ANY] * 4,
        out_specs=[VMEM] * 2,
        scratch_shapes=[pltpu.VMEM((D, D), BF), pltpu.SemaphoreType.DMA((BLOCKS,))],
        compiler_params=params(32),
        name="settle",
    )(order, vec, x, mixed, *win)


def rise_kernel(
    order_ref, bias_ref, second_ref, top_ref, w0, w1, w2, w3,
    active_ref, slope_ref, g0, g1, g2, g3,
    held, active, slope, grads, sems, tile_sems,
):
    copies = fetches(order_ref, (w0, w1, w2, w3), held, sems)
    for copy in copies:
        copy.start()
    for copy in copies:
        copy.wait()
    outs = []
    places = TILE // PIECE

    @each(FF // TILE)
    def _(step):
        columns = span(step, TILE)
        numbers = [order_ref[step * places + j] for j in range(places)]
        weight = jnp.concatenate([held[:, piece(number)] for number in numbers], 1)
        bias = jnp.concatenate([bias_ref[:, piece(number)] for number in numbers], 1)
        hidden = dot(second_ref[...], weight) + bias
        cdf = 0.5 + 0.5 * lax.erf(hidden * (0.5**0.5))
        grow = cdf + hidden * jnp.exp(-0.5 * hidden * hidden) * 0.3989422804014327
        low = (hidden * cdf).astype(BF)
        active[:, columns] = low
        slope[:, columns] = grow.astype(BF)
        grad = dot_tn(low, top_ref[...]).astype(BF)
        block = pl.ds(step * places, places)
        grads[block] = grad.reshape(places, PIECE, D)
        apiece = g0.shape[0]
        target = (g0, g1, g2, g3)[step * places // apiece]
        target = target.at[pl.ds(step * places % apiece, places)]
        for number, (source, target) in enumerate(
            (
                (active.at[:, columns], active_ref.at[:, columns]),
                (slope.at[:, columns], slope_ref.at[:, columns]),
                (grads.at[block], target),
            )
        ):
            copy = pltpu.make_async_copy(source, target, tile_sems.at[step, number])
            copy.start()
            outs.append(copy)

    for copy in outs:
        copy.wait()


def rise(order, bias, second, top, *win):
    count = second.shape[0]
    shape = jax.ShapeDtypeStruct
    grad = shape((BLOCKS // 4, PIECE, D), BF)
    return pl.pallas_call(
        rise_kernel,
        out_shape=[shape((count, FF), BF)] * 2 + [grad] * 4,
        in_specs=[SMEM] + [VMEM] * 3 + [ANY] * 4,
        out_specs=[ANY] * 6,
        scratch_shapes=[
            pltpu.VMEM((D, FF), BF),
            pltpu.VMEM((count, FF), BF),
            pltpu.VMEM((count, FF), BF),
            pltpu.VMEM((BLOCKS, PIECE, D), BF),
            pltpu.SemaphoreType.DMA((BLOCKS,)),
            pltpu.SemaphoreType.DMA((FF // TILE, 3)),
        ],
        compiler_params=params(48),
        name="rise",
    )(order, bias, second, top, *win)


def mlp_fetches(spot_ref, early_refs, late_refs, held_ref, sems):
    apiece, _, width = early_refs[0].shape
    early = [
        pltpu.make_async_copy(
            part, held_ref.at[pl.ds(i * apiece, apiece), :, pl.ds(0, width)], sems.at[BLOCKS + i]
        )
        for i, part in enumerate(early_refs)
    ]
    late = [
        pltpu.make_async_copy(
            late_refs[place // apiece].at[place % apiece],
            held_ref.at[spot_ref[place], :, pl.ds(width, width)],
            sems.at[spot_ref[place]],
        )
        for place in range(BLOCKS)
    ]
    return early, late


def start(copies):
    for copy in copies:
        copy.start()


def wait(copies):
    for copy in copies:
        copy.wait()


def block_rows(order_ref, ref, part, apiece, rows):
    return jnp.concatenate(
        [ref[span(order_ref[part * apiece + j], rows), :] for j in range(apiece)], 0
    )


def fall_kernel(
    order_ref, spot_ref, top_ref, slope_ref, second_ref,
    m0, m1, m2, m3, l0, l1, l2, l3,
    ghidden_ref, bias_ref, g0, g1, g2, g3,
    mheld, slope, ghidden, turned, grads, msems, tile_sems, out_sems,
):
    copies, late = mlp_fetches(spot_ref, (m0, m1, m2, m3), (l0, l1, l2, l3), mheld, msems)
    apiece, rows, _ = g0.shape
    places = TILE // PIECE
    slopes = [
        pltpu.make_async_copy(
            slope_ref.at[:, span(i, FF // 4)], slope.at[:, span(i, FF // 4)], tile_sems.at[i]
        )
        for i in range(4)
    ]
    for i in range(4):
        copies[i].start()
        slopes[i].start()
        if i == 0:
            for copy in late:
                copy.start()
    turned[...] = second_ref[...].T

    @each(FF // TILE)
    def _(step):
        part = step * places // apiece
        if step * places % apiece == 0:
            copies[part].wait()
            slopes[part].wait()
        for place in range(step * places, (step + 1) * places):
            pltpu.make_async_copy(
                l0.at[0], mheld.at[place, :, pl.ds(D // 2, D // 2)], msems.at[place]
            ).wait()
        weight = mheld[pl.ds(step * places, places)].reshape(TILE, D)
        grad_active = dot_nt(top_ref[...], weight)
        grad = grad_active * slope[:, span(step, TILE)].astype(F32)
        low = grad.astype(BF)
        sums = jnp.sum(low.astype(F32), axis=0, keepdims=True)
        for j in range(places):
            number = order_ref[step * places + j]
            ghidden[:, piece(number)] = low[:, j * PIECE : (j + 1) * PIECE]
            bias_ref[:, piece(number)] = sums[:, j * PIECE : (j + 1) * PIECE]

    outs = [pltpu.make_async_copy(ghidden, ghidden_ref, out_sems.at[4])]
    start(outs)
    for part in (3, 2, 1, 0):
        left = block_rows(order_ref, turned, part, apiece, rows)
        for i in range(FF // TILE):
            grad = dot(left, ghidden[:, span(i, TILE)]).astype(BF)
            grads[part, :, :, span(i, TILE)] = grad.reshape(apiece, rows, TILE)
        copy = pltpu.make_async_copy(grads.at[part], (g0, g1, g2, g3)[part], out_sems.at[part])
        copy.start()
        outs.append(copy)
    for copy in outs:
        copy.wait()


def fall(order, spot, top, slope, second, *mlp):
    count = second.shape[0]
    shape = jax.ShapeDtypeStruct
    grad = shape((BLOCKS // 4, D // BLOCKS, FF), BF)
    return pl.pallas_call(
        fall_kernel,
        out_shape=[shape((count, FF), BF), shape((1, FF), F32)] + [grad] * 4,
        in_specs=[SMEM, SMEM, VMEM, ANY, VMEM] + [ANY] * 8,
        out_specs=[HBM, VMEM] + [ANY] * 4,
        scratch_shapes=[
            pltpu.VMEM((BLOCKS, PIECE, D), BF),
            pltpu.VMEM((count, FF), BF),
            pltpu.VMEM((count, FF), BF),
            pltpu.VMEM((D, count), BF),
            pltpu.VMEM((4, *grad.shape), BF),
            pltpu.SemaphoreType.DMA((BLOCKS + 4,)),
            pltpu.SemaphoreType.DMA((4,)),
            pltpu.SemaphoreType.DMA((5,)),
        ],
        compiler_params=params(40),
        name="fall",
    )(order, spot, top, slope, second, *mlp)


def back_kernel(
    order_ref, vec_ref, ghidden_ref, top_ref, middle_ref, w0, w1, w2, w3,
    gmiddle_ref, branch_ref, sums_ref,
    held, ghidden, middle, gsecond, gmiddle, branch, sems, in_sems, out_sems,
):
    wide = FF // 2
    loads = [
        [
            pltpu.make_async_copy(
                ghidden_ref.at[:, span(k, wide)], ghidden.at[k], in_sems.at[k]
            ),
            *fetches(order_ref, (w0, w1, w2, w3), held.at[k], sems.at[k], k * wide, wide),
        ]
        for k in range(2)
    ]
    loads[1].append(pltpu.make_async_copy(middle_ref, middle, in_sems.at[2]))
    start(loads[0])
    start(loads[1])
    sums_ref[...] = jnp.zeros_like(sums_ref)
    outs = []
    wait(loads[0])
    for i in range(D // TILE):
        gsecond[:, span(i, TILE)] = dot_nt(ghidden[0], held[0, span(i, TILE), :])
    wait(loads[1])
    chunk = middle_ref.shape[0] // 2
    for half in range(2):
        where = span(half, chunk)
        for i in range(D // TILE):
            gsecond[where, span(i, TILE)] += dot_nt(ghidden[1, where, :], held[1, span(i, TILE), :])
        normed, inverse = norm_parts(middle[where, :])
        grad = gsecond[where, :]
        top = top_ref[where, :].astype(F32)
        total_grad = top + norm_back(grad * vec_ref[1:2, :], normed, inverse)
        gmiddle[where, :] = total_grad
        copy = pltpu.make_async_copy(
            gmiddle.at[where, :], gmiddle_ref.at[where, :], out_sems.at[half]
        )
        copy.start()
        outs.append(copy)
        branch[where, :] = total_grad.astype(BF)
        low = total_grad.astype(BF).astype(F32)
        for row, value in enumerate((grad * normed, grad, low, top)):
            sums_ref[row : row + 1, :] += jnp.sum(value, axis=0, keepdims=True)
    outs.append(pltpu.make_async_copy(branch, branch_ref, out_sems.at[2]))
    outs[-1].start()
    wait(outs)


def back(order, vec, ghidden, top, middle, *win):
    count = middle.shape[0]
    shape = jax.ShapeDtypeStruct
    return pl.pallas_call(
        back_kernel,
        out_shape=[shape((count, D), F32), shape((count, D), BF), shape((8, D), F32)],
        in_specs=[SMEM, VMEM, HBM, VMEM, HBM] + [ANY] * 4,
        out_specs=[HBM, HBM, VMEM],
        scratch_shapes=[
            pltpu.VMEM((2, D, FF // 2), BF),
            pltpu.VMEM((2, count, FF // 2), BF),
            pltpu.VMEM((count, D), F32),
            pltpu.VMEM((count, D), F32),
            pltpu.VMEM((count, D), F32),
            pltpu.VMEM((count, D), BF),
            pltpu.SemaphoreType.DMA((2, BLOCKS)),
            pltpu.SemaphoreType.DMA((3,)),
            pltpu.SemaphoreType.DMA((3,)),
        ],
        compiler_params=params(52),
        name="back",
    )(order, vec, ghidden, top, middle, *win)


def unattend_kernel(
    order_ref, vec_ref, x_ref, gmiddle_ref, branch_ref, project_ref, probs_ref, entry_ref, mixed_ref,
    w0, w1, w2, w3, f0, f1, f2, f3,
    ginputs_ref, sums_ref, g0, g1, g2, g3,
    oheld, held, project, probs, both, turned, gmiddle, branch, gmixed, gproject, gentry, ginputs, grads,
    osems, sems, in_sems, probs_sems, out_sems,
):
    count = x_ref.shape[0]
    groups = D // WIDE
    ocopies = fetches(order_ref, (w0, w1, w2, w3), oheld, osems, FF)
    load = [
        pltpu.make_async_copy(project_ref, project, in_sems.at[0]),
        pltpu.make_async_copy(entry_ref, both.at[0], in_sems.at[1]),
        pltpu.make_async_copy(mixed_ref, both.at[1], in_sems.at[2]),
        pltpu.make_async_copy(branch_ref, branch, in_sems.at[3]),
        pltpu.make_async_copy(gmiddle_ref, gmiddle, in_sems.at[4]),
    ]
    pieces = [
        pltpu.make_async_copy(probs_ref.at[i], probs.at[i], probs_sems.at[i])
        for i in range((count // SEQ) * groups)
    ]
    copies = fetches(order_ref, (f0, f1, f2, f3), held, sems)
    start([load[2], load[3], *ocopies])
    sums_ref[...] = jnp.zeros_like(sums_ref)
    apiece, rows, _ = g0.shape
    load[2].wait()
    start([load[0]])
    turned[1] = both[1].T
    load[3].wait()
    for part in (3, 2, 1, 0):
        left = block_rows(order_ref, turned.at[1], part, apiece, rows)
        for i in range(D // TILE):
            grad = dot(left, branch[:, span(i, TILE)]).astype(BF)
            grads[part, :, :, span(3 * D // TILE + i, TILE)] = grad.reshape(apiece, rows, TILE)
    wait(ocopies)
    start(pieces[:2])

    @each(D // TILE)
    def _(i):
        gmixed[:, span(i, TILE)] = dot_nt(branch[...], oheld[span(i, TILE), :]).astype(BF)

    load[0].wait()

    @each((count // SEQ) * groups)
    def _(i):
        row, group = i // groups, i % groups
        where = span(row, SEQ)
        scale = HEAD_DIM**-0.5
        pieces[i].wait()
        if i % 2 == 0:
            start(pieces[i + 2 : i + 4] if i + 2 < len(pieces) else [load[1], load[4], *copies])
        queries = stacked(project[where, span(group, WIDE)] * BF(scale))
        keys = project[where, span(groups + group, WIDE)]
        values = project[where, span(2 * groups + group, WIDE)]
        gmix = stacked(gmixed[where, span(group, WIDE)])
        low = probs[i]
        gprobs = dot_nt(gmix, values)
        gvalues = dot_tn(low, gmix)
        weight = low.astype(F32)
        inner = jnp.sum(weight * gprobs, axis=-1, keepdims=True)
        gscores = (weight * (gprobs - inner)).astype(BF)
        gqueries = unstacked(dot(gscores, keys)) * scale
        gkeys = dot_tn(gscores, queries)
        for third, grad in enumerate((gqueries, gkeys, gvalues)):
            low = grad.astype(BF)
            gproject[where, span(third * groups + group, WIDE)] = low
            sums_ref[third : third + 1, span(group, WIDE)] += jnp.sum(
                low.astype(F32), axis=0, keepdims=True
            )

    load[1].wait()
    turned[0] = both[0].T
    outs = []
    for part in (3, 2, 1, 0):
        left = block_rows(order_ref, turned.at[0], part, apiece, rows)
        for i in range(3 * D // TILE):
            grad = dot(left, gproject[:, span(i, TILE)]).astype(BF)
            grads[part, :, :, span(i, TILE)] = grad.reshape(apiece, rows, TILE)
        copy = pltpu.make_async_copy(grads.at[part], (g0, g1, g2, g3)[part], out_sems.at[part])
        copy.start()
        outs.append(copy)
    wait(copies)
    load[4].wait()
    chunk = count // 2
    for half in range(2):
        where = span(half, chunk)
        for i in range(D // TILE):
            gentry[where, span(i, TILE)] = dot_nt(gproject[where, :], held[span(i, TILE), :])
        normed, inverse = norm_parts(x_ref[where, :].astype(F32))
        grad = gentry[where, :]
        back = norm_back(grad * vec_ref[0:1, :], normed, inverse)
        ginputs[where, :] = gmiddle[where, :] + back
        copy = pltpu.make_async_copy(
            ginputs.at[where, :], ginputs_ref.at[where, :], out_sems.at[4 + half]
        )
        copy.start()
        outs.append(copy)
        sums_ref[3:4, :] += jnp.sum(grad * normed, axis=0, keepdims=True)
        sums_ref[4:5, :] += jnp.sum(grad, axis=0, keepdims=True)
    for copy in outs:
        copy.wait()


def unattend(order, vec, x, gmiddle, branch, project, probs, entry, mixed, win, first):
    count = gmiddle.shape[0]
    shape = jax.ShapeDtypeStruct
    grad = shape((BLOCKS // 4, D // BLOCKS, 4 * D), BF)
    return pl.pallas_call(
        unattend_kernel,
        out_shape=[shape((count, D), F32), shape((8, D), F32)] + [grad] * 4,
        in_specs=[SMEM] + [VMEM] * 2 + [HBM] * 6 + [ANY] * 8,
        out_specs=[ANY, VMEM] + [ANY] * 4,
        scratch_shapes=[
            pltpu.VMEM((D, D), BF),
            pltpu.VMEM((D, 3 * D), BF),
            pltpu.VMEM((count, 3 * D), BF),
            pltpu.VMEM(probs.shape, BF),
            pltpu.VMEM((2, count, D), BF),
            pltpu.VMEM((2, D, count), BF),
            pltpu.VMEM((count, D), F32),
            pltpu.VMEM((count, D), BF),
            pltpu.VMEM((count, D), BF),
            pltpu.VMEM((count, 3 * D), BF),
            pltpu.VMEM((count, D), F32),
            pltpu.VMEM((count, D), F32),
            pltpu.VMEM((4, *grad.shape), BF),
            pltpu.SemaphoreType.DMA((BLOCKS,)),
            pltpu.SemaphoreType.DMA((BLOCKS,)),
            pltpu.SemaphoreType.DMA((5,)),
            pltpu.SemaphoreType.DMA((probs.shape[0],)),
            pltpu.SemaphoreType.DMA((6,)),
        ],
        compiler_params=params(56),
        name="unattend",
    )(order, vec, x, gmiddle, branch, project, probs, entry, mixed, *win, *first)


def finish_kernel(
    spot_ref, vec_ref, middle_ref, active_ref, m0, m1, m2, m3, l0, l1, l2, l3,
    out_ref, held, active, sems, tile_sems,
):
    copies = [
        pltpu.make_async_copy(
            active_ref.at[:, span(half, FF // 2)], active.at[half], tile_sems.at[half]
        )
        for half in range(2)
    ]
    early, late = mlp_fetches(spot_ref, (m0, m1, m2, m3), (l0, l1, l2, l3), held, sems)
    fetch = early + late
    for copy in fetch + copies:
        copy.start()
    for copy in fetch + copies:
        copy.wait()

    @each(D // WIDE)
    def _(i):
        columns = span(i, WIDE)
        weight = held[:, :, columns].reshape(FF, WIDE)
        result = dot(active[0], weight[: FF // 2])
        result = result + dot(active[1], weight[FF // 2 :]) + vec_ref[7:8, columns]
        out_ref[:, columns] = (middle_ref[:, columns] + result).astype(BF)


def finish(spot, vec, middle, active, *mlp):
    count = middle.shape[0]
    return pl.pallas_call(
        finish_kernel,
        out_shape=jax.ShapeDtypeStruct((count, D), BF),
        in_specs=[SMEM, VMEM, VMEM, ANY] + [ANY] * 8,
        out_specs=VMEM,
        scratch_shapes=[
            pltpu.VMEM((BLOCKS, PIECE, D), BF),
            pltpu.VMEM((2, count, FF // 2), BF),
            pltpu.SemaphoreType.DMA((BLOCKS + 4,)),
            pltpu.SemaphoreType.DMA((2,)),
        ],
        compiler_params=params(32),
        name="finish",
    )(spot, vec, middle, active, *mlp)


def per_device(plan, late_plan, inputs, image_ids, cotangent, gains, biases, w_qkv, w_out, w_in, w_mlp):
    me = lax.axis_index(AXES)
    order = plan.positions(me)
    gain_dev, bias_dev = gains.shape[1], biases.shape[1]
    small_dev = gain_dev + bias_dev
    rows = D // plan.devices
    blocks, length = image_ids.shape
    count = blocks * length
    x = inputs.reshape(count, D)
    numbers = order if plan.devices == BLOCKS else jnp.arange(BLOCKS, dtype=jnp.int32)
    late_order = late_plan.positions(me)
    spot = jnp.arange(BLOCKS, dtype=jnp.int32)
    if plan.devices == BLOCKS:
        spot = jnp.sum(jnp.where(late_order[:, None] == order[None], spot[None], 0), axis=1)
    line = Line()
    side = 128

    small = jnp.concatenate([gains, biases], 1)
    small = jnp.pad(small, ((0, 0), (0, rows * side - small_dev))).reshape(rows, side)
    first = Gather(plan, line, "qkv", jnp.concatenate([w_qkv.reshape(rows, 3 * D), small], 1))
    win = Gather(
        plan, line, "in", jnp.concatenate([w_in.reshape(rows, FF), w_out.reshape(rows, D)], 1)
    )
    mlp_block = w_mlp.reshape(FF // plan.devices, D)
    mlp = Gather(plan, line, "mlp", mlp_block[:, : D // 2])
    late = Gather(late_plan, line, "late", mlp_block[:, D // 2 :])
    top = jnp.where(image_ids.reshape(count, 1) >= 0, cotangent.reshape(count, D), BF(0))
    first.start(0)
    late.start(0)
    first.take()
    late.take()
    first.start(1)
    win.start(0)
    late.start(1)
    first.take()
    win.take()
    late.take()
    first.start(2)
    first.take()
    first.start(3)
    first.swap_first()
    win.start(1)
    first.arrive()
    win.take()
    first.swap_second()
    win.start(2)
    mlp.start(0)
    first_parts = first.parts()

    def unpack(*parts):
        placed = jnp.concatenate([part[:, :, 3 * D :] for part in parts], 0)
        placed = placed.reshape(-1, rows * side)[:, :small_dev]
        spread = lax.dot_general(
            one_hot(order), placed, (((0,), (0,)), ((), ())), preferred_element_type=F32
        )
        return jnp.concatenate(
            [spread[:, :gain_dev].reshape(-1), spread[:, gain_dev:].reshape(-1)]
        ).reshape(-1, D)

    vec = line.run(unpack, *first_parts)
    line.wait(*first_parts)
    bias_in = vec[8:12].reshape(1, FF)
    vec = vec[:8]
    if plan.devices != BLOCKS:
        first_parts = [part[:, :, : 3 * D] for part in first_parts]
    first_parts = to_blocks(order, first_parts)
    entry, project = line.run(project_all, numbers, vec, x, *first_parts)
    line.wait(mlp.coming)
    win.take()
    win.start(3)
    win.swap_first()
    mlp.take()
    mlp.start(1)
    late.start(2)
    probs, mixed = line.run(attend, project, image_ids)
    line.wait(mlp.coming, late.coming)
    win.arrive()
    line.wait(win.first)
    win.swap_second()
    mlp.take()
    mlp.start(2)
    win_parts = to_blocks(order, win.parts())
    middle, second = line.run(settle, numbers, vec, x, mixed, *win_parts)
    line.wait(mlp.coming)
    late.take()
    late.start(3)
    late.swap_first()
    mlp.take()
    mlp.start(3)
    mlp.swap_first()
    active, slope, *grads = line.run(rise, numbers, bias_in, second, top, *win_parts)
    line.wait(mlp.first, late.first)
    mlp.arrive()
    late.arrive()
    sum_mlp = Scatter(plan, line, "mlp", from_blocks(order, grads))
    mlp.swap_second()
    late.swap_second()
    sum_mlp.start(3)
    mlp_parts = to_blocks(order, mlp.parts()) + to_blocks(late_order, late.parts())
    ghidden, grad_bias_in, *grads = line.run(fall, numbers, spot, top, slope, second, *mlp_parts)
    sum_in = Scatter(plan, line, "in", from_blocks(order, grads))
    gmiddle, branch, sums = line.run(back, numbers, vec, ghidden, top, middle, *win_parts)
    line.wait(sum_in.high[-1])
    sum_mlp.arrive()
    sum_in.start(3)
    sum_mlp.start(2)
    grad_inputs, sums_one, *grads = line.run(
        unattend, numbers, vec, x, gmiddle, branch, project, probs, entry, mixed, win_parts, first_parts
    )
    sum_mlp.start(1)
    sum_in.arrive()
    sum_first = Scatter(plan, line, "first", from_blocks(order, grads))

    def pack(sums_one, sums, grad_bias_in):
        flat_gains = jnp.concatenate([sums_one[3], sums[0]]).reshape(-1, gain_dev)
        flat_biases = jnp.concatenate(
            [sums_one[4], sums_one[0], sums_one[2], sums[2], sums[1], sums[3], grad_bias_in[0]]
        ).reshape(-1, bias_dev)
        flat_small = jnp.concatenate([flat_gains, flat_biases], 1).astype(BF)
        moved = jnp.dot(one_hot(order), flat_small, preferred_element_type=F32).astype(BF)
        moved = jnp.pad(moved, ((0, 0), (0, rows * side - small_dev)))
        return moved.reshape(plan.devices, rows, side)

    sum_first.join(pack(sums_one, sums, grad_bias_in))
    sum_in.start(2)
    sum_first.start(3)
    sum_mlp.start(0)
    output = line.run(finish, spot, vec, middle, active, *mlp_parts)
    sum_mlp.arrive()
    sum_in.start(1)
    sum_in.arrive()
    sum_first.start(2)
    sum_in.start(0)
    grad_mlp = sum_mlp.result()
    sum_in.arrive()
    sum_first.last()
    grad_in = sum_in.result()
    grad_first = sum_first.result()
    grad_small = grad_first[:, 4 * D :].reshape(1, -1)[:, :small_dev]
    return (
        output.reshape(blocks, length, D),
        grad_inputs.reshape(blocks, length, D),
        grad_small[:, :gain_dev],
        grad_small[:, gain_dev:],
        grad_first[:, : 3 * D].reshape(1, -1),
        grad_first[:, 3 * D : 4 * D].reshape(1, -1),
        grad_in.reshape(1, -1),
        grad_mlp.reshape(1, -1),
    )


def solution(mesh):
    plan, late_plan = Plan(mesh), Plan(mesh, late=True)
    whole = P(AXES, None, None)
    flat = P(AXES, None)

    def body(*arrays):
        return per_device(plan, late_plan, *arrays)

    return jax.shard_map(
        body,
        mesh=mesh,
        in_specs=(whole, flat, whole, flat, flat, flat, flat, flat, flat),
        out_specs=(whole, whole, flat, flat, flat, flat, flat, flat),
        check_vma=False,
    )
```
